32 devices in a mesh: section: 2 (over core), tensor: 4 (over y, x), dp: 4 (over z).
Axes of the slice: x: 2, y: 2, z: 4, core: 2. Of those that a mesh axis runs over, the one named last changes fastest.
Arguments:
- boundary: bfloat16 [2, 8, 512, 768], P('section', 'dp', 'tensor'), may hold values from -6 to 6
- lengths: int32 [8], P('dp'), may hold values from 128 to 512, as said below
- routes: int32 [2, 8, 512, 2], P('section', 'dp'), may hold values from 0 to 3, all different within a row; in each aligned block of 512 rows (0 to 511, 512 to 1023, ..., all dimensions but the last counted through in order) at most 320 rows name the same one
- attn_gain: float32 [2, 768], P('section'), may hold values from 0.5 to 1.5
- w_query: bfloat16 [2, 768, 768], P('section', None, 'tensor'), may hold values from -0.21875 to 0.21875
- w_key: bfloat16 [2, 768, 768], P('section', None, 'tensor'), may hold values from -0.21875 to 0.21875
- w_value: bfloat16 [2, 768, 768], P('section', None, 'tensor'), may hold values from -0.21875 to 0.21875
- w_out: bfloat16 [2, 768, 768], P('section', 'tensor'), may hold values from -1.25 to 1.25
- ffn_gain: float32 [2, 768], P('section'), may hold values from 0.5 to 1.5
- router: bfloat16 [2, 768, 4], P('section'), may hold values from -0.15625 to 0.15625
- expert_gate: bfloat16 [2, 4, 768, 2048], P('section', None, None, 'tensor'), may hold values from -0.21875 to 0.21875
- expert_up: bfloat16 [2, 4, 768, 2048], P('section', None, None, 'tensor'), may hold values from -0.21875 to 0.21875
- expert_down: bfloat16 [2, 4, 2048, 768], P('section', None, 'tensor'), may hold values from -0.125 to 0.125
- shared_gate: bfloat16 [2, 768, 2048], P('section', None, 'tensor'), may hold values from -0.21875 to 0.21875
- shared_up: bfloat16 [2, 768, 2048], P('section', None, 'tensor'), may hold values from -0.21875 to 0.21875
- shared_down: bfloat16 [2, 2048, 768], P('section', 'tensor'), may hold values from -0.125 to 0.125
Outputs:
- section_outputs: bfloat16 [2, 8, 512, 768], P('section', 'dp', 'tensor')
- section_input_grads: float32 [2, 8, 512, 768], P('section', 'dp', 'tensor')
- attn_gain_grad: float32 [2, 768], P('section')
- w_query_grad: float32 [2, 768, 768], P('section', 'dp', 'tensor')
- w_key_grad: float32 [2, 768, 768], P('section', 'dp', 'tensor')
- w_value_grad: float32 [2, 768, 768], P('section', 'dp', 'tensor')
- w_out_grad: float32 [2, 768, 768], P('section', 'tensor', 'dp')
- ffn_gain_grad: float32 [2, 768], P('section')
- router_grad: float32 [2, 768, 4], P('section')
- expert_gate_grad: float32 [2, 4, 768, 2048], P('section', None, 'dp', 'tensor')
- expert_up_grad: float32 [2, 4, 768, 2048], P('section', None, 'dp', 'tensor')
- expert_down_grad: float32 [2, 4, 2048, 768], P('section', None, 'tensor', 'dp')
- shared_gate_grad: float32 [2, 768, 2048], P('section', 'dp', 'tensor')
- shared_up_grad: float32 [2, 768, 2048], P('section', 'dp', 'tensor')
- shared_down_grad: float32 [2, 2048, 768], P('section', 'tensor', 'dp')
- balance_loss: float32 [2], P('section')
The draws below stay inside these ranges and needn't reach their ends.
Inputs may be any that keep to these rules, and one draw needn't show every extreme that they name: `lengths`: each group of 2 consecutive sequences holds one of length 512. The two routes of a token differ; within one sequence of one layer no expert is named by more than 320 tokens, a bound that some block reaches.
All inputs are finite; a program needn't handle non-finite values.
Results may differ from the reference program's by a relative error of at most 0.025.
Values may be sent and summed in bfloat16 or wider, within the bound.
A program may use at most 192 MiB of HBM per device.

```python
import math
import jax
import jax.numpy as jnp
import numpy as np
from jax import lax

D = 768
HEADS = 12
HEAD_DIM = 64
FF = 2048
EXPERTS = 4
TOP = 2
CAP = 320
LEN = 512
MICRO = 2
SEQ_MB = 1
SEQS = 8


def draw_lengths(key, part):
    key = jax.random.fold_in(key, 7)
    first_key, second_key = jax.random.split(key)
    group_size = SEQ_MB * MICRO
    groups = SEQS // group_size
    drawn = jax.random.randint(first_key, (groups, group_size), LEN // 4, LEN + 1)
    longest = jax.random.randint(second_key, (groups,), 0, group_size)
    filled = jnp.where(jnp.arange(group_size)[None, :] == longest[:, None], LEN, drawn)
    return filled.reshape(SEQS).astype(jnp.int32)


def level_of(rng, dims, shards, low, high):
    factor_of = 1.0
    for dim, parts in shards:
        heights = jax.random.uniform(jax.random.fold_in(jax.random.fold_in(rng, 6), dim), (parts,), jnp.float32, low / len(shards), high / len(shards))
        factor_of = factor_of * jnp.repeat(jnp.exp(heights), dims[dim] // parts).reshape((-1,) + (1,) * (len(dims) - 1 - dim))
    return factor_of


def deal_out(rng, own, number, rows, amount, top, limit, lean):
    ranking = jax.random.permutation(rng, amount)
    heavy_load, usual = shares(amount, rows * top, limit, lean, True), shares(amount, rows * top, limit, lean, False)
    places = jnp.arange(amount)

    def named(sizes, offset_by):
        used = int((sizes > 0).sum())
        fixed = max(1, used // 4)
        passed = fixed + (places - fixed + offset_by * (used - fixed)) % max(1, amount - fixed)
        return jnp.zeros((amount,), jnp.int32).at[ranking[jnp.where(places < fixed, places, passed)]].set(jnp.asarray(sizes, jnp.int32))

    sizes = jnp.where(number % 4 == 0, named(heavy_load, number // 4), named(usual, number - number // 4 - 1))
    mixed = jax.random.permutation(jax.random.fold_in(own, 3), amount)
    source_of, sink = mixed[0:amount // 2 * 2:2], mixed[1:amount // 2 * 2:2]
    slack = jnp.minimum(sizes[source_of] - 1, limit - sizes[sink]) // 2
    slack = jnp.where((source_of == ranking[0]) | (sink == ranking[0]) | (sizes[sink] == 0), 0, jnp.maximum(slack, 0))
    passed = jax.random.randint(jax.random.fold_in(own, 4), (amount // 2,), 0, 1 << 20) % (slack + 1)
    sizes = sizes.at[source_of].add(-passed).at[sink].add(passed)
    items = jnp.searchsorted(jnp.cumsum(sizes), jnp.arange(rows * top), side="right").astype(jnp.int32)
    grid = items.reshape(top, rows).T
    grid = grid[jax.random.permutation(jax.random.fold_in(own, 1), rows)]
    offset_by = jax.random.randint(jax.random.fold_in(own, 2), (rows, 1), 0, top)
    return jnp.take_along_axis(grid, (jnp.arange(top)[None, :] + offset_by) % top, axis=1)


def shares(amount, total, reach, skew, full):
    portions = [(1 << 20) // math.isqrt(grade ** skew) + 1 for grade in range(1, amount + 1)]
    largest = reach if full else min(reach, max(-(-total // amount), total * portions[0] // sum(portions)))
    least = 1 if total - largest >= amount - 1 else 0
    given, surplus = [largest] + [least] * (amount - 1), total - largest - least * (amount - 1)
    while surplus > 0:
        movable = [i for i in range(1, amount) if given[i] < largest] or [i for i in range(1, amount) if given[i] < reach]
        pool, left = sum([portions[i] for i in movable]), surplus
        for i in movable:
            addition = min(reach - given[i], max(1, left * portions[i] // pool), surplus)
            given[i] = given[i] + addition
            surplus = surplus - addition
    return np.array(given)


def scatter_about(stream_key, extent, deviation, most, pieces=(), held_as=jnp.bfloat16):
    array = jax.random.normal(stream_key, extent, jnp.float32) * deviation
    if len(pieces) > 0:
        array = level_of(stream_key, extent, pieces, -0.22, 0.18) * array
    return jnp.clip(array, min=-most, max=most).astype(held_as)


def setup_inputs(seed: int = 0) -> dict:
    seeds = jax.random.split(jax.random.key(seed), 17)
    boundary = scatter_about(seeds[0], (2, SEQS, LEN, D), 1.0, 6.0, ((0, 2), (1, 4), (2, 4)))
    lengths = draw_lengths(jax.random.fold_in(seeds[16], 71), 0)
    routes_keys = jax.random.split(jax.random.fold_in(seeds[2], 1), 2 * SEQS * LEN // LEN)
    routes_turns = jax.random.permutation(jax.random.fold_in(seeds[2], 3), 2 * SEQS * LEN // LEN)
    routes = jax.vmap(lambda own, number: deal_out(jax.random.fold_in(seeds[2], 2), own, number, LEN, EXPERTS, TOP, CAP, 1))(routes_keys, routes_turns).reshape((2, SEQS, LEN, TOP))
    attn_gain = jnp.clip(1.0 + 0.1 * jax.random.normal(seeds[3], (2, D), jnp.float32), 0.5, 1.5)
    w_query = scatter_about(seeds[4], (2, D, HEADS * HEAD_DIM), D ** -0.5, 0.21875, ((0, 2), (2, 4)))
    w_key = scatter_about(seeds[5], (2, D, HEADS * HEAD_DIM), D ** -0.5, 0.21875, ((0, 2), (2, 4)))
    w_value = scatter_about(seeds[6], (2, D, HEADS * HEAD_DIM), D ** -0.5, 0.21875, ((0, 2), (2, 4)))
    w_out = scatter_about(seeds[7], (2, HEADS * HEAD_DIM, D), (HEADS * HEAD_DIM // 32) ** -0.5, 1.25, ((0, 2), (1, 4)))
    ffn_gain = jnp.clip(1.0 + 0.1 * jax.random.normal(seeds[8], (2, D), jnp.float32), 0.5, 1.5)
    router = scatter_about(seeds[9], (2, D, EXPERTS), (2 * D) ** -0.5, 0.15625, ((0, 2),))
    expert_gate = scatter_about(seeds[10], (2, EXPERTS, D, FF), D ** -0.5, 0.21875, ((0, 2), (3, 4)))
    expert_up = scatter_about(seeds[11], (2, EXPERTS, D, FF), D ** -0.5, 0.21875, ((0, 2), (3, 4)))
    expert_down = scatter_about(seeds[12], (2, EXPERTS, FF, D), FF ** -0.5, 0.125, ((0, 2), (2, 4)))
    shared_gate = scatter_about(seeds[13], (2, D, FF), D ** -0.5, 0.21875, ((0, 2), (2, 4)))
    shared_up = scatter_about(seeds[14], (2, D, FF), D ** -0.5, 0.21875, ((0, 2), (2, 4)))
    shared_down = scatter_about(seeds[15], (2, FF, D), FF ** -0.5, 0.125, ((0, 2), (1, 4)))
    return {"boundary": boundary, "lengths": lengths, "routes": routes, "attn_gain": attn_gain, "w_query": w_query, "w_key": w_key, "w_value": w_value, "w_out": w_out, "ffn_gain": ffn_gain, "router": router, "expert_gate": expert_gate, "expert_up": expert_up, "expert_down": expert_down, "shared_gate": shared_gate, "shared_up": shared_up, "shared_down": shared_down}


EPSILON = 1e-06
ALPHA = 0.01
THETA = 10000.0
MASKED = -1e+30
HIGHEST = lax.Precision.HIGHEST

@jax.custom_vjp
def low(v):
    return lax.optimization_barrier(v.astype(jnp.bfloat16)).astype(jnp.float32)

@jax.custom_vjp
def low_back(v):
    return v

def low_keep(v):
    return (low(v), None)

def low_pass(kept, grad):
    return (grad,)

def back_keep(v):
    return (v, None)

def back_low(kept, grad):
    return (low(grad),)
low.defvjp(low_keep, low_pass)
low_back.defvjp(back_keep, back_low)

def rms_norm(values, gains):
    return values * lax.rsqrt(lax.optimization_barrier(jnp.mean(values * values, axis=-1, keepdims=True)) + EPSILON) * gains

def rope_tables(positions, head_dim):
    half_dim = head_dim // 2
    frequency = THETA ** (-jnp.arange(half_dim, dtype=jnp.float32) / half_dim)
    angles = positions.astype(jnp.float32)[:, None] * frequency[None, :]
    cosine_table = jnp.concatenate([jnp.cos(angles), jnp.cos(angles)], axis=-1)
    sine_table = jnp.concatenate([jnp.sin(angles), jnp.sin(angles)], axis=-1)
    return (cosine_table[:, None, :], sine_table[:, None, :])

def rotate(values, cosine_table, sine_table):
    half_dim = values.shape[-1] // 2
    turned = jnp.concatenate([-values[..., half_dim:], values[..., :half_dim]], axis=-1)
    return values * cosine_table + turned * sine_table

def slot_index(route, capacity, experts):
    flat_route = route.reshape(route.shape[0], -1)
    chosen_one = (flat_route[..., None] == jnp.arange(experts, dtype=jnp.int32)).astype(jnp.int32)
    position = lax.optimization_barrier(jnp.sum((jnp.cumsum(chosen_one, axis=1) - 1) * chosen_one, axis=2))
    return (flat_route * capacity + position).astype(jnp.int32)

def gated_unit(gate_vals, up_vals):
    return jax.nn.silu(gate_vals) * up_vals

def router_piece(logits, route_rows, weights_aux):
    chances = jax.nn.softmax(logits, axis=-1)
    chosen = jnp.take_along_axis(chances, route_rows, axis=-1)
    gate_values = chosen / lax.optimization_barrier(jnp.sum(chosen, axis=-1, keepdims=True))
    return (gate_values, jnp.sum(chances * weights_aux))

def matmul(left, right):
    return jnp.dot(left, right, precision=HIGHEST)

def sequence_layer(weights, inputs, route, length):
    attn_gain, w_query, w_key, w_value, w_out, ffn_gain, router, expert_gate, expert_up, expert_down, shared_gate, shared_up, shared_down = weights
    positions = jnp.arange(LEN, dtype=jnp.int32)
    valid_keys = positions < length
    cosine_table, sine_table = rope_tables(positions, HEAD_DIM)
    head_shape = (LEN, HEADS, HEAD_DIM)
    normed = low(rms_norm(inputs, attn_gain))
    query_rot = low(rotate(low_back(matmul(normed, w_query)).reshape(head_shape), cosine_table, sine_table))
    key_rot = low(rotate(low_back(matmul(normed, w_key)).reshape(head_shape), cosine_table, sine_table))
    value_low = low(low_back(matmul(normed, w_value))).reshape(head_shape)
    scores = low_back(jnp.einsum('qhd,khd->hqk', query_rot, key_rot, precision=HIGHEST) * HEAD_DIM ** (-0.5))
    allowed = (positions[None, :] <= positions[:, None]) & valid_keys[None, :]
    scores = jnp.where(allowed[None], scores, MASKED)
    soft_weights = low(jax.nn.softmax(scores, axis=-1))
    mixed_heads = low(low_back(jnp.einsum('hqk,khd->qhd', soft_weights, value_low, precision=HIGHEST))).reshape(LEN, HEADS * HEAD_DIM)
    middle = inputs + low_back(matmul(mixed_heads, w_out))
    hidden = low(rms_norm(middle, ffn_gain))
    logits = matmul(hidden, router)
    gate_values, unused_term = router_piece(logits, route, 0.0)
    chances = jax.nn.softmax(logits, axis=-1)
    slot_ids = slot_index(route[None], CAP, EXPERTS)[0]
    buffer = jnp.zeros((EXPERTS * CAP, D), jnp.float32).at[slot_ids].add(jnp.repeat(hidden, TOP, axis=0))
    buffer = buffer.reshape(EXPERTS, CAP, D)
    gate_h = low_back(jnp.einsum('ecd,edf->ecf', buffer, expert_gate, precision=HIGHEST))
    up_h = low_back(jnp.einsum('ecd,edf->ecf', buffer, expert_up, precision=HIGHEST))
    acted_low = low(gated_unit(gate_h, up_h))
    returned = low_back(jnp.einsum('ecf,efd->ecd', acted_low, expert_down, precision=HIGHEST)).reshape(EXPERTS * CAP, D)
    picked = returned[slot_ids].reshape(LEN, TOP, D)
    mixture = lax.optimization_barrier(jnp.sum(gate_values[:, :, None] * picked, axis=1))
    shared_g = low_back(matmul(hidden, shared_gate))
    shared_u = low_back(matmul(hidden, shared_up))
    shared_out = matmul(low(gated_unit(shared_g, shared_u)), shared_down)
    output = middle + low_back(mixture + shared_out)
    totals = lax.optimization_barrier(jnp.sum(jnp.where(valid_keys[:, None], chances, 0.0), axis=0))
    return (output, totals)

def run_layer(weights, inputs, route, lengths):
    stepper = jax.checkpoint(lambda packed: sequence_layer(weights, packed[0], packed[1], packed[2]))
    outputs, totals = lax.map(stepper, (inputs, route, lengths))
    return (outputs, lax.optimization_barrier(jnp.sum(totals, axis=0)))

def reference(boundary, lengths, routes, attn_gain, w_query, w_key, w_value, w_out, ffn_gain, router, expert_gate, expert_up, expert_down, shared_gate, shared_up, shared_down):
    stacked = tuple((weight_item.astype(jnp.float32) for weight_item in (attn_gain, w_query, w_key, w_value, w_out, ffn_gain, router, expert_gate, expert_up, expert_down, shared_gate, shared_up, shared_down)))
    inputs = boundary[0].astype(jnp.float32)
    cotangent = boundary[1].astype(jnp.float32)
    positions = jnp.arange(LEN, dtype=jnp.int32)
    valid_mask = (positions[None, :] < lengths[:, None]).astype(jnp.float32)
    named_mask = (routes[..., None] == jnp.arange(EXPERTS, dtype=jnp.int32)).astype(jnp.float32)
    counts = lax.optimization_barrier(jnp.sum(named_mask * valid_mask[None, :, :, None, None], axis=(1, 2, 3)))
    tokens_all = jnp.sum(lengths).astype(jnp.float32)
    load_share = counts / (TOP * tokens_all)
    probe_zero = jnp.zeros_like(inputs)

    def forward(layer_input, probe_input, *weights):
        layer_one = tuple((weight_item[0] for weight_item in weights))
        layer_two = tuple((weight_item[1] for weight_item in weights))
        first_out, totals_one = run_layer(layer_one, layer_input, routes[0], lengths)
        second, totals_two = run_layer(layer_two, low(low_back(first_out + probe_input)), routes[1], lengths)
        balance = EXPERTS * lax.optimization_barrier(jnp.sum(load_share * jnp.stack([totals_one, totals_two]), axis=1)) / tokens_all
        total_loss = jnp.sum(valid_mask[:, :, None] * cotangent * second) + ALPHA * jnp.sum(balance)
        return (total_loss, (first_out, second, balance))
    total_loss, pullback, kept_values = jax.vjp(forward, inputs, probe_zero, *stacked, has_aux=True)
    gradients = pullback(jnp.ones_like(total_loss))
    first_out, second, balance = kept_values
    return (jnp.stack([first_out, second]).astype(jnp.bfloat16), jnp.stack([gradients[0], gradients[1]]), gradients[2], gradients[3], gradients[4], gradients[5], gradients[6], gradients[7], gradients[8], gradients[9], gradients[10], gradients[11], gradients[12], gradients[13], gradients[14], balance)
```

```python
import functools

import jax
import jax.numpy as jnp
from jax import lax
from jax.experimental import pallas as pl
from jax.experimental.pallas import tpu as pltpu
from jax.sharding import PartitionSpec as P

HEAD_DIM = 64
HALF_DIM = HEAD_DIM // 2
EPSILON = 1e-06
ALPHA = 0.01
THETA = 10000.0
MASKED = -1e30
LANES = 256
VMEM_LIMIT = 60 * 2**20

f32 = jnp.float32
bf16 = jnp.bfloat16
MESH = pl.DeviceIdType.MESH
ANY = pl.BlockSpec(memory_space=pl.ANY)
VMEM = pl.BlockSpec(memory_space=pltpu.VMEM)
SMEM = pl.BlockSpec(memory_space=pltpu.SMEM)


def dot(left, right, left_dim, right_dim):
    return lax.dot_general(
        left, right, (((left_dim,), (right_dim,)), ((), ())), preferred_element_type=f32
    )


def rope_tables(seq_len):
    frequency = THETA ** (-jnp.arange(HALF_DIM, dtype=f32) / HALF_DIM)
    angles = jnp.arange(seq_len, dtype=jnp.int32).astype(f32)[:, None] * frequency[None, :]
    cosine, sine = jnp.cos(angles), jnp.sin(angles)
    return jnp.concatenate([cosine, cosine, -sine, sine], axis=-1)


def turn_halves(values):
    return jnp.concatenate([values[:, HALF_DIM:], values[:, :HALF_DIM]], axis=1)


class Place:
    def __init__(self, ranks):
        self.s = lax.axis_index("section")
        self.t = lax.axis_index("tensor")
        self.z = lax.axis_index("dp")
        self.ranks = ranks
        self.sibling = (1 - self.s, self.t, self.z)

    def peer(self, k):
        return lax.rem(self.t + k, self.ranks)

    def peer_id(self, k):
        return (self.s, self.peer(k), self.z)

    def greet(self):
        barrier = pltpu.get_barrier_semaphore()
        others = [self.sibling] + [self.peer_id(k) for k in range(1, self.ranks)]
        for other in others:
            pl.semaphore_signal(barrier, inc=1, device_id=other, device_id_type=MESH)
        pl.semaphore_wait(barrier, len(others))


def remote(src, dst, send, recv, device):
    return pltpu.make_async_remote_copy(
        src_ref=src, dst_ref=dst, send_sem=send, recv_sem=recv, device_id=device, device_id_type=MESH
    )


def gather_rows(place, full, rows, send, recv):
    mine = full.at[pl.ds(place.t * rows, rows)]
    copies = []
    for k in range(1, place.ranks):
        copy = remote(mine, mine, send.at[k - 1], recv.at[k - 1], place.peer_id(k))
        copy.start()
        copies.append(copy)
    return copies


def scatter_block(place, stage, landing, rows, lo, width, send, recv):
    copies = []
    for k in range(1, place.ranks):
        src = stage.at[pl.ds(place.peer(k) * rows, rows), pl.ds(lo, width)]
        dst = landing.at[k - 1, :, pl.ds(lo, width)]
        copy = remote(src, dst, send.at[k - 1], recv.at[k - 1], place.peer_id(k))
        copy.start()
        copies.append(copy)
    return copies


def landed_sum(own, landing, ranks):
    total = own
    for k in range(ranks - 1):
        total = total + landing[k].astype(f32)
    return total


def rms_rows(values, gain):
    return values * lax.rsqrt(jnp.mean(values * values, axis=-1, keepdims=True) + EPSILON) * gain


def rms_back(values, gain, grad):
    r = lax.rsqrt(jnp.mean(values * values, axis=-1, keepdims=True) + EPSILON)
    normed = values * r
    scaled = grad * gain
    inner = jnp.mean(scaled * normed, axis=-1, keepdims=True)
    return r * (scaled - normed * inner), jnp.sum(grad * normed, axis=0, keepdims=True)


def column(matrix, index):
    lane = lax.broadcasted_iota(jnp.int32, matrix.shape, 1)
    return jnp.sum(jnp.where(lane == index, matrix, 0.0), axis=1, keepdims=True)


def load_choice(first, pairs, sems):
    for i, (own, other, dst) in enumerate(pairs):

        @pl.when(first)
        def _(own=own, dst=dst, i=i):
            pltpu.make_async_copy(own, dst, sems.at[i]).start()

        @pl.when(jnp.logical_not(first))
        def _(other=other, dst=dst, i=i):
            pltpu.make_async_copy(other, dst, sems.at[i]).start()

    return [pltpu.make_async_copy(own, dst, sems.at[i]) for i, (own, other, dst) in enumerate(pairs)]


N_ATTN = 4
N_FFN = 6


def forward_kernel(
    ranks,
    lens,
    bnd,
    chosen,
    gains,
    router,
    tables,
    *refs,
):
    own = refs[:10]
    refs = refs[10:]
    other = refs[:10]
    (o_gains, o_router, o_chosen, out_rows, cot, probs_sum) = refs[10:16]
    (nf_o, q_o, k_o, v_o, p_o, mx_o, hf_o, g_o, u_o) = refs[16:25]
    (xs, mid, coef, small) = refs[25:29]
    refs = refs[29:]
    (nf, qs, ks, vs, ps, mx, hf, gs, us) = refs[:9]
    refs = refs[9:]
    (wq, wk, wv, wo, wg, wu, wd, acts, stage, land_a, land_f, tmp, own_part, o_bnd, y_low) = refs[:15]
    (ag_s, ag_r, rsa_s, rsa_r, rsf_s, rsf_r, ex_s, ex_r, load_sem, save_sem, row_s, row_r) = refs[15:]

    place = Place(ranks)
    s, t = place.s, place.t
    rows, width = bnd.shape[1], bnd.shape[2]
    seq_len = nf.shape[1]
    experts = wg.shape[0] - 1
    heads = qs.shape[1]
    mine = pl.ds(t * rows, rows)
    place.greet()

    ex_pairs = [
        (bnd.at[1 - s], o_bnd),
        (gains, o_gains),
        (router, o_router),
        (chosen.at[1 - s], o_chosen),
    ] + [(own[i], other[i]) for i in range(10)]
    exchange = [
        remote(src, dst, ex_s.at[i], ex_r.at[i], place.sibling) for i, (src, dst) in enumerate(ex_pairs)
    ]
    for copy in exchange:
        copy.start()
    for copy in exchange[:4]:
        copy.wait()
    is_first = s == 0
    xs[0] = jnp.where(is_first, bnd[0], o_bnd[...])
    cot[...] = jnp.where(is_first, o_bnd[...], bnd[1])
    length = lens[s]

    ffn_targets = [
        (wg.at[pl.ds(0, experts)]),
        (wu.at[pl.ds(0, experts)]),
        (wd.at[pl.ds(0, experts)]),
        wg.at[experts],
        wu.at[experts],
        wd.at[experts],
    ]
    attn_targets = [wq, wk, wv, wo]

    def layer(l, carry):
        here = s == l
        gain_a = jnp.where(here, gains[0:1], o_gains[0:1])
        gain_f = jnp.where(here, gains[1:2], o_gains[1:2])
        x = xs[l].astype(f32)
        nf[l, mine] = rms_rows(x, gain_a).astype(bf16)
        ag = gather_rows(place, nf.at[l], rows, ag_s.at[l, 0], ag_r.at[l, 0])

        @pl.when(jnp.logical_not(here))
        def _():
            for copy in exchange[4 : 4 + N_ATTN]:
                copy.wait_recv()

        loads = load_choice(
            here, [(own[i], other[i], attn_targets[i]) for i in range(N_ATTN)], load_sem
        )

        @pl.when(jnp.logical_not(here))
        def _():
            for copy in exchange[4 + N_ATTN :]:
                copy.wait_recv()

        ffn_loads = load_choice(
            here,
            [(own[4 + i], other[4 + i], ffn_targets[i]) for i in range(N_FFN)],
            load_sem.at[pl.ds(N_ATTN, N_FFN)],
        )
        for copy in loads:
            copy.wait()
        for copy in ag:
            copy.wait()
        pltpu.make_async_copy(nf.at[l], nf_o.at[l], save_sem.at[l, 0]).start()
        cosine, signed = tables[:, :HEAD_DIM], tables[:, HEAD_DIM:]
        normed = nf[l]
        for w, dst, turned in ((wq, qs, True), (wk, ks, True), (wv, vs, False)):
            projected = dot(normed, w[...], 1, 0)
            for h in range(heads):
                piece = projected[:, h * HEAD_DIM : (h + 1) * HEAD_DIM]
                if turned:
                    piece = piece * cosine + turn_halves(piece) * signed
                dst[l, h] = piece.astype(bf16)
        scat = []
        for i in range(ranks):
            lo, reach = i * rows, (i + 1) * rows
            place_q = lax.broadcasted_iota(jnp.int32, (rows, reach), 0) + lo
            place_k = lax.broadcasted_iota(jnp.int32, (rows, reach), 1)
            allowed = (place_k <= place_q) & (place_k < length)
            for h in range(heads):
                scores = dot(qs[l, h, lo:reach], ks[l, h, 0:reach], 1, 1) * HEAD_DIM ** (-0.5)
                scores = jnp.where(allowed, scores, MASKED)
                peak = jnp.max(scores, axis=-1, keepdims=True)
                raised = jnp.exp(scores - peak)
                total = jnp.sum(raised, axis=-1, keepdims=True)
                weights = (raised / total).astype(bf16)
                ps[l, h, lo:reach, 0:reach] = weights
                if reach < seq_len:
                    ps[l, h, lo:reach, reach:] = jnp.zeros((rows, seq_len - reach), bf16)
                mixed = dot(weights, vs[l, h, 0:reach], 1, 0)
                mx[l, lo:reach, h * HEAD_DIM : (h + 1) * HEAD_DIM] = mixed.astype(bf16)
            part = dot(mx[l, lo:reach], wo[...], 1, 0)
            stage[lo:reach] = part.astype(bf16)

            @pl.when(t == i)
            def _(part=part):
                own_part[...] = part

            @pl.when(t != i)
            def _(i=i, lo=lo):
                k = lax.rem(i - t + ranks, ranks)
                remote(
                    stage.at[pl.ds(lo, rows)],
                    land_a.at[l, k - 1],
                    rsa_s.at[l, k - 1],
                    rsa_r.at[l, k - 1],
                    (s, i, place.z),
                ).start()

        saves = [(qs, q_o), (ks, k_o), (vs, v_o), (ps, p_o), (mx, mx_o)]
        for i, (src, dst) in enumerate(saves):
            pltpu.make_async_copy(src.at[l], dst.at[l], save_sem.at[l, 1 + i]).start()
        for k in range(1, ranks):
            remote(
                stage.at[pl.ds(place.peer(k) * rows, rows)],
                land_a.at[l, k - 1],
                rsa_s.at[l, k - 1],
                rsa_r.at[l, k - 1],
                place.peer_id(k),
            ).wait()
        middle = x + landed_sum(own_part[...], land_a.at[l], ranks)
        mid[l] = middle
        hf[l, mine] = rms_rows(middle, gain_f).astype(bf16)
        ag = gather_rows(place, hf.at[l], rows, ag_s.at[l, 1], ag_r.at[l, 1])
        for copy in ffn_loads:
            copy.wait()
        for copy in ag:
            copy.wait()
        pltpu.make_async_copy(hf.at[l], hf_o.at[l], save_sem.at[l, 6]).start()
        hidden = hf[l]
        route_w = jnp.where(here, router[...], o_router[...])
        names = jnp.where(here, chosen[s], o_chosen[...])
        logits = dot(route_w, hidden, 1, 1)
        expert_row = lax.broadcasted_iota(jnp.int32, logits.shape, 0)
        logits = jnp.where(expert_row < experts, logits, MASKED)
        raised = jnp.exp(logits - jnp.max(logits, axis=0, keepdims=True))
        raised = jnp.where(expert_row < experts, raised, 0.0)
        chances = raised / jnp.sum(raised, axis=0, keepdims=True)
        per_chosen = names / jnp.sum(chances * names, axis=0, keepdims=True)
        gates = chances * per_chosen
        small[l, 0:8] = chances
        small[l, 8:16] = gates
        small[l, 16:24] = per_chosen
        token = lax.broadcasted_iota(jnp.int32, logits.shape, 1)
        summed = jnp.sum(jnp.where(token < length, chances, 0.0), axis=1, keepdims=True)
        probs_sum[l] = jnp.broadcast_to(summed, (8, 128))
        coef[l] = jnp.where(expert_row == experts, 1.0, gates).T

        def one_expert(e, carry):
            gate_h = dot(hf[l], wg[e], 1, 0)
            up_h = dot(hf[l], wu[e], 1, 0)
            gs[l, e] = gate_h.astype(bf16)
            us[l, e] = up_h.astype(bf16)
            weight = column(coef[l], e)
            acts[e] = (gate_h * jax.nn.sigmoid(gate_h) * up_h * weight).astype(bf16)
            return carry

        lax.fori_loop(0, experts + 1, one_expert, 0)
        pltpu.make_async_copy(gs.at[l], g_o.at[l], save_sem.at[l, 7]).start()
        pltpu.make_async_copy(us.at[l], u_o.at[l], save_sem.at[l, 8]).start()
        scat = []
        for n in range(width // LANES):
            lanes = slice(n * LANES, (n + 1) * LANES)
            total = dot(acts[0], wd[0, :, lanes], 1, 0)
            for e in range(1, experts + 1):
                total = total + dot(acts[e], wd[e, :, lanes], 1, 0)
            tmp[...] = total
            stage[:, lanes] = total.astype(bf16)
            own_part[:, lanes] = tmp[mine]
            scat += scatter_block(
                place, stage, land_f.at[l], rows, n * LANES, LANES, rsf_s.at[l, n], rsf_r.at[l, n]
            )
        for copy in scat:
            copy.wait()
        output = mid[l] + landed_sum(own_part[...], land_f.at[l], ranks)
        y_low[l] = output.astype(bf16)
        xs[1] = jnp.where(l == 0, y_low[l], xs[1])

        @pl.when(here)
        def _():
            out_rows[s] = y_low[l]

        @pl.when(jnp.logical_not(here))
        def _():
            remote(y_low.at[l], out_rows.at[s], row_s, row_r, place.sibling).start()

        return carry

    xs[1] = jnp.zeros_like(xs[1])
    lax.fori_loop(0, 2, layer, 0)
    remote(y_low.at[1 - s], out_rows.at[s], row_s, row_r, place.sibling).wait_send()
    remote(y_low.at[1 - s], out_rows.at[1 - s], row_s, row_r, place.sibling).wait_recv()
    for copy in exchange[4:]:
        copy.wait_send()
    pairs = [(nf, nf_o), (qs, q_o), (ks, k_o), (vs, v_o), (ps, p_o), (mx, mx_o), (hf, hf_o), (gs, g_o), (us, u_o)]
    for l in range(2):
        for i, (src, dst) in enumerate(pairs):
            pltpu.make_async_copy(src.at[l], dst.at[l], save_sem.at[l, i]).wait()


def ffn_back_kernel(l, ranks, *refs):
    (lens, dy_in, aux, gains, o_gains, router, o_router, mid, coef, small, hf_i, g_i, u_i) = refs[:13]
    own, other = refs[13:19], refs[19:25]
    (d_mid, grads, gain_grad, router_grad) = refs[25:29]
    (hf, gs, us, wg, wu, wd, dyf, acts, stage, land, tmp, own_part, gate_sum, sent, got) = refs[29:44]
    (ag_s, ag_r, rs_s, rs_r, ex_s, ex_r, load_sem, st_sem) = refs[44:]

    place = Place(ranks)
    s, t = place.s, place.t
    rows, width = dy_in.shape
    seq_len = hf.shape[0]
    experts = wg.shape[0] - 1
    inner = wg.shape[2]
    half = inner // 2
    mine = pl.ds(t * rows, rows)
    here = s == l
    state = [
        pltpu.make_async_copy(src.at[l], dst, st_sem.at[i])
        for i, (src, dst) in enumerate([(g_i, gs), (u_i, us), (hf_i, hf)])
    ]
    targets = [
        wg.at[pl.ds(0, experts)],
        wu.at[pl.ds(0, experts)],
        wd.at[pl.ds(0, experts)],
        wg.at[experts],
        wu.at[experts],
        wd.at[experts],
    ]
    order = (2, 5, 0, 1, 3, 4)
    loads = load_choice(here, [(own[i], other[i], targets[i]) for i in order], load_sem)
    for copy in state:
        copy.start()
    dy = dy_in[...]
    if l == 1:
        position = lax.broadcasted_iota(jnp.int32, (rows, width), 0) + t * rows
        dy = jnp.where(position < lens[s], dy.astype(f32), 0.0).astype(bf16)
    dyf[mine] = dy
    place.greet()
    ag = gather_rows(place, dyf, rows, ag_s, ag_r)
    for copy in loads:
        copy.wait()
    for copy in state:
        copy.wait()
    gate_sum[...] = jnp.zeros_like(gate_sum)
    for copy in ag:
        copy.wait()
    lane8 = lax.broadcasted_iota(jnp.int32, gate_sum.shape, 1)

    def one_expert(e, carry):
        raw = dot(dyf[...], wd[e], 1, 1)
        gate_h = gs[e].astype(f32)
        up_h = us[e].astype(f32)
        sig = jax.nn.sigmoid(gate_h)
        silu = gate_h * sig
        acted = silu * up_h
        inner_sum = jnp.sum(acted * raw, axis=1, keepdims=True)
        gate_sum[...] = jnp.where(lane8 == e, inner_sum, gate_sum[...])
        weight = column(coef[l], e)
        acts[e] = (acted * weight).astype(bf16)
        d_acted = raw * weight
        gs[e] = (d_acted * up_h * (sig + silu * (1.0 - sig))).astype(bf16)
        us[e] = (d_acted * silu).astype(bf16)
        return carry

    lax.fori_loop(0, experts + 1, one_expert, 0)
    chances, gates, per_chosen = small[l, 0:8], small[l, 8:16], small[l, 16:24]
    d_gates = gate_sum[...].T
    common = jnp.sum(d_gates * gates, axis=0, keepdims=True)
    d_chances = per_chosen * (d_gates - common) + jnp.where(t == 0, aux[l], 0.0)
    d_logits = chances * (d_chances - jnp.sum(chances * d_chances, axis=0, keepdims=True))
    d_logits = d_logits.astype(bf16)
    router_grad[...] = dot(d_logits, hf[...], 1, 0)
    route_w = jnp.where(here, router[...], o_router[...])
    scat = []
    for n in range(width // LANES):
        lanes = slice(n * LANES, (n + 1) * LANES)
        total = dot(d_logits, route_w[:, lanes], 0, 0)
        for e in range(experts + 1):
            total = total + dot(gs[e], wg[e, lanes], 1, 1)
            total = total + dot(us[e], wu[e, lanes], 1, 1)
        tmp[...] = total
        stage[:, lanes] = total.astype(bf16)
        own_part[:, lanes] = tmp[mine]
        scat += scatter_block(place, stage, land, rows, n * LANES, LANES, rs_s.at[n], rs_r.at[n])

    theirs = pl.ds(pl.multiple_of((1 - s) * half, half), half)
    ours = pl.ds(pl.multiple_of(s * half, half), half)
    sources = ((hf, gs), (hf, us), (dyf, acts))

    def give(e, carry):
        for j, (left, right) in enumerate(sources):
            sent[e * 3 + j] = dot(left[...], right[e, :, theirs], 0, 0).astype(bf16)
            at = e * 3 + j
            remote(sent.at[at], got.at[at], ex_s.at[at], ex_r.at[at], place.sibling).start()
        return carry

    lax.fori_loop(0, experts + 1, give, 0)
    for copy in scat:
        copy.wait()
    d_hidden = landed_sum(own_part[...], land, ranks)
    gain_f = jnp.where(here, gains[1:2], o_gains[1:2])
    d_norm, g_gain = rms_back(mid[l], gain_f, d_hidden)
    d_mid[...] = dyf[mine].astype(f32) + d_norm
    gain_grad[...] = g_gain

    def keep(e, carry):
        for j, (left, right) in enumerate(sources):
            at = e * 3 + j
            value = dot(left[...], right[e, :, ours], 0, 0)
            remote(sent.at[at], got.at[at], ex_s.at[at], ex_r.at[at], place.sibling).wait()
            lanes = pl.ds(pl.multiple_of((j * (experts + 1) + e) * half, half), half)
            grads[:, lanes] = (value + got[at].astype(f32)).astype(bf16)
        return carry

    lax.fori_loop(0, experts + 1, keep, 0)


def attn_back_kernel(l, ranks, *refs):
    (d_mid, gains, o_gains, tables, xs, nf_i, q_i, k_i, v_i, p_i, mx_i) = refs[:11]
    own, other = refs[11:15], refs[15:19]
    (dx_low, in_grads, grads, gain_grad) = refs[19:23]
    (nf, qs, ks, vs, ps, mx, wq, wk, wv, wo, df, ds, dq, dk, dv, stage, land, tmp, own_part) = refs[23:42]
    (gw, got, row_buf, ag_s, ag_r, rs_s, rs_r, ex_s, ex_r, load_sem, st_sem, row_s, row_r) = refs[42:]

    place = Place(ranks)
    s, t = place.s, place.t
    rows, width = d_mid.shape
    seq_len = nf.shape[0]
    heads = qs.shape[0]
    mine = pl.ds(t * rows, rows)
    here = s == l
    targets = [wq, wk, wv, wo]
    loads = load_choice(here, [(own[i], other[i], targets[i]) for i in range(N_ATTN)], load_sem)
    pairs = [(nf_i, nf), (q_i, qs), (k_i, ks), (v_i, vs), (p_i, ps), (mx_i, mx)]
    state = [pltpu.make_async_copy(src.at[l], dst, st_sem.at[i]) for i, (src, dst) in enumerate(pairs)]
    for copy in state:
        copy.start()
    df[mine] = d_mid[...].astype(bf16)
    place.greet()
    ag = gather_rows(place, df, rows, ag_s, ag_r)
    for copy in loads:
        copy.wait()
    for copy in state:
        copy.wait()
    for copy in ag:
        copy.wait()
    cosine, signed = tables[:, :HEAD_DIM], tables[:, HEAD_DIM:]
    scale = HEAD_DIM ** (-0.5)
    for h in range(heads):
        span = slice(h * HEAD_DIM, (h + 1) * HEAD_DIM)
        d_mixed = dot(df[...], wo[span], 1, 1).astype(bf16)
        for i in range(ranks):
            lo, reach = i * rows, (i + 1) * rows
            weights = ps[h, lo:reach, 0:reach].astype(f32)
            d_probs = dot(d_mixed[lo:reach], vs[h, 0:reach], 1, 1)
            inner = jnp.sum(weights * d_probs, axis=-1, keepdims=True)
            ds[lo:reach, 0:reach] = (weights * (d_probs - inner)).astype(bf16)
            if reach < seq_len:
                ds[lo:reach, reach:] = jnp.zeros((rows, seq_len - reach), bf16)
        d_value = dot(ps[h], d_mixed, 0, 0)
        d_query = dot(ds[...], ks[h], 1, 0) * scale
        d_key = dot(ds[...], qs[h], 0, 0) * scale
        dq[:, span] = (d_query * cosine - turn_halves(d_query) * signed).astype(bf16)
        dk[:, span] = (d_key * cosine - turn_halves(d_key) * signed).astype(bf16)
        dv[:, span] = d_value.astype(bf16)
    scat = []
    for n in range(width // LANES):
        lanes = slice(n * LANES, (n + 1) * LANES)
        total = dot(dq[...], wq[lanes], 1, 1) + dot(dk[...], wk[lanes], 1, 1) + dot(dv[...], wv[lanes], 1, 1)
        tmp[...] = total
        stage[:, lanes] = total.astype(bf16)
        own_part[:, lanes] = tmp[mine]
        scat += scatter_block(place, stage, land, rows, n * LANES, LANES, rs_s.at[n], rs_r.at[n])
    for j, (left, right) in enumerate(((nf, dq), (nf, dk), (nf, dv), (df, mx))):
        gw[j] = dot(left[...], right[...], 0, 0).astype(bf16)
    swap = remote(gw.at[pl.ds((1 - s) * 2, 2)], got, ex_s, ex_r, place.sibling)
    swap.start()
    for copy in scat:
        copy.wait()
    d_normed = landed_sum(own_part[...], land, ranks)
    gain_a = jnp.where(here, gains[0:1], o_gains[0:1])
    d_norm, g_gain = rms_back(xs[l].astype(f32), gain_a, d_normed)
    dx = d_mid[...] + d_norm
    gain_grad[...] = g_gain
    low = dx.astype(bf16)
    dx_low[...] = low
    row_buf[...] = low.astype(f32) if l == 1 else dx

    @pl.when(here)
    def _():
        in_grads[s] = row_buf[...]
        remote(row_buf, in_grads.at[1 - s], row_s, row_r, place.sibling).wait_recv()

    @pl.when(jnp.logical_not(here))
    def _():
        copy = remote(row_buf, in_grads.at[s], row_s, row_r, place.sibling)
        copy.start()
        copy.wait_send()

    swap.wait()
    for j in range(2):
        grads[j] = (gw[2 * s + j].astype(f32) + got[j].astype(f32)).astype(bf16)


def params(collective_id):
    return pltpu.CompilerParams(
        collective_id=collective_id, has_side_effects=True, vmem_limit_bytes=VMEM_LIMIT
    )


def shape_of(*dims, dtype=bf16):
    return jax.ShapeDtypeStruct(dims, dtype)


def on_device(ranks, *args):
    (boundary, lengths, routes, attn_gain, w_query, w_key, w_value, w_out, ffn_gain, router) = args[:10]
    ffn_own = tuple(a[0] for a in args[10:])
    attn_own = (w_query[0], w_key[0], w_value[0], w_out[0])
    section = lax.axis_index("section")
    first_section = section == 0
    rows, width = boundary.shape[2:]
    seqs, seq_len = routes.shape[1:3]
    top = routes.shape[3]
    experts, _, inner = ffn_own[0].shape
    blocks = experts + 1
    heads_width = w_query.shape[2]
    heads = heads_width // HEAD_DIM
    chunks = width // LANES
    half = inner // 2
    dma = pltpu.SemaphoreType.DMA

    expert_ids = jnp.arange(8, dtype=jnp.int32)
    chosen = jnp.any(routes[0][:, None, :, :] == expert_ids[None, :, None, None], axis=-1).astype(f32)
    valid = (jnp.arange(seq_len, dtype=jnp.int32)[None, :] < lengths[:, None]).astype(f32)
    counts_here = jnp.sum(chosen * valid[:, None, :], axis=(0, 2))
    counts_placed = jnp.where(section == jnp.arange(2)[:, None], counts_here[None, :], 0.0)
    counts, doubled = lax.psum(
        (counts_placed, jnp.sum(lengths).astype(f32)), ("section", "dp")
    )
    tokens_all = doubled / 2.0
    share = counts / (top * tokens_all)
    own_valid = jnp.where(first_section, valid[0], valid[1])
    aux = (ALPHA * experts / tokens_all) * share[:, :, None] * own_valid[None, None, :]

    gains = jnp.concatenate([attn_gain, ffn_gain], axis=0)
    router_t = jnp.pad(router[0].T, ((0, 8 - experts), (0, 0)))
    tables = rope_tables(seq_len)

    states = [
        shape_of(2, seq_len, width),
        shape_of(2, heads, seq_len, HEAD_DIM),
        shape_of(2, heads, seq_len, HEAD_DIM),
        shape_of(2, heads, seq_len, HEAD_DIM),
        shape_of(2, heads, seq_len, seq_len),
        shape_of(2, seq_len, heads_width),
        shape_of(2, seq_len, width),
        shape_of(2, blocks, seq_len, inner),
        shape_of(2, blocks, seq_len, inner),
    ]
    weights = attn_own + ffn_own
    ffn_scratch = [
        pltpu.VMEM((blocks, width, inner), bf16),
        pltpu.VMEM((blocks, width, inner), bf16),
        pltpu.VMEM((blocks, inner, width), bf16),
    ]
    attn_scratch = [
        pltpu.VMEM((width, heads_width), bf16),
        pltpu.VMEM((width, heads_width), bf16),
        pltpu.VMEM((width, heads_width), bf16),
        pltpu.VMEM((heads_width, width), bf16),
    ]
    peers = ranks - 1
    result = pl.pallas_call(
        functools.partial(forward_kernel, ranks),
        out_shape=[shape_of(*w.shape) for w in weights]
        + [
            shape_of(2, width, dtype=f32),
            shape_of(8, width),
            shape_of(8, seq_len, dtype=f32),
            shape_of(2, rows, width),
            shape_of(rows, width),
            shape_of(2, 8, 128, dtype=f32),
        ]
        + states
        + [
            shape_of(2, rows, width),
            shape_of(2, rows, width, dtype=f32),
            shape_of(2, seq_len, 8, dtype=f32),
            shape_of(2, 24, seq_len, dtype=f32),
        ],
        in_specs=[SMEM] + [VMEM] * 5 + [ANY] * 10,
        out_specs=[ANY] * 10 + [VMEM] * 6 + [ANY] * 9 + [VMEM] * 4,
        scratch_shapes=[pltpu.VMEM(st.shape, st.dtype) for st in states]
        + attn_scratch
        + ffn_scratch
        + [
            pltpu.VMEM((blocks, seq_len, inner), bf16),
            pltpu.VMEM((seq_len, width), bf16),
            pltpu.VMEM((2, peers, rows, width), bf16),
            pltpu.VMEM((2, peers, rows, width), bf16),
            pltpu.VMEM((seq_len, LANES), f32),
            pltpu.VMEM((rows, width), f32),
            pltpu.VMEM((rows, width), bf16),
            pltpu.VMEM((2, rows, width), bf16),
            dma((2, 2, peers)),
            dma((2, 2, peers)),
            dma((2, peers)),
            dma((2, peers)),
            dma((2, chunks, peers)),
            dma((2, chunks, peers)),
            dma((14,)),
            dma((14,)),
            dma((10,)),
            dma((2, 9)),
            dma,
            dma,
        ],
        compiler_params=params(0),
        name="forward",
    )(lengths, boundary[0], chosen, gains, router_t, tables, *weights)
    other = result[:10]
    (o_gains, o_router, _, out_rows, cot, probs_sum) = result[10:16]
    (nf, qs, ks, vs, ps, mx, hf, gs, us) = result[16:25]
    (xs, mid, coef, small) = result[25:29]

    def ffn_back(l, dy):
        return pl.pallas_call(
            functools.partial(ffn_back_kernel, l, ranks),
            out_shape=[
                shape_of(rows, width, dtype=f32),
                shape_of(width, 3 * blocks * half),
                shape_of(1, width, dtype=f32),
                shape_of(8, width, dtype=f32),
            ],
            in_specs=[SMEM] + [VMEM] * 9 + [ANY] * 15,
            out_specs=[VMEM] * 4,
            scratch_shapes=[
                pltpu.VMEM((seq_len, width), bf16),
                pltpu.VMEM((blocks, seq_len, inner), bf16),
                pltpu.VMEM((blocks, seq_len, inner), bf16),
            ]
            + ffn_scratch
            + [
                pltpu.VMEM((seq_len, width), bf16),
                pltpu.VMEM((blocks, seq_len, inner), bf16),
                pltpu.VMEM((seq_len, width), bf16),
                pltpu.VMEM((peers, rows, width), bf16),
                pltpu.VMEM((seq_len, LANES), f32),
                pltpu.VMEM((rows, width), f32),
                pltpu.VMEM((seq_len, 8), f32),
                pltpu.VMEM((3 * blocks, width, half), bf16),
                pltpu.VMEM((3 * blocks, width, half), bf16),
                dma((peers,)),
                dma((peers,)),
                dma((chunks, peers)),
                dma((chunks, peers)),
                dma((3 * blocks,)),
                dma((3 * blocks,)),
                dma((6,)),
                dma((3,)),
            ],
            compiler_params=params(1 + l),
            name=f"ffn_back_{l}",
        )(lengths, dy, aux, gains, o_gains, router_t, o_router, mid, coef, small, hf, gs, us, *ffn_own, *other[4:])

    def attn_back(l, d_mid):
        return pl.pallas_call(
            functools.partial(attn_back_kernel, l, ranks),
            out_shape=[
                shape_of(rows, width),
                shape_of(seqs, rows, width, dtype=f32),
                shape_of(2, width, heads_width),
                shape_of(1, width, dtype=f32),
            ],
            in_specs=[VMEM] * 5 + [ANY] * 14,
            out_specs=[VMEM] * 4,
            scratch_shapes=[pltpu.VMEM(st.shape[1:], st.dtype) for st in states[:6]]
            + attn_scratch
            + [
                pltpu.VMEM((seq_len, width), bf16),
                pltpu.VMEM((seq_len, seq_len), bf16),
                pltpu.VMEM((seq_len, heads_width), bf16),
                pltpu.VMEM((seq_len, heads_width), bf16),
                pltpu.VMEM((seq_len, heads_width), bf16),
                pltpu.VMEM((seq_len, width), bf16),
                pltpu.VMEM((peers, rows, width), bf16),
                pltpu.VMEM((seq_len, LANES), f32),
                pltpu.VMEM((rows, width), f32),
                pltpu.VMEM((4, width, heads_width), bf16),
                pltpu.VMEM((2, width, heads_width), bf16),
                pltpu.VMEM((rows, width), f32),
                dma((peers,)),
                dma((peers,)),
                dma((chunks, peers)),
                dma((chunks, peers)),
                dma,
                dma,
                dma((4,)),
                dma((6,)),
                dma,
                dma,
            ],
            compiler_params=params(3 + l),
            name=f"attn_back_{l}",
        )(d_mid, gains, o_gains, tables, xs, nf, qs, ks, vs, ps, mx, *attn_own, *other[:4])

    def over_dp(array, dim):
        return lax.psum_scatter(array, "dp", scatter_dimension=dim, tiled=True)

    d_mid_1, ffn_grads_1, ffn_gain_1, router_1 = ffn_back(1, cot)
    ffn_done_1 = over_dp(ffn_grads_1, 0)
    dx_low_1, in_grads_1, attn_grads_1, attn_gain_1 = attn_back(1, d_mid_1)
    attn_done_1 = over_dp(attn_grads_1, 1)
    d_mid_0, ffn_grads_0, ffn_gain_0, router_0 = ffn_back(0, dx_low_1)
    ffn_done_0 = over_dp(ffn_grads_0, 0)
    _, in_grads_0, attn_grads_0, attn_gain_0 = attn_back(0, d_mid_0)
    attn_done_0 = over_dp(attn_grads_0, 1)

    tensor_first = (lax.axis_index("tensor") == 0).astype(f32)
    small_sums = lax.psum(
        jnp.stack(
            [
                jnp.concatenate([attn_gain_0, ffn_gain_0, router_0], axis=0),
                jnp.concatenate([attn_gain_1, ffn_gain_1, router_1], axis=0),
            ]
        ),
        ("section", "tensor", "dp"),
    )
    prob_sum = lax.psum(probs_sum[:, :, 0] * tensor_first, ("section", "tensor", "dp"))
    here_sums = jnp.where(first_section, small_sums[0], small_sums[1])
    here_prob = jnp.where(first_section, prob_sum[0], prob_sum[1])
    here_share = jnp.where(first_section, share[0], share[1])
    balance = (experts * jnp.sum(here_share * here_prob) / tokens_all).reshape(1)

    def swap(first, second):
        mine = jnp.where(first_section, first, second)
        theirs = lax.ppermute(jnp.where(first_section, second, first), "section", [(0, 1), (1, 0)])
        return jnp.where(first_section, mine, theirs), jnp.where(first_section, theirs, mine)

    low_half, high_half = swap(ffn_done_0, ffn_done_1)
    part = low_half.shape[0]
    shaped = [h.reshape(part, 3, blocks, half) for h in (low_half, high_half)]
    merged = jnp.concatenate(shaped, axis=-1).astype(f32)
    expert_gate = merged[:, 0, :experts].transpose(1, 0, 2)
    expert_up = merged[:, 1, :experts].transpose(1, 0, 2)
    expert_down = merged[:, 2, :experts].transpose(1, 2, 0)
    shared_gate, shared_up = merged[:, 0, experts], merged[:, 1, experts]
    shared_down = merged[:, 2, experts].T
    qk, vo = swap(attn_done_0, attn_done_1)
    qk, vo = qk.astype(f32), vo.astype(f32)
    in_grads = jnp.where(first_section, in_grads_0, in_grads_1)
    return (
        out_rows[None],
        in_grads[None],
        here_sums[0][None],
        qk[0][None],
        qk[1][None],
        vo[0][None],
        vo[1].T[None],
        here_sums[1][None],
        here_sums[2 : 2 + experts].T[None],
        expert_gate[None],
        expert_up[None],
        expert_down[None],
        shared_gate[None],
        shared_up[None],
        shared_down[None],
        balance,
    )


def solution(mesh):
    placed = (
        P("section", "dp", "tensor", None),
        P("dp"),
        P("section", "dp", None, None),
        P("section", None),
        P("section", None, "tensor"),
        P("section", None, "tensor"),
        P("section", None, "tensor"),
        P("section", "tensor", None),
        P("section", None),
        P("section", None, None),
        P("section", None, None, "tensor"),
        P("section", None, None, "tensor"),
        P("section", None, "tensor", None),
        P("section", None, "tensor"),
        P("section", None, "tensor"),
        P("section", "tensor", None),
    )
    return jax.shard_map(
        functools.partial(on_device, mesh.shape["tensor"]),
        mesh=mesh,
        in_specs=placed,
        out_specs=(
            P("section", "dp", "tensor", None),
            P("section", "dp", "tensor", None),
            P("section", None),
            P("section", "dp", "tensor"),
            P("section", "dp", "tensor"),
            P("section", "dp", "tensor"),
            P("section", "tensor", "dp"),
            P("section", None),
            P("section", None, None),
            P("section", None, "dp", "tensor"),
            P("section", None, "dp", "tensor"),
            P("section", None, "tensor", "dp"),
            P("section", "dp", "tensor"),
            P("section", "dp", "tensor"),
            P("section", "tensor", "dp"),
            P("section"),
        ),
        check_vma=False,
    )
```

```python
import functools

import jax
import jax.numpy as jnp
import numpy as np
from jax import lax
from jax.experimental import pallas as pl
from jax.experimental.pallas import tpu as pltpu
from jax.sharding import PartitionSpec as P

HEAD_DIM = 64
HALF_DIM = HEAD_DIM // 2
EPSILON = 1e-06
ALPHA = 0.01
THETA = 10000.0
MASKED = -1e30
LANES = 256
VMEM_LIMIT = 63 * 2**20

f32 = jnp.float32
bf16 = jnp.bfloat16
MESH = pl.DeviceIdType.MESH
ANY = pl.BlockSpec(memory_space=pl.ANY)
VMEM = pl.BlockSpec(memory_space=pltpu.VMEM)
SMEM = pl.BlockSpec(memory_space=pltpu.SMEM)


def dot(left, right, left_dim, right_dim):
    return lax.dot_general(
        left, right, (((left_dim,), (right_dim,)), ((), ())), preferred_element_type=f32
    )


def rope_tables(seq_len):
    frequency = (THETA ** (-np.arange(HALF_DIM, dtype=np.float32) / HALF_DIM)).astype(np.float32)
    angles = np.arange(seq_len, dtype=np.float32)[:, None] * frequency[None, :]
    cosine, sine = np.cos(angles), np.sin(angles)
    return np.concatenate([cosine, cosine, -sine, sine], axis=-1).astype(np.float32)


def turn_halves(values):
    return jnp.concatenate([values[:, HALF_DIM:], values[:, :HALF_DIM]], axis=1)


class Place:
    def __init__(self, ranks, planes):
        self.s = lax.axis_index("section")
        self.t = lax.axis_index("tensor")
        self.z = lax.axis_index("dp")
        self.ranks, self.planes = ranks, planes
        self.odd = lax.rem(self.z, 2)
        self.sibling = (1 - self.s, self.t, self.z)
        self.partner = (self.s, self.t, self.z + 1 - 2 * self.odd)

    def peer(self, k):
        return lax.rem(self.t + k, self.ranks)

    def peer_id(self, k):
        return (self.s, self.peer(k), self.z)

    def plane_id(self, k):
        return (self.s, self.t, lax.rem(self.z + k, self.planes))

    def greet(self, both_cores):
        barrier = pltpu.get_barrier_semaphore()
        others = [self.sibling] + [self.peer_id(k) for k in range(1, self.ranks)]
        for k in range(1, self.planes):
            _, t, z = self.plane_id(k)
            others += [(self.s, t, z)] + ([(1 - self.s, t, z)] if both_cores else [])
        for other in others:
            pl.semaphore_signal(barrier, inc=1, device_id=other, device_id_type=MESH)
        pl.semaphore_wait(barrier, len(others))


def remote(src, dst, send, recv, device):
    return pltpu.make_async_remote_copy(
        src_ref=src, dst_ref=dst, send_sem=send, recv_sem=recv, device_id=device, device_id_type=MESH
    )


def gather_rows(place, full, rows, send, recv):
    mine = full.at[pl.ds(place.t * rows, rows)]
    copies = []
    for k in range(1, place.ranks):
        copy = remote(mine, mine, send.at[k - 1], recv.at[k - 1], place.peer_id(k))
        copy.start()
        copies.append(copy)
    return copies


def scatter_block(place, stage, landing, rows, lo, width, send, recv):
    copies = []
    for k in range(1, place.ranks):
        src = stage.at[pl.ds(place.peer(k) * rows, rows), pl.ds(lo, width)]
        dst = landing.at[k - 1, :, pl.ds(lo, width)]
        copy = remote(src, dst, send.at[k - 1], recv.at[k - 1], place.peer_id(k))
        copy.start()
        copies.append(copy)
    return copies


def landed_sum(own, landing, ranks):
    total = own
    for k in range(ranks - 1):
        total = total + landing[k].astype(f32)
    return total


def rms_rows(values, gain):
    return values * lax.rsqrt(jnp.mean(values * values, axis=-1, keepdims=True) + EPSILON) * gain


def rms_back(values, gain, grad):
    r = lax.rsqrt(jnp.mean(values * values, axis=-1, keepdims=True) + EPSILON)
    normed = values * r
    scaled = grad * gain
    inner = jnp.mean(scaled * normed, axis=-1, keepdims=True)
    return r * (scaled - normed * inner), jnp.sum(grad * normed, axis=0, keepdims=True)


def name_rows(routes):
    expert = lax.broadcasted_iota(jnp.int32, (8, routes.shape[1]), 0)
    named = routes[0:1] == expert
    for j in range(1, routes.shape[0]):
        named = named | (routes[j : j + 1] == expert)
    return named.astype(f32)


def column(matrix, index):
    lane = lax.broadcasted_iota(jnp.int32, matrix.shape, 1)
    return jnp.sum(jnp.where(lane == index, matrix, 0.0), axis=1, keepdims=True)


def load_choice(first, pairs, sems):
    for i, (own, other, dst) in enumerate(pairs):

        @pl.when(first)
        def _(own=own, dst=dst, i=i):
            pltpu.make_async_copy(own, dst, sems.at[i]).start()

        @pl.when(jnp.logical_not(first))
        def _(other=other, dst=dst, i=i):
            pltpu.make_async_copy(other, dst, sems.at[i]).start()

    return [pltpu.make_async_copy(own, dst, sems.at[i]) for i, (own, other, dst) in enumerate(pairs)]


N_ATTN = 4
N_FFN = 6
N_STATE = 9


def attn_targets(w_in, w_out, heads_width):
    return [w_in.at[pl.ds(i * heads_width, heads_width)] for i in range(3)] + [w_out]


def ffn_targets(wg, wu, wd):
    experts = wg.shape[0] - 1
    first = pl.ds(0, experts)
    return [wg.at[first], wu.at[first], wd.at[first], wg.at[experts], wu.at[experts], wd.at[experts]]


def forward_kernel(ranks, planes, lens, bnd, routes, gain_a_own, gain_f_own, router, tables, *refs):
    own, refs = refs[:10], refs[10:]
    other, refs = refs[:10], refs[10:]
    (o_gain_a, o_gain_f, o_router, out_rows, cot, probs_sum, cnt, o_cnt), refs = refs[:8], refs[8:]
    (nf_o, q_o, k_o, v_o, p_o, mx_o, hf_o, g_o, u_o, hp_o), refs = refs[:10], refs[10:]
    (xs, mid, small, o_small), refs = refs[:4], refs[4:]
    (nf, qs, ks, vs, ps, mx, hf, gs, us), refs = refs[:9], refs[9:]
    (w_in, wo, wg, wu, wd, acts, stage, land_a, land_f, tmp, own_part), refs = refs[:11], refs[11:]
    (o_bnd, o_routes, y_low, coef, cnt_in), refs = refs[:5], refs[5:]
    (ag_s, ag_r, rsa_s, rsa_r, rsf_s, rsf_r, ex_s, ex_r, load_sem, save_sem, row_s, row_r), refs = (
        refs[:12],
        refs[12:],
    )
    (hp_s, hp_r, cz_s, cz_r, cs_s, cs_r) = refs

    place = Place(ranks, planes)
    s, t = place.s, place.t
    rows, width = bnd.shape[1], bnd.shape[2]
    seq_len = nf.shape[1]
    experts = wg.shape[0] - 1
    heads = qs.shape[1]
    heads_width = heads * HEAD_DIM
    mine = pl.ds(t * rows, rows)
    place.greet(False)

    ex_pairs = [
        (bnd.at[1 - s], o_bnd),
        (gain_a_own, o_gain_a),
        (gain_f_own, o_gain_f),
        (router, o_router),
        (routes.at[1 - s], o_routes),
    ] + [(own[i], other[i]) for i in range(10)]
    exchange = [
        remote(src, dst, ex_s.at[i], ex_r.at[i], place.sibling) for i, (src, dst) in enumerate(ex_pairs)
    ]
    for copy in exchange:
        copy.start()
    first_w = 5
    here_tokens = lax.broadcasted_iota(jnp.int32, (8, seq_len), 1)
    counted = jnp.zeros((8, 1), f32)
    for q in range(2):
        live = jnp.where(here_tokens < lens[q], 1.0, 0.0)
        row8 = lax.broadcasted_iota(jnp.int32, (8, seq_len), 0)
        counts = jnp.where(row8 == 7, live, name_rows(routes[q]) * live)
        counted = counted + jnp.sum(counts, axis=1, keepdims=True)
    cnt[...] = jnp.broadcast_to(counted, cnt.shape)
    count_copies = []
    for k in range(1, planes):
        copy = remote(cnt, cnt_in.at[k - 1], cz_s.at[k - 1], cz_r.at[k - 1], place.plane_id(k))
        copy.start()
        count_copies.append(copy)
    for copy in exchange[:first_w]:
        copy.wait()
    is_first = s == 0
    xs[0] = jnp.where(is_first, bnd[0], o_bnd[...])
    xs[1] = jnp.zeros_like(xs[1])
    cot[...] = jnp.where(is_first, o_bnd[...], bnd[1])
    length = lens[s]

    def layer(l, carry):
        here = s == l
        gain_a = jnp.where(here, gain_a_own[...], o_gain_a[...])
        gain_f = jnp.where(here, gain_f_own[...], o_gain_f[...])
        x = xs[l].astype(f32)
        nf[l, mine] = rms_rows(x, gain_a).astype(bf16)
        ag = gather_rows(place, nf.at[l], rows, ag_s.at[l, 0], ag_r.at[l, 0])

        @pl.when(jnp.logical_not(here))
        def _():
            for copy in exchange[first_w : first_w + N_ATTN]:
                copy.wait_recv()

        attn_dst = attn_targets(w_in, wo, heads_width)
        loads = load_choice(here, [(own[i], other[i], attn_dst[i]) for i in range(N_ATTN)], load_sem)

        @pl.when(jnp.logical_not(here))
        def _():
            for copy in exchange[first_w + N_ATTN :]:
                copy.wait_recv()

        ffn_dst = ffn_targets(wg, wu, wd)
        ffn_loads = load_choice(
            here,
            [(own[4 + i], other[4 + i], ffn_dst[i]) for i in range(N_FFN)],
            load_sem.at[pl.ds(N_ATTN, N_FFN)],
        )
        for copy in loads:
            copy.wait()
        for copy in ag:
            copy.wait()
        pltpu.make_async_copy(nf.at[l], nf_o.at[l], save_sem.at[l, 0]).start()
        cosine, signed = tables[:, :HEAD_DIM], tables[:, HEAD_DIM:]
        projected = dot(nf[l], w_in[...], 1, 1)
        for j, dst in enumerate((qs, ks, vs)):
            for h in range(heads):
                at = j * heads_width + h * HEAD_DIM
                piece = projected[:, at : at + HEAD_DIM]
                if j < 2:
                    piece = piece * cosine + turn_halves(piece) * signed
                dst[l, h] = piece.astype(bf16)
        for i in range(ranks):
            lo, reach = i * rows, (i + 1) * rows
            place_q = lax.broadcasted_iota(jnp.int32, (rows, reach), 0) + lo
            place_k = lax.broadcasted_iota(jnp.int32, (rows, reach), 1)
            allowed = (place_k <= place_q) & (place_k < length)
            for h in range(heads):
                scores = dot(qs[l, h, lo:reach], ks[l, h, 0:reach], 1, 1) * HEAD_DIM ** (-0.5)
                scores = jnp.where(allowed, scores, MASKED)
                peak = jnp.max(scores, axis=-1, keepdims=True)
                raised = jnp.exp(scores - peak)
                total = jnp.sum(raised, axis=-1, keepdims=True)
                weights = (raised / total).astype(bf16)
                ps[l, h, lo:reach, 0:reach] = weights
                if reach < seq_len:
                    ps[l, h, lo:reach, reach:] = jnp.zeros((rows, seq_len - reach), bf16)
                mixed = dot(weights, vs[l, h, 0:reach], 1, 0)
                mx[l, lo:reach, h * HEAD_DIM : (h + 1) * HEAD_DIM] = mixed.astype(bf16)
            part = dot(mx[l, lo:reach], wo[...], 1, 0)
            stage[lo:reach] = part.astype(bf16)

            @pl.when(t == i)
            def _(part=part):
                own_part[...] = part

            @pl.when(t != i)
            def _(i=i, lo=lo):
                k = lax.rem(i - t + ranks, ranks)
                remote(
                    stage.at[pl.ds(lo, rows)],
                    land_a.at[l, k - 1],
                    rsa_s.at[l, k - 1],
                    rsa_r.at[l, k - 1],
                    (s, i, place.z),
                ).start()

        saves = [(qs, q_o), (ks, k_o), (vs, v_o), (ps, p_o), (mx, mx_o)]
        for i, (src, dst) in enumerate(saves):
            pltpu.make_async_copy(src.at[l], dst.at[l], save_sem.at[l, 1 + i]).start()

        @pl.when(l == 1)
        def _():
            for copy in count_copies:
                copy.wait()
            total = cnt[...]
            for k in range(planes - 1):
                total = total + cnt_in[k]
            cnt[...] = total
            remote(cnt, o_cnt, cs_s, cs_r, place.sibling).start()

        for k in range(1, ranks):
            remote(
                stage.at[pl.ds(place.peer(k) * rows, rows)],
                land_a.at[l, k - 1],
                rsa_s.at[l, k - 1],
                rsa_r.at[l, k - 1],
                place.peer_id(k),
            ).wait()
        middle = x + landed_sum(own_part[...], land_a.at[l], ranks)
        mid[l] = middle
        hf[l, mine] = rms_rows(middle, gain_f).astype(bf16)
        ag = gather_rows(place, hf.at[l], rows, ag_s.at[l, 1], ag_r.at[l, 1])
        for copy in ffn_loads:
            copy.wait()
        for copy in ag:
            copy.wait()
        pltpu.make_async_copy(hf.at[l], hf_o.at[l], save_sem.at[l, 6]).start()
        remote(hf.at[l], hp_o.at[l], hp_s.at[l, 0], hp_r.at[l, 0], place.partner).start()
        hidden = hf[l]
        route_w = jnp.where(here, router[...], o_router[...])
        names = name_rows(jnp.where(here, routes[s], o_routes[...]))
        logits = dot(route_w, hidden, 1, 1)
        expert_row = lax.broadcasted_iota(jnp.int32, logits.shape, 0)
        logits = jnp.where(expert_row < experts, logits, MASKED)
        raised = jnp.exp(logits - jnp.max(logits, axis=0, keepdims=True))
        raised = jnp.where(expert_row < experts, raised, 0.0)
        chances = raised / jnp.sum(raised, axis=0, keepdims=True)
        per_chosen = names / jnp.sum(chances * names, axis=0, keepdims=True)
        gates = chances * per_chosen
        small[l, 0:8] = chances
        small[l, 8:16] = gates
        small[l, 16:24] = per_chosen
        remote(small.at[l], o_small.at[l], hp_s.at[l, 1], hp_r.at[l, 1], place.partner).start()
        token = lax.broadcasted_iota(jnp.int32, logits.shape, 1)
        summed = jnp.sum(jnp.where(token < length, chances, 0.0), axis=1, keepdims=True)
        probs_sum[l] = jnp.broadcast_to(summed, (8, 128))
        coef[...] = jnp.where(expert_row == experts, 1.0, gates).T

        def one_expert(e, carry):
            gate_h = dot(hf[l], wg[e], 1, 0)
            up_h = dot(hf[l], wu[e], 1, 0)
            gs[l, e] = gate_h.astype(bf16)
            us[l, e] = up_h.astype(bf16)
            weight = column(coef[...], e)
            acts[e] = (gate_h * jax.nn.sigmoid(gate_h) * up_h * weight).astype(bf16)
            return carry

        lax.fori_loop(0, experts + 1, one_expert, 0)
        pltpu.make_async_copy(gs.at[l], g_o.at[l], save_sem.at[l, 7]).start()
        pltpu.make_async_copy(us.at[l], u_o.at[l], save_sem.at[l, 8]).start()
        scat = []
        for n in range(width // LANES):
            lanes = slice(n * LANES, (n + 1) * LANES)
            total = dot(acts[0], wd[0, :, lanes], 1, 0)
            for e in range(1, experts + 1):
                total = total + dot(acts[e], wd[e, :, lanes], 1, 0)
            tmp[...] = total
            stage[:, lanes] = total.astype(bf16)
            own_part[:, lanes] = tmp[mine]
            scat += scatter_block(
                place, stage, land_f.at[l], rows, n * LANES, LANES, rsf_s.at[l, n], rsf_r.at[l, n]
            )
        for copy in scat:
            copy.wait()
        output = mid[l] + landed_sum(own_part[...], land_f.at[l], ranks)
        y_low[l] = output.astype(bf16)
        xs[1] = jnp.where(l == 0, y_low[l], xs[1])

        @pl.when(here)
        def _():
            out_rows[s] = y_low[l]

        @pl.when(jnp.logical_not(here))
        def _():
            remote(y_low.at[l], out_rows.at[s], row_s, row_r, place.sibling).start()

        return carry

    lax.fori_loop(0, 2, layer, 0)
    remote(y_low.at[1 - s], out_rows.at[s], row_s, row_r, place.sibling).wait_send()
    remote(y_low.at[1 - s], out_rows.at[1 - s], row_s, row_r, place.sibling).wait_recv()
    remote(cnt, o_cnt, cs_s, cs_r, place.sibling).wait()
    for copy in exchange[first_w:]:
        copy.wait_send()
    pairs = [(nf, nf_o), (qs, q_o), (ks, k_o), (vs, v_o), (ps, p_o), (mx, mx_o), (hf, hf_o), (gs, g_o), (us, u_o)]
    for l in range(2):
        remote(hf.at[l], hp_o.at[l], hp_s.at[l, 0], hp_r.at[l, 0], place.partner).wait()
        remote(small.at[l], o_small.at[l], hp_s.at[l, 1], hp_r.at[l, 1], place.partner).wait()
        for i, (src, dst) in enumerate(pairs):
            pltpu.make_async_copy(src.at[l], dst.at[l], save_sem.at[l, i]).wait()


def back_kernel(ranks, planes, top, *refs):
    (lens, cot, gain_a_own, o_gain_a, gain_f_own, o_gain_f, router, o_router, tables), refs = refs[:9], refs[9:]
    (xs, mid, small, small_p, probs_sum, cnt, o_cnt), refs = refs[:7], refs[7:]
    (nf_i, q_i, k_i, v_i, p_i, mx_i, hf_i, g_i, u_i, hp_i), refs = refs[:10], refs[10:]
    own, refs = refs[:10], refs[10:]
    other, refs = refs[:10], refs[10:]
    (in_grads, wq_out, wk_out, wv_out, wo_out, gain_a_out, gain_f_out, router_out, balance), refs = (
        refs[:9],
        refs[9:],
    )
    ffn_outs, refs = refs[:6], refs[6:]
    (hf, gs, us, hp, wg, wu, wd), refs = refs[:7], refs[7:]
    (nf, qs, ks, vs, ps, mx, w_in, wo), refs = refs[:8], refs[8:]
    (dyf, dyp, acts, gp, up, ap, coef, coef_p, gate_sum), refs = refs[:9], refs[9:]
    (stage, land_f, land_a, tmp, own_part, d_mid), refs = refs[:6], refs[6:]
    (sent, got, quarter, land, df, ds, dqkv), refs = refs[:7], refs[7:]
    (gw, got_a, half_a, land_z, row_buf, packs, pack_t, pack_z, steps), refs = refs[:9], refs[9:]
    (ag_s, ag_r, rs_s, rs_r, agd_s, agd_r, rsd_s, rsd_r, dp_s, dp_r, ex_s, ex_r), refs = refs[:12], refs[12:]
    (zs, zr, zl, as_s, as_r, az_s, az_r, az_l, row_s, row_r, pk_s, pk_r), refs = refs[:12], refs[12:]
    (pt_s, pt_r, pz_s, pz_r, ffn_sem, attn_sem, step_sem) = refs

    place = Place(ranks, planes)
    s, t, z, odd = place.s, place.t, place.z, place.odd
    rows, width = cot.shape
    seq_len = hf.shape[0]
    experts = wg.shape[0] - 1
    blocks = experts + 1
    inner = wg.shape[2]
    half = inner // 2
    part = half // 2
    heads = qs.shape[0]
    heads_width = heads * HEAD_DIM
    chunk = width // planes
    mine = pl.ds(t * rows, rows)
    here_lanes = pl.ds(pl.multiple_of(odd * half, half), half)
    slot = s * planes + z
    scale = HEAD_DIM ** (-0.5)

    def ffn_loads(l):
        pairs = [(g_i, gs), (u_i, us), (hf_i, hf), (hp_i, hp)]
        state = [
            pltpu.make_async_copy(src.at[l], dst, ffn_sem.at[N_FFN + i]) for i, (src, dst) in enumerate(pairs)
        ]
        for copy in state:
            copy.start()
        targets = ffn_targets(wg, wu, wd)
        order = (2, 5, 0, 1, 3, 4)
        return state + load_choice(s == l, [(own[4 + i], other[4 + i], targets[i]) for i in order], ffn_sem)

    def attn_loads(l):
        pairs = [(nf_i, nf), (q_i, qs), (k_i, ks), (v_i, vs), (p_i, ps), (mx_i, mx)]
        state = [
            pltpu.make_async_copy(src.at[l], dst, attn_sem.at[N_ATTN + i])
            for i, (src, dst) in enumerate(pairs)
        ]
        for copy in state:
            copy.start()
        targets = attn_targets(w_in, wo, heads_width)
        return state + load_choice(s == l, [(own[i], other[i], targets[i]) for i in range(N_ATTN)], attn_sem)

    def to_owner(l, src, dst, send, recv, local):
        for c in range(planes):
            own_copy = (z == c) & (s == l)

            @pl.when(own_copy)
            def _(c=c):
                pltpu.make_async_copy(src(c), dst, local).start()

            @pl.when(jnp.logical_not(own_copy))
            def _(c=c):
                remote(src(c), dst, send.at[c], recv.at[slot], (l, t, c)).start()

    def sent_to_owner(l, whole, dst, send, recv, local):
        for c in range(planes):
            own_copy = (z == c) & (s == l)

            @pl.when(own_copy)
            def _(c=c):
                pltpu.make_async_copy(whole.at[c], dst.at[slot], local).wait()

            @pl.when(jnp.logical_not(own_copy))
            def _(c=c):
                remote(whole.at[c], dst.at[slot], send.at[c], recv.at[slot], (l, t, c)).wait_send()

    def arrived(dst, send, recv):
        for source in range(2 * planes):

            @pl.when(source != slot)
            def _(source=source):
                remote(
                    dst.at[source], dst.at[source], send.at[0], recv.at[source], place.sibling
                ).wait_recv()

    pending_ffn = ffn_loads(1)
    pending_attn = attn_loads(1)
    position = lax.broadcasted_iota(jnp.int32, (rows, width), 0) + t * rows
    dyf[mine] = jnp.where(position < lens[s], cot[...].astype(f32), 0.0).astype(bf16)
    place.greet(True)
    ag = gather_rows(place, dyf, rows, ag_s.at[1], ag_r.at[1])

    for l in (1, 0):
        here = s == l
        for copy in pending_ffn:
            copy.wait()
        expert_row = lax.broadcasted_iota(jnp.int32, (8, seq_len), 0)
        coef[...] = jnp.where(expert_row == experts, 1.0, small[l, 8:16]).T
        coef_p[...] = jnp.where(expert_row == experts, 1.0, small_p[l, 8:16]).T
        gate_sum[...] = jnp.zeros_like(gate_sum)
        for copy in ag:
            copy.wait()
        to_partner = remote(dyf, dyp.at[l], dp_s.at[l], dp_r.at[l], place.partner)
        to_partner.start()

        def one_expert(e, carry, l=l):
            raw = dot(dyf[...], wd[e], 1, 1)
            gate_h = gs[e].astype(f32)
            up_h = us[e].astype(f32)
            sig = jax.nn.sigmoid(gate_h)
            silu = gate_h * sig
            acted = silu * up_h
            inner_sum = jnp.sum(acted * raw, axis=1, keepdims=True)
            lane8 = lax.broadcasted_iota(jnp.int32, gate_sum.shape, 1)
            gate_sum[...] = jnp.where(lane8 == e, inner_sum, gate_sum[...])
            weight = column(coef[...], e)
            chosen_acts = acted * weight
            acts[e] = jnp.where(odd == 0, chosen_acts[:, :half], chosen_acts[:, half:]).astype(bf16)
            d_acted = raw * weight
            gs[e] = (d_acted * up_h * (sig + silu * (1.0 - sig))).astype(bf16)
            us[e] = (d_acted * silu).astype(bf16)
            return carry

        lax.fori_loop(0, blocks, one_expert, 0)
        chances, gates, per_chosen = small[l, 0:8], small[l, 8:16], small[l, 16:24]
        totals = jnp.where(here, cnt[...], o_cnt[...])
        tokens_all = totals[7:8, 0:1]
        share = totals[:, 0:1] / (top * tokens_all)
        token = lax.broadcasted_iota(jnp.int32, (8, seq_len), 1)
        aux = jnp.where((token < lens[s]) & (t == 0), ALPHA * experts * share / tokens_all, 0.0)
        d_gates = gate_sum[...].T
        common = jnp.sum(d_gates * gates, axis=0, keepdims=True)
        d_chances = per_chosen * (d_gates - common) + aux
        d_logits = chances * (d_chances - jnp.sum(chances * d_chances, axis=0, keepdims=True))
        d_logits = d_logits.astype(bf16)
        router_grad = dot(d_logits, hf[...], 1, 0)
        route_w = jnp.where(here, router[...], o_router[...])
        scat = []
        for n in range(width // LANES):
            lanes = slice(n * LANES, (n + 1) * LANES)
            total = dot(d_logits, route_w[:, lanes], 0, 0)
            for e in range(blocks):
                total = total + dot(gs[e], wg[e, lanes], 1, 1)
                total = total + dot(us[e], wu[e, lanes], 1, 1)
            tmp[...] = total
            stage[:, lanes] = total.astype(bf16)
            own_part[:, lanes] = tmp[mine]
            scat += scatter_block(
                place, stage, land_f, rows, n * LANES, LANES, rs_s.at[l, n], rs_r.at[l, n]
            )
        to_partner.wait()

        def partner_expert(e, carry, l=l):
            gate_h = dot(hp[...], wg[e, :, here_lanes], 1, 0)
            up_h = dot(hp[...], wu[e, :, here_lanes], 1, 0)
            raw = dot(dyp[l], wd[e, here_lanes], 1, 1)
            sig = jax.nn.sigmoid(gate_h)
            silu = gate_h * sig
            weight = column(coef_p[...], e)
            ap[e] = (silu * up_h * weight).astype(bf16)
            d_acted = raw * weight
            gp[e] = (d_acted * up_h * (sig + silu * (1.0 - sig))).astype(bf16)
            up[e] = (d_acted * silu).astype(bf16)
            return carry

        lax.fori_loop(0, blocks, partner_expert, 0)
        for copy in scat:
            copy.wait()
        d_hidden = landed_sum(own_part[...], land_f, ranks)
        gain_f = jnp.where(here, gain_f_own[...], o_gain_f[...])
        d_norm, gain_f_grad = rms_back(mid[l], gain_f, d_hidden)
        d_mid[...] = dyf[mine].astype(f32) + d_norm
        df[mine] = d_mid[...].astype(bf16)
        ag = gather_rows(place, df, rows, agd_s.at[l], agd_r.at[l])

        def swap_of(e, l=l):
            return remote(sent.at[lax.rem(e, 2)], got.at[e], ex_s.at[e], ex_r.at[e], place.sibling)

        def finish(e, l=l):
            swap_of(e).wait()
            for j in range(3):
                at = e * 3 + j
                for c in range(planes):
                    quarter[l, c, at] = (
                        quarter[l, c, at].astype(f32) + got[e, j, c].astype(f32)
                    ).astype(bf16)
            three = pl.ds(e * 3, 3)
            to_owner(
                l, lambda c: quarter.at[l, c, three], land.at[slot, three], zs.at[l], zr, zl.at[l]
            )

        def weight_grads(e, carry, l=l):
            sources = ((hf, gs, hp, gp), (hf, us, hp, up))
            for j in range(3):
                if j < 2:
                    left, right, left_p, right_p = sources[j]
                    value = dot(left[...], right[e, :, here_lanes], 0, 0) + dot(left_p[...], right_p[e], 0, 0)
                else:
                    value = dot(dyf[...], acts[e], 0, 0) + dot(dyp[l], ap[e], 0, 0)
                low, high = value[:, :part], value[:, part:]
                kept = jnp.where(s == 0, low, high).astype(bf16)
                given = jnp.where(s == 0, high, low).astype(bf16)
                for c in range(planes):
                    quarter[l, c, e * 3 + j] = kept[c * chunk : (c + 1) * chunk]
                    sent[lax.rem(e, 2), j, c] = given[c * chunk : (c + 1) * chunk]
            swap_of(e).start()

            @pl.when(e > 0)
            def _():
                finish(e - 1)

            return carry

        lax.fori_loop(0, blocks, weight_grads, 0)
        finish(blocks - 1)
        if l == 1:
            pending_ffn = ffn_loads(0)
        for copy in pending_attn:
            copy.wait()
        for copy in ag:
            copy.wait()
        cosine, signed = tables[:, :HEAD_DIM], tables[:, HEAD_DIM:]
        for h in range(heads):
            span = slice(h * HEAD_DIM, (h + 1) * HEAD_DIM)
            d_mixed = dot(df[...], wo[span], 1, 1).astype(bf16)
            for i in range(ranks):
                lo, reach = i * rows, (i + 1) * rows
                weights = ps[h, lo:reach, 0:reach].astype(f32)
                d_probs = dot(d_mixed[lo:reach], vs[h, 0:reach], 1, 1)
                total = jnp.sum(weights * d_probs, axis=-1, keepdims=True)
                ds[lo:reach, 0:reach] = (weights * (d_probs - total)).astype(bf16)
                if reach < seq_len:
                    ds[lo:reach, reach:] = jnp.zeros((rows, seq_len - reach), bf16)
            d_value = dot(ps[h], d_mixed, 0, 0)
            d_query = dot(ds[...], ks[h], 1, 0) * scale
            d_key = dot(ds[...], qs[h], 0, 0) * scale
            d_query = d_query * cosine - turn_halves(d_query) * signed
            d_key = d_key * cosine - turn_halves(d_key) * signed
            for j, value in enumerate((d_query, d_key, d_value)):
                at = j * heads_width + h * HEAD_DIM
                dqkv[:, at : at + HEAD_DIM] = value.astype(bf16)
        scat = []
        for n in range(width // LANES):
            lanes = slice(n * LANES, (n + 1) * LANES)
            total = dot(dqkv[...], w_in[:, lanes], 1, 0)
            tmp[...] = total
            stage[:, lanes] = total.astype(bf16)
            own_part[:, lanes] = tmp[mine]
            scat += scatter_block(
                place, stage, land_a, rows, n * LANES, LANES, rsd_s.at[l, n], rsd_r.at[l, n]
            )
        three_widths = 3 * heads_width
        gw[:, :three_widths] = dot(nf[...], dqkv[...], 0, 0).astype(bf16)
        gw[:, three_widths:] = dot(df[...], mx[...], 0, 0).astype(bf16)
        side = 2 * heads_width
        swap = remote(
            gw.at[:, pl.ds(pl.multiple_of((1 - s) * side, 128), side)], got_a, as_s.at[l], as_r.at[l], place.sibling
        )
        swap.start()
        for copy in scat:
            copy.wait()
        d_normed = landed_sum(own_part[...], land_a, ranks)
        gain_a = jnp.where(here, gain_a_own[...], o_gain_a[...])
        d_norm, gain_a_grad = rms_back(xs[l].astype(f32), gain_a, d_normed)
        dx = d_mid[...] + d_norm
        if l == 1:
            low_dx = dx.astype(bf16)
            dyf[mine] = low_dx
            ag = gather_rows(place, dyf, rows, ag_s.at[0], ag_r.at[0])
            dx = low_dx.astype(f32)
        swap.wait()
        kept = gw[:, pl.ds(pl.multiple_of(s * side, 128), side)].astype(f32) + got_a[...].astype(f32)
        kept = kept.astype(bf16)
        if l == 0:
            sent_to_owner(1, half_a, land_z, az_s.at[1], az_r, az_l.at[1])
        for c in range(planes):
            half_a[c] = kept[c * chunk : (c + 1) * chunk]
        to_owner(l, lambda c: half_a.at[c], land_z.at[slot], az_s.at[l], az_r, az_l.at[l])
        if l == 1:
            pending_attn = attn_loads(0)
        pack = jnp.concatenate(
            [
                jnp.concatenate([gain_a_grad, gain_f_grad, jnp.zeros((6, width), f32), router_grad], axis=0),
                jnp.concatenate(
                    [jnp.zeros((8, 128), f32), jnp.where(t == 0, probs_sum[l], 0.0)], axis=0
                ),
            ],
            axis=1,
        )

        @pl.when(here)
        def _(dx=dx, pack=pack):
            in_grads[s] = dx
            packs[0] = pack

        @pl.when(jnp.logical_not(here))
        def _(dx=dx, pack=pack):
            row_buf[...] = dx
            packs[1] = pack
            remote(row_buf, in_grads.at[s], row_s, row_r, place.sibling).start()
            remote(packs.at[1], packs.at[2], pk_s, pk_r, place.sibling).start()

    remote(packs.at[1], packs.at[2], pk_s, pk_r, place.sibling).wait()
    packs[0] = packs[0] + packs[2]
    copies = []
    for k in range(1, ranks):
        copy = remote(packs.at[0], pack_t.at[k - 1], pt_s.at[k - 1], pt_r.at[k - 1], place.peer_id(k))
        copy.start()
        copies.append(copy)
    for copy in copies:
        copy.wait()
    total = packs[0]
    for k in range(ranks - 1):
        total = total + pack_t[k]
    packs[0] = total
    copies = []
    for k in range(1, planes):
        copy = remote(packs.at[0], pack_z.at[k - 1], pz_s.at[k - 1], pz_r.at[k - 1], place.plane_id(k))
        copy.start()
        copies.append(copy)
    for copy in copies:
        copy.wait()
    total = packs[0]
    for k in range(planes - 1):
        total = total + pack_z[k]
    gain_a_out[...] = total[0:1, :width]
    gain_f_out[...] = total[1:2, :width]
    router_out[...] = total[8 : 8 + experts, :width]
    tokens_all = cnt[7:8, 0:1]
    products = cnt[0:experts, 0:1] / (top * tokens_all) * total[8 : 8 + experts, width : width + 1]
    balance[...] = experts * jnp.sum(products, axis=0, keepdims=True) / tokens_all

    remote(row_buf, in_grads.at[s], row_s, row_r, place.sibling).wait_send()
    remote(row_buf, in_grads.at[1 - s], row_s, row_r, place.sibling).wait_recv()
    for l in (1, 0):
        sent_to_owner(l, quarter.at[l], land, zs.at[l], zr, zl.at[l])
    sent_to_owner(0, half_a, land_z, az_s.at[0], az_r, az_l.at[0])
    arrived(land, zs.at[0], zr)
    pieces = []
    for e in range(blocks):
        for j in range(3):
            at = len(pieces)
            room = at % 2
            if e < experts:
                target = ffn_outs[j].at[e]
            else:
                target = ffn_outs[3 + j]
            if at >= 2:
                pieces[at - 2].wait()
            for core in range(2):
                for parity in range(2):
                    value = land[core * planes + parity, e * 3 + j].astype(f32)
                    for pair in range(1, planes // 2):
                        value = value + land[core * planes + 2 * pair + parity, e * 3 + j].astype(f32)
                    lo = (2 * parity + core) * part
                    steps[room, :, lo : lo + part] = value
            copy = pltpu.make_async_copy(steps.at[room], target, step_sem.at[room])
            copy.start()
            pieces.append(copy)
    arrived(land_z, az_s.at[0], az_r)
    sides = []
    for core in range(2):
        value = land_z[core * planes].astype(f32)
        for plane in range(1, planes):
            value = value + land_z[core * planes + plane].astype(f32)
        sides.append(value)
    wq_out[...] = sides[0][:, :heads_width]
    wk_out[...] = sides[0][:, heads_width:]
    wv_out[...] = sides[1][:, :heads_width]
    wo_out[...] = sides[1][:, heads_width:].T
    for copy in pieces[-2:]:
        copy.wait()


def params(collective_id):
    return pltpu.CompilerParams(
        collective_id=collective_id, has_side_effects=True, vmem_limit_bytes=VMEM_LIMIT
    )


def shape_of(*dims, dtype=bf16):
    return jax.ShapeDtypeStruct(dims, dtype)


def on_device(ranks, planes, *args):
    (boundary, lengths, routes, attn_gain, w_query, w_key, w_value, w_out, ffn_gain, router) = args[:10]
    ffn_own = tuple(a[0] for a in args[10:])
    attn_own = (w_query[0].T, w_key[0].T, w_value[0].T, w_out[0])
    rows, width = boundary.shape[2:]
    seqs, seq_len = routes.shape[1:3]
    top = routes.shape[3]
    experts, _, inner = ffn_own[0].shape
    blocks = experts + 1
    heads_width = w_query.shape[2]
    heads = heads_width // HEAD_DIM
    chunks = width // LANES
    half, part = inner // 2, inner // 4
    chunk = width // planes
    peers = ranks - 1
    dma = pltpu.SemaphoreType.DMA

    routes_t = jnp.swapaxes(routes[0], 1, 2)
    router_t = jnp.pad(router[0].T, ((0, 8 - experts), (0, 0)))
    tables = jnp.asarray(rope_tables(seq_len))

    states = [
        shape_of(2, seq_len, width),
        shape_of(2, heads, seq_len, HEAD_DIM),
        shape_of(2, heads, seq_len, HEAD_DIM),
        shape_of(2, heads, seq_len, HEAD_DIM),
        shape_of(2, heads, seq_len, seq_len),
        shape_of(2, seq_len, heads_width),
        shape_of(2, seq_len, width),
        shape_of(2, blocks, seq_len, inner),
        shape_of(2, blocks, seq_len, inner),
    ]
    partner_hidden = shape_of(2, seq_len, width)
    weights = attn_own + ffn_own
    ffn_scratch = [
        pltpu.VMEM((blocks, width, inner), bf16),
        pltpu.VMEM((blocks, width, inner), bf16),
        pltpu.VMEM((blocks, inner, width), bf16),
    ]
    attn_scratch = [pltpu.VMEM((3 * heads_width, width), bf16), pltpu.VMEM((heads_width, width), bf16)]
    result = pl.pallas_call(
        functools.partial(forward_kernel, ranks, planes),
        out_shape=[shape_of(*w.shape) for w in weights]
        + [
            shape_of(1, width, dtype=f32),
            shape_of(1, width, dtype=f32),
            shape_of(8, width),
            shape_of(2, rows, width),
            shape_of(rows, width),
            shape_of(2, 8, 128, dtype=f32),
            shape_of(8, 128, dtype=f32),
            shape_of(8, 128, dtype=f32),
        ]
        + states
        + [partner_hidden]
        + [
            shape_of(2, rows, width),
            shape_of(2, rows, width, dtype=f32),
            shape_of(2, 24, seq_len, dtype=f32),
            shape_of(2, 24, seq_len, dtype=f32),
        ],
        in_specs=[SMEM] + [VMEM] * 6 + [ANY] * 10,
        out_specs=[ANY] * 10 + [VMEM] * 8 + [ANY] * 10 + [VMEM] * 4,
        scratch_shapes=[pltpu.VMEM(st.shape, st.dtype) for st in states]
        + attn_scratch
        + ffn_scratch
        + [
            pltpu.VMEM((blocks, seq_len, inner), bf16),
            pltpu.VMEM((seq_len, width), bf16),
            pltpu.VMEM((2, peers, rows, width), bf16),
            pltpu.VMEM((2, peers, rows, width), bf16),
            pltpu.VMEM((seq_len, LANES), f32),
            pltpu.VMEM((rows, width), f32),
            pltpu.VMEM((rows, width), bf16),
            pltpu.VMEM((top, seq_len), jnp.int32),
            pltpu.VMEM((2, rows, width), bf16),
            pltpu.VMEM((seq_len, 8), f32),
            pltpu.VMEM((planes - 1, 8, 128), f32),
            dma((2, 2, peers)),
            dma((2, 2, peers)),
            dma((2, peers)),
            dma((2, peers)),
            dma((2, chunks, peers)),
            dma((2, chunks, peers)),
            dma((15,)),
            dma((15,)),
            dma((10,)),
            dma((2, 9)),
            dma,
            dma,
            dma((2, 2)),
            dma((2, 2)),
            dma((planes - 1,)),
            dma((planes - 1,)),
            dma,
            dma,
        ],
        compiler_params=params(0),
        name="forward",
    )(lengths, boundary[0], routes_t, attn_gain, ffn_gain, router_t, tables, *weights)
    other, result = result[:10], result[10:]
    (o_gain_a, o_gain_f, o_router, out_rows, cot, probs_sum, cnt, o_cnt), result = result[:8], result[8:]
    saved, result = result[:10], result[10:]
    (xs, mid, small, o_small) = result

    (in_grads, g_q, g_k, g_v, g_o, g_gain_a, g_gain_f, g_router, balance, *g_ffn) = pl.pallas_call(
        functools.partial(back_kernel, ranks, planes, top),
        out_shape=[shape_of(seqs, rows, width, dtype=f32)]
        + [shape_of(chunk, heads_width, dtype=f32)] * 3
        + [
            shape_of(heads_width, chunk, dtype=f32),
            shape_of(1, width, dtype=f32),
            shape_of(1, width, dtype=f32),
            shape_of(experts, width, dtype=f32),
            shape_of(1, 1, dtype=f32),
        ]
        + [shape_of(experts, chunk, inner, dtype=f32)] * 3
        + [shape_of(chunk, inner, dtype=f32)] * 3,
        in_specs=[SMEM] + [VMEM] * 15 + [ANY] * 30,
        out_specs=[VMEM] * 9 + [ANY] * 6,
        scratch_shapes=[
            pltpu.VMEM((seq_len, width), bf16),
            pltpu.VMEM((blocks, seq_len, inner), bf16),
            pltpu.VMEM((blocks, seq_len, inner), bf16),
            pltpu.VMEM((seq_len, width), bf16),
        ]
        + ffn_scratch
        + [pltpu.VMEM(st.shape[1:], st.dtype) for st in states[:6]]
        + attn_scratch
        + [
            pltpu.VMEM((seq_len, width), bf16),
            pltpu.VMEM((2, seq_len, width), bf16),
            pltpu.VMEM((blocks, seq_len, half), bf16),
            pltpu.VMEM((blocks, seq_len, half), bf16),
            pltpu.VMEM((blocks, seq_len, half), bf16),
            pltpu.VMEM((blocks, seq_len, half), bf16),
            pltpu.VMEM((seq_len, 8), f32),
            pltpu.VMEM((seq_len, 8), f32),
            pltpu.VMEM((seq_len, 8), f32),
            pltpu.VMEM((seq_len, width), bf16),
            pltpu.VMEM((peers, rows, width), bf16),
            pltpu.VMEM((peers, rows, width), bf16),
            pltpu.VMEM((seq_len, LANES), f32),
            pltpu.VMEM((rows, width), f32),
            pltpu.VMEM((rows, width), f32),
            pltpu.VMEM((2, 3, planes, chunk, part), bf16),
            pltpu.VMEM((blocks, 3, planes, chunk, part), bf16),
            pltpu.VMEM((2, planes, 3 * blocks, chunk, part), bf16),
            pltpu.VMEM((2 * planes, 3 * blocks, chunk, part), bf16),
            pltpu.VMEM((seq_len, width), bf16),
            pltpu.VMEM((seq_len, seq_len), bf16),
            pltpu.VMEM((seq_len, 3 * heads_width), bf16),
            pltpu.VMEM((width, 4 * heads_width), bf16),
            pltpu.VMEM((width, 2 * heads_width), bf16),
            pltpu.VMEM((planes, chunk, 2 * heads_width), bf16),
            pltpu.VMEM((2 * planes, chunk, 2 * heads_width), bf16),
            pltpu.VMEM((rows, width), f32),
            pltpu.VMEM((3, 16, width + 128), f32),
            pltpu.VMEM((peers, 16, width + 128), f32),
            pltpu.VMEM((planes - 1, 16, width + 128), f32),
            pltpu.VMEM((2, chunk, inner), f32),
            dma((2, peers)),
            dma((2, peers)),
            dma((2, chunks, peers)),
            dma((2, chunks, peers)),
            dma((2, peers)),
            dma((2, peers)),
            dma((2, chunks, peers)),
            dma((2, chunks, peers)),
            dma((2,)),
            dma((2,)),
            dma((blocks,)),
            dma((blocks,)),
            dma((2, planes)),
            dma((2 * planes,)),
            dma((2,)),
            dma((2,)),
            dma((2,)),
            dma((2, planes)),
            dma((2 * planes,)),
            dma((2,)),
            dma,
            dma,
            dma,
            dma,
            dma((peers,)),
            dma((peers,)),
            dma((planes - 1,)),
            dma((planes - 1,)),
            dma((10,)),
            dma((10,)),
            dma((2,)),
        ],
        compiler_params=params(1),
        name="backward",
    )(
        lengths,
        cot,
        attn_gain,
        o_gain_a,
        ffn_gain,
        o_gain_f,
        router_t,
        o_router,
        tables,
        xs,
        mid,
        small,
        o_small,
        probs_sum,
        cnt,
        o_cnt,
        *saved,
        *weights,
        *other,
    )
    g_eg, g_eu, g_ed, g_sg, g_su, g_sd = g_ffn
    return (
        out_rows[None],
        in_grads[None],
        g_gain_a,
        g_q[None],
        g_k[None],
        g_v[None],
        g_o[None],
        g_gain_f,
        g_router.T[None],
        g_eg[None],
        g_eu[None],
        jnp.swapaxes(g_ed, 1, 2)[None],
        g_sg[None],
        g_su[None],
        g_sd.T[None],
        balance.reshape(1),
    )


def solution(mesh):
    placed = (
        P("section", "dp", "tensor", None),
        P("dp"),
        P("section", "dp", None, None),
        P("section", None),
        P("section", None, "tensor"),
        P("section", None, "tensor"),
        P("section", None, "tensor"),
        P("section", "tensor", None),
        P("section", None),
        P("section", None, None),
        P("section", None, None, "tensor"),
        P("section", None, None, "tensor"),
        P("section", None, "tensor", None),
        P("section", None, "tensor"),
        P("section", None, "tensor"),
        P("section", "tensor", None),
    )
    return jax.shard_map(
        functools.partial(on_device, mesh.shape["tensor"], mesh.shape["dp"]),
        mesh=mesh,
        in_specs=placed,
        out_specs=(
            P("section", "dp", "tensor", None),
            P("section", "dp", "tensor", None),
            P("section", None),
            P("section", "dp", "tensor"),
            P("section", "dp", "tensor"),
            P("section", "dp", "tensor"),
            P("section", "tensor", "dp"),
            P("section", None),
            P("section", None, None),
            P("section", None, "dp", "tensor"),
            P("section", None, "dp", "tensor"),
            P("section", None, "tensor", "dp"),
            P("section", "dp", "tensor"),
            P("section", "dp", "tensor"),
            P("section", "tensor", "dp"),
            P("section"),
        ),
        check_vma=False,
    )
```

```python
import functools

import jax
import jax.numpy as jnp
import numpy as np
from jax import lax
from jax.experimental import pallas as pl
from jax.experimental.pallas import tpu as pltpu
from jax.sharding import PartitionSpec as P

HEAD_DIM = 64
HALF_DIM = HEAD_DIM // 2
EPSILON = 1e-06
ALPHA = 0.01
THETA = 10000.0
MASKED = -1e30
LANES = 256
VMEM_LIMIT = 63 * 2**20

f32 = jnp.float32
bf16 = jnp.bfloat16
MESH = pl.DeviceIdType.MESH
ANY = pl.BlockSpec(memory_space=pl.ANY)
VMEM = pl.BlockSpec(memory_space=pltpu.VMEM)
SMEM = pl.BlockSpec(memory_space=pltpu.SMEM)


def dot(left, right, left_dim, right_dim):
    return lax.dot_general(
        left, right, (((left_dim,), (right_dim,)), ((), ())), preferred_element_type=f32
    )


def rope_tables(seq_len):
    frequency = (THETA ** (-np.arange(HALF_DIM, dtype=np.float32) / HALF_DIM)).astype(np.float32)
    angles = np.arange(seq_len, dtype=np.float32)[:, None] * frequency[None, :]
    cosine, sine = np.cos(angles), np.sin(angles)
    return np.concatenate([cosine, cosine, -sine, sine], axis=-1).astype(np.float32)


def turn_halves(values):
    return jnp.concatenate([values[:, HALF_DIM:], values[:, :HALF_DIM]], axis=1)


class Place:
    def __init__(self, ranks, planes):
        self.s = lax.axis_index("section")
        self.t = lax.axis_index("tensor")
        self.z = lax.axis_index("dp")
        self.ranks, self.planes = ranks, planes
        self.odd = lax.rem(self.z, 2)
        self.sibling = (1 - self.s, self.t, self.z)
        self.partner = (self.s, self.t, self.z + 1 - 2 * self.odd)

    def peer(self, k):
        return lax.rem(self.t + k, self.ranks)

    def peer_id(self, k):
        return (self.s, self.peer(k), self.z)

    def plane_id(self, k):
        return (self.s, self.t, lax.rem(self.z + k, self.planes))

    def greet(self):
        barrier = pltpu.get_barrier_semaphore()
        others = [self.sibling] + [self.peer_id(k) for k in range(1, self.ranks)]
        for k in range(1, self.planes):
            _, t, z = self.plane_id(k)
            others += [(self.s, t, z), (1 - self.s, t, z)]
        for other in others:
            pl.semaphore_signal(barrier, inc=1, device_id=other, device_id_type=MESH)
        pl.semaphore_wait(barrier, len(others))


def remote(src, dst, send, recv, device):
    return pltpu.make_async_remote_copy(
        src_ref=src, dst_ref=dst, send_sem=send, recv_sem=recv, device_id=device, device_id_type=MESH
    )


def gather_rows(place, full, rows, send, recv):
    mine = full.at[pl.ds(place.t * rows, rows)]
    copies = []
    for k in range(1, place.ranks):
        copy = remote(mine, mine, send.at[k - 1], recv.at[k - 1], place.peer_id(k))
        copy.start()
        copies.append(copy)
    return copies


def scatter_block(place, stage, landing, rows, lo, width, send, recv):
    copies = []
    for k in range(1, place.ranks):
        src = stage.at[pl.ds(place.peer(k) * rows, rows), pl.ds(lo, width)]
        dst = landing.at[k - 1, :, pl.ds(lo, width)]
        copy = remote(src, dst, send.at[k - 1], recv.at[k - 1], place.peer_id(k))
        copy.start()
        copies.append(copy)
    return copies


def landed_sum(own, landing, ranks):
    total = own
    for k in range(ranks - 1):
        total = total + landing[k].astype(f32)
    return total


def rms_rows(values, gain):
    return values * lax.rsqrt(jnp.mean(values * values, axis=-1, keepdims=True) + EPSILON) * gain


def rms_back(values, gain, grad):
    r = lax.rsqrt(jnp.mean(values * values, axis=-1, keepdims=True) + EPSILON)
    normed = values * r
    scaled = grad * gain
    inner = jnp.mean(scaled * normed, axis=-1, keepdims=True)
    return r * (scaled - normed * inner), jnp.sum(grad * normed, axis=0, keepdims=True)


def name_rows(routes):
    expert = lax.broadcasted_iota(jnp.int32, (8, routes.shape[1]), 0)
    named = routes[0:1] == expert
    for j in range(1, routes.shape[0]):
        named = named | (routes[j : j + 1] == expert)
    return named.astype(f32)


def column(matrix, index):
    lane = lax.broadcasted_iota(jnp.int32, matrix.shape, 1)
    return jnp.sum(jnp.where(lane == index, matrix, 0.0), axis=1, keepdims=True)


def load_choice(first, pairs, sems):
    for i, (own, other, dst) in enumerate(pairs):

        @pl.when(first)
        def _(own=own, dst=dst, i=i):
            pltpu.make_async_copy(own, dst, sems.at[i]).start()

        @pl.when(jnp.logical_not(first))
        def _(other=other, dst=dst, i=i):
            pltpu.make_async_copy(other, dst, sems.at[i]).start()

    return [pltpu.make_async_copy(own, dst, sems.at[i]) for i, (own, other, dst) in enumerate(pairs)]


N_ATTN = 4
N_FFN = 6


def attn_targets(w_in, w_out, heads_width):
    return [w_in.at[pl.ds(i * heads_width, heads_width)] for i in range(3)] + [w_out]


def ffn_targets(wg, wu, wd):
    experts = wg.shape[0] - 1
    first = pl.ds(0, experts)
    return [wg.at[first], wu.at[first], wd.at[first], wg.at[experts], wu.at[experts], wd.at[experts]]


def both_kernel(ranks, planes, top, *refs):
    (lens, bnd, routes, gain_a_own, gain_f_own, router, tables), refs = refs[:7], refs[7:]
    own, refs = refs[:10], refs[10:]
    other, refs = refs[:10], refs[10:]
    (nf_o, q_o, k_o, v_o, p_o, mx_o, hf_o, g_o, u_o, hp_o, land, land_z), refs = refs[:12], refs[12:]
    (out_rows, in_grads, gain_a_out, gain_f_out, router_out, balance), refs = refs[:6], refs[6:]
    (nf, qs, ks, vs, ps, mx, hf, gs, us, hp), refs = refs[:10], refs[10:]
    (w_in, wo, wg, wu, wd), refs = refs[:5], refs[5:]
    (dyf, dyp, acts, gp, up, ap, coef, coef_p, gate_sum), refs = refs[:9], refs[9:]
    (stage, stage_y, land_a, land_f, land_y, tmp, own_part, own_y, d_mid), refs = refs[:9], refs[9:]
    (sent, got, quarter, df, ds, dqkv, gw, got_a, half_a), refs = refs[:9], refs[9:]
    (xs, mid, small, o_small, probs_sum, cnt, o_cnt, cnt_in), refs = refs[:8], refs[8:]
    (o_bnd, o_routes, o_gain_a, o_gain_f, o_router, y_low), refs = refs[:6], refs[6:]
    (row_buf, packs, pack_t, pack_z), refs = refs[:4], refs[4:]
    (ag_s, ag_r, rsa_s, rsa_r, rsf_s, rsf_r, rsy_s, rsy_r, ex_s, ex_r), refs = refs[:10], refs[10:]
    (hp_s, hp_r, dp_s, dp_r, cz_s, cz_r, cs_s, cs_r, row_s, row_r), refs = refs[:10], refs[10:]
    (sw_s, sw_r, zs, zr, zl, as_s, as_r, az_s, az_r, az_l), refs = refs[:10], refs[10:]
    (gr_s, gr_r, pk_s, pk_r, pt_s, pt_r, pz_s, pz_r, ffn_sem, attn_sem, save_sem) = refs

    place = Place(ranks, planes)
    s, t, z, odd = place.s, place.t, place.z, place.odd
    rows, width = bnd.shape[1], bnd.shape[2]
    seq_len = hf.shape[0]
    experts = wg.shape[0] - 1
    blocks = experts + 1
    inner = wg.shape[2]
    half = inner // 2
    part = half // 2
    heads = qs.shape[0]
    heads_width = heads * HEAD_DIM
    chunk = width // planes
    chunks = width // LANES
    mine = pl.ds(t * rows, rows)
    my_lanes = pl.ds(pl.multiple_of(odd * half, half), half)
    far_lanes = pl.ds(pl.multiple_of((1 - odd) * half, half), half)
    slot = s * planes + z
    scale = HEAD_DIM ** (-0.5)

    def ffn_weights(l):
        targets = ffn_targets(wg, wu, wd)
        return load_choice(s == l, [(own[4 + i], other[4 + i], targets[i]) for i in range(N_FFN)], ffn_sem)

    def attn_weights(l):
        targets = attn_targets(w_in, wo, heads_width)
        return load_choice(s == l, [(own[i], other[i], targets[i]) for i in range(N_ATTN)], attn_sem)

    ffn_state = [(gs, g_o), (us, u_o), (hf, hf_o), (hp, hp_o)]
    attn_state = [(nf, nf_o), (qs, q_o), (ks, k_o), (vs, v_o), (ps, p_o), (mx, mx_o)]

    def moves(pairs, first, back):
        copies = []
        for i, (inside, outside) in enumerate(pairs):
            src, dst = (outside, inside) if back else (inside, outside)
            copies.append(pltpu.make_async_copy(src, dst, save_sem.at[first + i]))
        return copies

    def begin(copies):
        for copy in copies:
            copy.start()
        return copies

    def finish_all(copies):
        for copy in copies:
            copy.wait()

    def gain_of(l, mine_ref, other_ref):
        return jnp.where(s == l, mine_ref[...], other_ref[...])

    def route_weights(l):
        value = jnp.where(s == l, router[...], o_router[...]).astype(f32)
        if experts < 8:
            value = jnp.concatenate([value, jnp.zeros((8 - experts, width), f32)], axis=0)
        return value.astype(bf16)

    def to_owner(l, src, dst, send, recv, local):
        for c in range(planes):
            own_copy = (z == c) & (s == l)

            @pl.when(own_copy)
            def _(c=c):
                pltpu.make_async_copy(src(c), dst, local).start()

            @pl.when(jnp.logical_not(own_copy))
            def _(c=c):
                remote(src(c), dst, send.at[c], recv.at[slot], (l, t, c)).start()

    def sent_to_owner(l, whole, dst, send, recv, local):
        for c in range(planes):
            own_copy = (z == c) & (s == l)

            @pl.when(own_copy)
            def _(c=c):
                pltpu.make_async_copy(whole.at[c], dst.at[slot], local).wait()

            @pl.when(jnp.logical_not(own_copy))
            def _(c=c):
                remote(whole.at[c], dst.at[slot], send.at[c], recv.at[slot], (l, t, c)).wait_send()

    def arrived(dst, send, recv):
        for source in range(2 * planes):

            @pl.when(source != slot)
            def _(source=source):
                remote(
                    dst.at[source], dst.at[source], send.at[0], recv.at[source], place.sibling
                ).wait_recv()

    def scatter_product(product, staged, landing, own_rows, send, recv):
        copies = []
        for n in range(chunks):
            lanes = slice(n * LANES, (n + 1) * LANES)
            total = product(lanes)
            tmp[...] = total
            staged[:, lanes] = total.astype(bf16)
            own_rows[:, lanes] = tmp[mine]
            copies += scatter_block(
                place, staged, landing, rows, n * LANES, LANES, send.at[n], recv.at[n]
            )
        return copies

    place.greet()
    first_w = 5
    ex_pairs = [
        (bnd.at[1 - s], o_bnd),
        (gain_a_own, o_gain_a),
        (gain_f_own, o_gain_f),
        (router, o_router),
        (routes.at[1 - s], o_routes),
    ] + [(own[i], other[i]) for i in range(10)]
    exchange = [
        remote(src, dst, ex_s.at[i], ex_r.at[i], place.sibling) for i, (src, dst) in enumerate(ex_pairs)
    ]
    begin(exchange)
    row8 = lax.broadcasted_iota(jnp.int32, (8, seq_len), 0)
    token8 = lax.broadcasted_iota(jnp.int32, (8, seq_len), 1)
    counted = jnp.zeros((8, 1), f32)
    for q in range(2):
        live = jnp.where(token8 < lens[q], 1.0, 0.0)
        counts = jnp.where(row8 == 7, live, name_rows(routes[q]) * live)
        counted = counted + jnp.sum(counts, axis=1, keepdims=True)
    cnt[...] = jnp.broadcast_to(counted, cnt.shape)
    count_copies = begin(
        [
            remote(cnt, cnt_in.at[k - 1], cz_s.at[k - 1], cz_r.at[k - 1], place.plane_id(k))
            for k in range(1, planes)
        ]
    )
    finish_all(exchange[:first_w])
    is_first = s == 0
    length = lens[s]
    xs[0] = jnp.where(is_first, bnd[0], o_bnd[...])
    cotangent = jnp.where(is_first, o_bnd[...], bnd[1]).astype(f32)
    position = lax.broadcasted_iota(jnp.int32, (rows, width), 0) + t * rows
    dyf[mine] = jnp.where(position < length, cotangent, 0.0).astype(bf16)
    cosine, signed = tables[:, :HEAD_DIM], tables[:, HEAD_DIM:]

    def attn_begin(l):
        nf[mine] = rms_rows(xs[l].astype(f32), gain_of(l, gain_a_own, o_gain_a)).astype(bf16)
        return gather_rows(place, nf, rows, ag_s.at[l, 0], ag_r.at[l, 0])

    def attn_forward(l, gathering, loads, between):
        finish_all(loads)
        finish_all(gathering)
        between()
        projected = dot(nf[...], w_in[...], 1, 1)
        for j, dst in enumerate((qs, ks, vs)):
            for h in range(heads):
                at = j * heads_width + h * HEAD_DIM
                piece = projected[:, at : at + HEAD_DIM]
                if j < 2:
                    piece = piece * cosine + turn_halves(piece) * signed
                dst[h] = piece.astype(bf16)
        for i in range(ranks):
            lo, reach = i * rows, (i + 1) * rows
            place_q = lax.broadcasted_iota(jnp.int32, (rows, reach), 0) + lo
            place_k = lax.broadcasted_iota(jnp.int32, (rows, reach), 1)
            allowed = (place_k <= place_q) & (place_k < length)
            for h in range(heads):
                scores = dot(qs[h, lo:reach], ks[h, 0:reach], 1, 1) * scale
                scores = jnp.where(allowed, scores, MASKED)
                peak = jnp.max(scores, axis=-1, keepdims=True)
                raised = jnp.exp(scores - peak)
                total = jnp.sum(raised, axis=-1, keepdims=True)
                weights = (raised / total).astype(bf16)
                ps[h, lo:reach, 0:reach] = weights
                if reach < seq_len:
                    ps[h, lo:reach, reach:] = jnp.zeros((rows, seq_len - reach), bf16)
                mixed = dot(weights, vs[h, 0:reach], 1, 0)
                mx[lo:reach, h * HEAD_DIM : (h + 1) * HEAD_DIM] = mixed.astype(bf16)
            product = dot(mx[lo:reach], wo[...], 1, 0)
            stage[lo:reach] = product.astype(bf16)

            @pl.when(t == i)
            def _(product=product):
                own_part[...] = product

            @pl.when(t != i)
            def _(i=i, lo=lo):
                k = lax.rem(i - t + ranks, ranks)
                remote(
                    stage.at[pl.ds(lo, rows)],
                    land_a.at[k - 1],
                    rsa_s.at[l, 0, k - 1],
                    rsa_r.at[l, 0, k - 1],
                    (s, i, z),
                ).start()

    def attn_finish(l):
        for k in range(1, ranks):
            remote(
                stage.at[pl.ds(place.peer(k) * rows, rows)],
                land_a.at[k - 1],
                rsa_s.at[l, 0, k - 1],
                rsa_r.at[l, 0, k - 1],
                place.peer_id(k),
            ).wait()
        middle = xs[l].astype(f32) + landed_sum(own_part[...], land_a, ranks)
        mid[l] = middle
        hf[mine] = rms_rows(middle, gain_of(l, gain_f_own, o_gain_f)).astype(bf16)
        return gather_rows(place, hf, rows, ag_s.at[l, 1], ag_r.at[l, 1])

    def route(l):
        names = name_rows(jnp.where(s == l, routes[s], o_routes[...]))
        logits = dot(route_weights(l), hf[...], 1, 1)
        logits = jnp.where(row8 < experts, logits, MASKED)
        raised = jnp.exp(logits - jnp.max(logits, axis=0, keepdims=True))
        raised = jnp.where(row8 < experts, raised, 0.0)
        chances = raised / jnp.sum(raised, axis=0, keepdims=True)
        per_chosen = names / jnp.sum(chances * names, axis=0, keepdims=True)
        gates = chances * per_chosen
        small[l, 0:8] = chances
        small[l, 8:16] = gates
        small[l, 16:24] = per_chosen
        remote(small.at[l], o_small.at[l], hp_s.at[l, 1], hp_r.at[l, 1], place.partner).start()
        summed = jnp.sum(jnp.where(token8 < length, chances, 0.0), axis=1, keepdims=True)
        probs_sum[l] = jnp.broadcast_to(summed, (8, 128))
        coef[...] = jnp.where(row8 == experts, 1.0, gates).T

    def split_acts(e, value):
        low, high = value[:, :half], value[:, half:]
        acts[e] = jnp.where(odd == 0, low, high).astype(bf16)
        gp[e] = jnp.where(odd == 0, high, low).astype(bf16)

    def branch_product(lanes):
        total = dot(acts[0], wd[0, my_lanes, lanes], 1, 0) + dot(gp[0], wd[0, far_lanes, lanes], 1, 0)
        for e in range(1, blocks):
            total = total + dot(acts[e], wd[e, my_lanes, lanes], 1, 0)
            total = total + dot(gp[e], wd[e, far_lanes, lanes], 1, 0)
        return total

    def output_rows(l, landing, own_rows):
        output = mid[l] + landed_sum(own_rows[...], landing, ranks)
        y_low[l] = output.astype(bf16)

        @pl.when(s == l)
        def _():
            out_rows[s] = y_low[l]

        @pl.when(s != l)
        def _():
            remote(y_low.at[l], out_rows.at[s], row_s, row_r, place.sibling).start()

    gathering = attn_begin(0)

    @pl.when(s != 0)
    def _():
        for copy in exchange[first_w : first_w + N_ATTN]:
            copy.wait_recv()

    loads = attn_weights(0)
    cot_gather = []

    def gather_cotangent():
        cot_gather.extend(gather_rows(place, dyf, rows, ag_s.at[1, 2], ag_r.at[1, 2]))

    attn_forward(0, gathering, loads, gather_cotangent)

    @pl.when(s != 0)
    def _():
        for copy in exchange[first_w + N_ATTN :]:
            copy.wait_recv()

    ffn_loads = ffn_weights(0)
    attn_saves = begin(moves(attn_state, 4, False))
    gathering = attn_finish(0)

    @pl.when(s == 0)
    def _():
        for copy in exchange[first_w : first_w + N_ATTN]:
            copy.wait_recv()

    attn_w = attn_weights(1)
    finish_all(count_copies)
    total = cnt[...]
    for k in range(planes - 1):
        total = total + cnt_in[k]
    cnt[...] = total
    share_counts = remote(cnt, o_cnt, cs_s, cs_r, place.sibling)
    share_counts.start()
    finish_all(ffn_loads)
    finish_all(gathering)
    ffn_saves = begin(moves(ffn_state[2:3], 2, False))
    hidden_sent = [remote(hf, hp_o, hp_s.at[0, 0], hp_r.at[0, 0], place.partner)]
    begin(hidden_sent)
    route(0)

    def forward_expert(e, carry):
        gate_h = dot(hf[...], wg[e], 1, 0)
        up_h = dot(hf[...], wu[e], 1, 0)
        gs[e] = gate_h.astype(bf16)
        us[e] = up_h.astype(bf16)
        split_acts(e, gate_h * jax.nn.sigmoid(gate_h) * up_h * column(coef[...], e))
        return carry

    lax.fori_loop(0, blocks, forward_expert, 0)
    ffn_saves += begin(moves(ffn_state[:2], 0, False))
    finish_all(attn_saves)
    scat = scatter_product(branch_product, stage, land_f, own_part, rsf_s.at[0, 0], rsf_r.at[0, 0])

    @pl.when(s == 0)
    def _():
        for copy in exchange[first_w + N_ATTN :]:
            copy.wait_recv()

    ffn_loads = ffn_weights(1)
    finish_all(cot_gather)
    cot_sent = remote(dyf, dyp.at[1], dp_s.at[1, 0], dp_r.at[1, 0], place.partner)
    cot_sent.start()
    finish_all(scat)
    output_rows(0, land_f, own_part)
    xs[1] = y_low[0]

    gathering = attn_begin(1)
    finish_all(hidden_sent)
    finish_all(ffn_saves)
    attn_forward(1, gathering, attn_w, lambda: None)
    gathering = attn_finish(1)
    finish_all(ffn_loads)
    finish_all(gathering)
    hidden_sent = [remote(hf, hp, hp_s.at[1, 0], hp_r.at[1, 0], place.partner)]
    begin(hidden_sent)
    route(1)
    gate_sum[...] = jnp.zeros_like(gate_sum)
    lane8 = lax.broadcasted_iota(jnp.int32, gate_sum.shape, 1)

    def expert_grads(e, gate_h, up_h, raw):
        sig = jax.nn.sigmoid(gate_h)
        silu = gate_h * sig
        acted = silu * up_h
        inner_sum = jnp.sum(acted * raw, axis=1, keepdims=True)
        gate_sum[...] = jnp.where(lane8 == e, inner_sum, gate_sum[...])
        weight = column(coef[...], e)
        d_acted = raw * weight
        gs[e] = (d_acted * up_h * (sig + silu * (1.0 - sig))).astype(bf16)
        us[e] = (d_acted * silu).astype(bf16)
        return acted * weight

    def both_expert(e, carry):
        gate_h = dot(hf[...], wg[e], 1, 0)
        up_h = dot(hf[...], wu[e], 1, 0)
        raw = dot(dyf[...], wd[e], 1, 1)
        split_acts(e, expert_grads(e, gate_h, up_h, raw))
        return carry

    def back_expert(e, carry):
        raw = dot(dyf[...], wd[e], 1, 1)
        value = expert_grads(e, gs[e].astype(f32), us[e].astype(f32), raw)
        acts[e] = jnp.where(odd == 0, value[:, :half], value[:, half:]).astype(bf16)
        return carry

    lax.fori_loop(0, blocks, both_expert, 0)
    share_counts.wait()
    y_scat = []

    for l in (1, 0):
        here = s == l
        if l == 0:
            finish_all(ffn_loads)
            finish_all(ffn_back)
            coef[...] = jnp.where(row8 == experts, 1.0, small[l, 8:16]).T
            gate_sum[...] = jnp.zeros_like(gate_sum)
            to_partner = [remote(dyf.at[mine], dyp.at[l, mine], dp_s.at[l, 0], dp_r.at[l, 0], place.partner)]
            begin(to_partner)
            for k, copy in enumerate(gathering, 1):
                copy.wait()
                they = pl.ds(place.peer(ranks - k) * rows, rows)
                to_partner += begin(
                    [remote(dyf.at[they], dyp.at[l, they], dp_s.at[l, k], dp_r.at[l, k], place.partner)]
                )
            lax.fori_loop(0, blocks, back_expert, 0)
        else:
            to_partner = [cot_sent]
        chances, gates, per_chosen = small[l, 0:8], small[l, 8:16], small[l, 16:24]
        totals = jnp.where(here, cnt[...], o_cnt[...])
        tokens_all = totals[7:8, 0:1]
        share = totals[:, 0:1] / (top * tokens_all)
        aux = jnp.where((token8 < length) & (t == 0), ALPHA * experts * share / tokens_all, 0.0)
        d_gates = gate_sum[...].T
        common = jnp.sum(d_gates * gates, axis=0, keepdims=True)
        d_chances = per_chosen * (d_gates - common) + aux
        d_logits = chances * (d_chances - jnp.sum(chances * d_chances, axis=0, keepdims=True))
        d_logits = d_logits.astype(bf16)
        router_grad = dot(d_logits, hf[...], 1, 0)
        route_w = route_weights(l)

        def hidden_product(lanes, d_logits=d_logits, route_w=route_w):
            total = dot(d_logits, route_w[:, lanes], 0, 0)
            for e in range(blocks):
                total = total + dot(gs[e], wg[e, lanes], 1, 1)
                total = total + dot(us[e], wu[e, lanes], 1, 1)
            return total

        scat = scatter_product(hidden_product, stage, land_f, own_part, rsf_s.at[l, 1], rsf_r.at[l, 1])
        if l == 1:
            y_scat = scatter_product(branch_product, stage_y, land_y, own_y, rsy_s, rsy_r)
        finish_all(to_partner)
        if l == 1:
            finish_all(hidden_sent)
        remote(small.at[l], o_small.at[l], hp_s.at[l, 1], hp_r.at[l, 1], place.partner).wait()
        coef_p[...] = jnp.where(row8 == experts, 1.0, o_small[l, 8:16]).T

        def partner_expert(e, carry, l=l):
            gate_h = dot(hp[...], wg[e, :, my_lanes], 1, 0)
            up_h = dot(hp[...], wu[e, :, my_lanes], 1, 0)
            raw = dot(dyp[l], wd[e, my_lanes], 1, 1)
            sig = jax.nn.sigmoid(gate_h)
            silu = gate_h * sig
            weight = column(coef_p[...], e)
            ap[e] = (silu * up_h * weight).astype(bf16)
            d_acted = raw * weight
            gp[e] = (d_acted * up_h * (sig + silu * (1.0 - sig))).astype(bf16)
            up[e] = (d_acted * silu).astype(bf16)
            return carry

        lax.fori_loop(0, blocks, partner_expert, 0)
        finish_all(scat)
        d_hidden = landed_sum(own_part[...], land_f, ranks)
        d_norm, gain_f_grad = rms_back(mid[l], gain_of(l, gain_f_own, o_gain_f), d_hidden)
        d_mid[...] = dyf[mine].astype(f32) + d_norm
        df[mine] = d_mid[...].astype(bf16)
        gathering = gather_rows(place, df, rows, ag_s.at[l, 3], ag_r.at[l, 3])

        def swap_of(e, l=l):
            return remote(sent.at[lax.rem(e, 2)], got.at[e], sw_s.at[e], sw_r.at[e], place.sibling)

        def finish(e, l=l):
            swap_of(e).wait()
            for j in range(3):
                at = e * 3 + j
                for c in range(planes):
                    quarter[l, c, at] = (
                        quarter[l, c, at].astype(f32) + got[e, j, c].astype(f32)
                    ).astype(bf16)
            three = pl.ds(e * 3, 3)
            to_owner(l, lambda c: quarter.at[l, c, three], land.at[slot, three], zs.at[l], zr, zl.at[l])

        def weight_grads(e, carry, l=l):
            sources = ((hf, gs, hp, gp), (hf, us, hp, up))
            for j in range(3):
                if j < 2:
                    left, right, left_p, right_p = sources[j]
                    value = dot(left[...], right[e, :, my_lanes], 0, 0) + dot(left_p[...], right_p[e], 0, 0)
                else:
                    value = dot(dyf[...], acts[e], 0, 0) + dot(dyp[l], ap[e], 0, 0)
                low, high = value[:, :part], value[:, part:]
                kept = jnp.where(s == 0, low, high).astype(bf16)
                given = jnp.where(s == 0, high, low).astype(bf16)
                for c in range(planes):
                    quarter[l, c, e * 3 + j] = kept[c * chunk : (c + 1) * chunk]
                    sent[lax.rem(e, 2), j, c] = given[c * chunk : (c + 1) * chunk]
            swap_of(e).start()

            @pl.when(e > 0)
            def _():
                finish(e - 1)

            return carry

        lax.fori_loop(0, blocks, weight_grads, 0)
        finish(blocks - 1)
        if l == 1:
            ffn_loads = ffn_weights(0)
            ffn_back = begin(moves(ffn_state, 0, True))
        else:
            finish_all(attn_w)
            finish_all(attn_back)
        finish_all(gathering)
        for h in range(heads):
            span = slice(h * HEAD_DIM, (h + 1) * HEAD_DIM)
            d_mixed = dot(df[...], wo[span], 1, 1).astype(bf16)
            for i in range(ranks):
                lo, reach = i * rows, (i + 1) * rows
                weights = ps[h, lo:reach, 0:reach].astype(f32)
                d_probs = dot(d_mixed[lo:reach], vs[h, 0:reach], 1, 1)
                total = jnp.sum(weights * d_probs, axis=-1, keepdims=True)
                ds[lo:reach, 0:reach] = (weights * (d_probs - total)).astype(bf16)
                if reach < seq_len:
                    ds[lo:reach, reach:] = jnp.zeros((rows, seq_len - reach), bf16)
            d_value = dot(ps[h], d_mixed, 0, 0)
            d_query = dot(ds[...], ks[h], 1, 0) * scale
            d_key = dot(ds[...], qs[h], 0, 0) * scale
            d_query = d_query * cosine - turn_halves(d_query) * signed
            d_key = d_key * cosine - turn_halves(d_key) * signed
            for j, value in enumerate((d_query, d_key, d_value)):
                at = j * heads_width + h * HEAD_DIM
                dqkv[:, at : at + HEAD_DIM] = value.astype(bf16)
        scat = scatter_product(
            lambda lanes: dot(dqkv[...], w_in[:, lanes], 1, 0), stage, land_a, own_part, rsa_s.at[l, pl.ds(1, chunks)], rsa_r.at[l, pl.ds(1, chunks)]
        )
        three_widths = 3 * heads_width
        gw[:, :three_widths] = dot(nf[...], dqkv[...], 0, 0).astype(bf16)
        gw[:, three_widths:] = dot(df[...], mx[...], 0, 0).astype(bf16)
        side = 2 * heads_width
        swap = remote(
            gw.at[:, pl.ds(pl.multiple_of((1 - s) * side, 128), side)],
            got_a,
            as_s.at[l],
            as_r.at[l],
            place.sibling,
        )
        swap.start()
        finish_all(scat)
        d_normed = landed_sum(own_part[...], land_a, ranks)
        d_norm, gain_a_grad = rms_back(xs[l].astype(f32), gain_of(l, gain_a_own, o_gain_a), d_normed)
        dx = d_mid[...] + d_norm
        if l == 1:
            low_dx = dx.astype(bf16)
            dyf[mine] = low_dx
            gathering = gather_rows(place, dyf, rows, ag_s.at[0, 2], ag_r.at[0, 2])
            dx = low_dx.astype(f32)
            attn_w = attn_weights(0)
            attn_back = begin(moves(attn_state, 4, True))
            finish_all(y_scat)
            output_rows(1, land_y, own_y)
        swap.wait()
        kept = gw[:, pl.ds(pl.multiple_of(s * side, 128), side)].astype(f32) + got_a[...].astype(f32)
        kept = kept.astype(bf16)
        if l == 0:
            sent_to_owner(1, half_a, land_z, az_s.at[1], az_r, az_l.at[1])
        for c in range(planes):
            half_a[c] = kept[c * chunk : (c + 1) * chunk]
        to_owner(l, lambda c: half_a.at[c], land_z.at[slot], az_s.at[l], az_r, az_l.at[l])
        pack = jnp.concatenate(
            [
                jnp.concatenate([gain_a_grad, gain_f_grad, jnp.zeros((6, width), f32), router_grad], axis=0),
                jnp.concatenate(
                    [jnp.zeros((8, 128), f32), jnp.where(t == 0, probs_sum[l], 0.0)], axis=0
                ),
            ],
            axis=1,
        )

        @pl.when(here)
        def _(dx=dx, pack=pack):
            in_grads[s] = dx
            packs[0] = pack

        @pl.when(jnp.logical_not(here))
        def _(dx=dx, pack=pack):
            row_buf[...] = dx
            packs[1] = pack
            remote(row_buf, in_grads.at[s], gr_s, gr_r, place.sibling).start()
            remote(packs.at[1], packs.at[2], pk_s, pk_r, place.sibling).start()

    remote(packs.at[1], packs.at[2], pk_s, pk_r, place.sibling).wait()
    packs[0] = packs[0] + packs[2]
    finish_all(
        begin(
            [
                remote(packs.at[0], pack_t.at[k - 1], pt_s.at[k - 1], pt_r.at[k - 1], place.peer_id(k))
                for k in range(1, ranks)
            ]
        )
    )
    total = packs[0]
    for k in range(ranks - 1):
        total = total + pack_t[k]
    packs[0] = total
    finish_all(
        begin(
            [
                remote(packs.at[0], pack_z.at[k - 1], pz_s.at[k - 1], pz_r.at[k - 1], place.plane_id(k))
                for k in range(1, planes)
            ]
        )
    )
    total = packs[0]
    for k in range(planes - 1):
        total = total + pack_z[k]
    gain_a_out[...] = total[0:1, :width]
    gain_f_out[...] = total[1:2, :width]
    router_out[...] = total[8 : 8 + experts, :width]
    tokens_all = cnt[7:8, 0:1]
    products = cnt[0:experts, 0:1] / (top * tokens_all) * total[8 : 8 + experts, width : width + 1]
    balance[...] = experts * jnp.sum(products, axis=0, keepdims=True) / tokens_all

    for copy in exchange[first_w:]:
        copy.wait_send()
    remote(y_low.at[1 - s], out_rows.at[s], row_s, row_r, place.sibling).wait_send()
    remote(y_low.at[1 - s], out_rows.at[1 - s], row_s, row_r, place.sibling).wait_recv()
    remote(row_buf, in_grads.at[s], gr_s, gr_r, place.sibling).wait_send()
    remote(row_buf, in_grads.at[1 - s], gr_s, gr_r, place.sibling).wait_recv()
    for l in (1, 0):
        sent_to_owner(l, quarter.at[l], land, zs.at[l], zr, zl.at[l])
    sent_to_owner(0, half_a, land_z, az_s.at[0], az_r, az_l.at[0])
    arrived(land, zs.at[0], zr)
    arrived(land_z, az_s.at[0], az_r)


def finish_kernel(planes, land, land_z, *refs):
    ins, outs = refs[:6], refs[6:12]
    g_gate, g_up, g_down, s_gate, s_up, s_down, wq_out, wk_out, wv_out, wo_out = refs[12:]
    e = pl.program_id(0)
    experts = pl.num_programs(0) - 1
    part = land.shape[3]
    heads_width = wq_out.shape[1]
    for j, (routed, common) in enumerate(((g_gate, s_gate), (g_up, s_up), (g_down, s_down))):
        for core in range(2):
            for parity in range(2):
                value = land[core * planes + parity, j].astype(f32)
                for pair in range(1, planes // 2):
                    value = value + land[core * planes + 2 * pair + parity, j].astype(f32)
                lo = (2 * parity + core) * part

                @pl.when(e < experts)
                def _(value=value, lo=lo, routed=routed):
                    routed[0, :, lo : lo + part] = value

                @pl.when(e == experts)
                def _(value=value, lo=lo, common=common):
                    common[:, lo : lo + part] = value

    @pl.when(e == 0)
    def _():
        for src, dst in zip(ins, outs):
            dst[...] = src[...]
        sides = []
        for core in range(2):
            value = land_z[core * planes].astype(f32)
            for plane in range(1, planes):
                value = value + land_z[core * planes + plane].astype(f32)
            sides.append(value)
        wq_out[...] = sides[0][:, :heads_width]
        wk_out[...] = sides[0][:, heads_width:]
        wv_out[...] = sides[1][:, :heads_width]
        wo_out[...] = sides[1][:, heads_width:].T


def params(collective_id):
    return pltpu.CompilerParams(
        collective_id=collective_id, has_side_effects=True, vmem_limit_bytes=VMEM_LIMIT
    )


def shape_of(*dims, dtype=bf16):
    return jax.ShapeDtypeStruct(dims, dtype)


def on_device(ranks, planes, *args):
    (boundary, lengths, routes, attn_gain, w_query, w_key, w_value, w_out, ffn_gain, router) = args[:10]
    ffn_own = tuple(a[0] for a in args[10:])
    attn_own = (w_query[0].T, w_key[0].T, w_value[0].T, w_out[0])
    rows, width = boundary.shape[2:]
    seqs, seq_len = routes.shape[1:3]
    top = routes.shape[3]
    experts, _, inner = ffn_own[0].shape
    blocks = experts + 1
    heads_width = w_query.shape[2]
    heads = heads_width // HEAD_DIM
    chunks = width // LANES
    half, part = inner // 2, inner // 4
    chunk = width // planes
    peers = ranks - 1
    dma = pltpu.SemaphoreType.DMA

    def vmem(*dims, dtype=bf16):
        return pltpu.VMEM(dims, dtype)

    routes_t = jnp.swapaxes(routes[0], 1, 2)
    router_t = router[0].T
    tables = jnp.asarray(rope_tables(seq_len))
    head_shape = (heads, seq_len, HEAD_DIM)
    states = [
        (seq_len, width),
        head_shape,
        head_shape,
        head_shape,
        (heads, seq_len, seq_len),
        (seq_len, heads_width),
        (seq_len, width),
        (blocks, seq_len, inner),
        (blocks, seq_len, inner),
        (seq_len, width),
    ]
    weights = attn_own + ffn_own
    small_outs = [
        shape_of(2, rows, width),
        shape_of(seqs, rows, width, dtype=f32),
        shape_of(1, width, dtype=f32),
        shape_of(1, width, dtype=f32),
        shape_of(experts, width, dtype=f32),
        shape_of(1, 1, dtype=f32),
    ]
    result = pl.pallas_call(
        functools.partial(both_kernel, ranks, planes, top),
        out_shape=[shape_of(*w.shape) for w in weights]
        + [shape_of(*dims) for dims in states]
        + [
            shape_of(2 * planes, 3 * blocks, chunk, part),
            shape_of(2 * planes, chunk, 2 * heads_width),
        ]
        + small_outs,
        in_specs=[SMEM] + [VMEM] * 6 + [ANY] * 10,
        out_specs=[ANY] * 22 + [VMEM] * 6,
        scratch_shapes=[vmem(*dims) for dims in states]
        + [
            vmem(3 * heads_width, width),
            vmem(heads_width, width),
            vmem(blocks, width, inner),
            vmem(blocks, width, inner),
            vmem(blocks, inner, width),
        ]
        + [vmem(seq_len, width), vmem(2, seq_len, width)]
        + [vmem(blocks, seq_len, half)] * 4
        + [vmem(seq_len, 8, dtype=f32)] * 3
        + [vmem(seq_len, width)] * 2
        + [vmem(peers, rows, width)] * 3
        + [vmem(seq_len, LANES, dtype=f32)]
        + [vmem(rows, width, dtype=f32)] * 3
        + [
            vmem(2, 3, planes, chunk, part),
            vmem(blocks, 3, planes, chunk, part),
            vmem(2, planes, 3 * blocks, chunk, part),
            vmem(seq_len, width),
            vmem(seq_len, seq_len),
            vmem(seq_len, 3 * heads_width),
            vmem(width, 4 * heads_width),
            vmem(width, 2 * heads_width),
            vmem(planes, chunk, 2 * heads_width),
        ]
        + [
            vmem(2, rows, width),
            vmem(2, rows, width, dtype=f32),
            vmem(2, 24, seq_len, dtype=f32),
            vmem(2, 24, seq_len, dtype=f32),
            vmem(2, 8, 128, dtype=f32),
            vmem(8, 128, dtype=f32),
            vmem(8, 128, dtype=f32),
            vmem(planes - 1, 8, 128, dtype=f32),
        ]
        + [
            vmem(rows, width),
            vmem(top, seq_len, dtype=jnp.int32),
            vmem(1, width, dtype=f32),
            vmem(1, width, dtype=f32),
            vmem(*router_t.shape),
            vmem(2, rows, width),
        ]
        + [
            vmem(rows, width, dtype=f32),
            vmem(3, 16, width + 128, dtype=f32),
            vmem(peers, 16, width + 128, dtype=f32),
            vmem(planes - 1, 16, width + 128, dtype=f32),
        ]
        + [dma((2, 4, peers))] * 2
        + [dma((2, 1 + chunks, peers))] * 2
        + [dma((2, 2, chunks, peers))] * 2
        + [dma((chunks, peers))] * 2
        + [dma((15,))] * 2
        + [dma((2, 2))] * 2
        + [dma((2, ranks))] * 2
        + [dma((planes - 1,))] * 2
        + [dma] * 4
        + [dma((blocks,))] * 2
        + [dma((2, planes)), dma((2 * planes,)), dma((2,))]
        + [dma((2,))] * 2
        + [dma((2, planes)), dma((2 * planes,)), dma((2,))]
        + [dma] * 4
        + [dma((peers,))] * 2
        + [dma((planes - 1,))] * 2
        + [dma((N_FFN,)), dma((N_ATTN,)), dma((10,))],
        compiler_params=params(0),
        name="forward_backward",
    )(lengths, boundary[0], routes_t, attn_gain, ffn_gain, router_t, tables, *weights)
    land, land_z, *small_results = result[20:]

    def whole(shape):
        return pl.BlockSpec(shape, lambda e: (0,) * len(shape))

    routed = shape_of(experts, chunk, inner, dtype=f32)
    common = shape_of(chunk, inner, dtype=f32)
    square = shape_of(chunk, heads_width, dtype=f32)
    turned = shape_of(heads_width, chunk, dtype=f32)
    last = experts - 1
    done = pl.pallas_call(
        functools.partial(finish_kernel, planes),
        grid=(blocks,),
        out_shape=small_outs + [routed] * 3 + [common] * 3 + [square] * 3 + [turned],
        in_specs=[
            pl.BlockSpec((2 * planes, 3, chunk, part), lambda e: (0, e, 0, 0)),
            whole(land_z.shape),
        ]
        + [whole(o.shape) for o in small_outs],
        out_specs=[whole(o.shape) for o in small_outs]
        + [pl.BlockSpec((1, chunk, inner), lambda e: (jnp.minimum(e, last), 0, 0))] * 3
        + [whole(common.shape)] * 3
        + [whole(square.shape)] * 3
        + [whole(turned.shape)],
        compiler_params=pltpu.CompilerParams(vmem_limit_bytes=VMEM_LIMIT),
        name="finish",
    )(land, land_z, *small_results)
    (out_rows, in_grads, g_gain_a, g_gain_f, g_router, balance), done = done[:6], done[6:]
    g_eg, g_eu, g_ed, g_sg, g_su, g_sd, g_q, g_k, g_v, g_o = done
    return (
        out_rows[None],
        in_grads[None],
        g_gain_a,
        g_q[None],
        g_k[None],
        g_v[None],
        g_o[None],
        g_gain_f,
        g_router.T[None],
        g_eg[None],
        g_eu[None],
        jnp.swapaxes(g_ed, 1, 2)[None],
        g_sg[None],
        g_su[None],
        g_sd.T[None],
        balance.reshape(1),
    )


def solution(mesh):
    placed = (
        P("section", "dp", "tensor", None),
        P("dp"),
        P("section", "dp", None, None),
        P("section", None),
        P("section", None, "tensor"),
        P("section", None, "tensor"),
        P("section", None, "tensor"),
        P("section", "tensor", None),
        P("section", None),
        P("section", None, None),
        P("section", None, None, "tensor"),
        P("section", None, None, "tensor"),
        P("section", None, "tensor", None),
        P("section", None, "tensor"),
        P("section", None, "tensor"),
        P("section", "tensor", None),
    )
    return jax.shard_map(
        functools.partial(on_device, mesh.shape["tensor"], mesh.shape["dp"]),
        mesh=mesh,
        in_specs=placed,
        out_specs=(
            P("section", "dp", "tensor", None),
            P("section", "dp", "tensor", None),
            P("section", None),
            P("section", "dp", "tensor"),
            P("section", "dp", "tensor"),
            P("section", "dp", "tensor"),
            P("section", "tensor", "dp"),
            P("section", None),
            P("section", None, None),
            P("section", None, "dp", "tensor"),
            P("section", None, "dp", "tensor"),
            P("section", None, "tensor", "dp"),
            P("section", "dp", "tensor"),
            P("section", "dp", "tensor"),
            P("section", "tensor", "dp"),
            P("section"),
        ),
        check_vma=False,
    )
```

```python
import functools

import jax
import jax.numpy as jnp
import numpy as np
from jax import lax
from jax.experimental import pallas as pl
from jax.experimental.pallas import tpu as pltpu
from jax.sharding import PartitionSpec as P

HEAD_DIM = 64
HALF_DIM = HEAD_DIM // 2
EPSILON = 1e-06
ALPHA = 0.01
THETA = 10000.0
MASKED = -1e30
LANES = 256
VMEM_LIMIT = 63 * 2**20 + 2**19

f32 = jnp.float32
bf16 = jnp.bfloat16
MESH = pl.DeviceIdType.MESH
ANY = pl.BlockSpec(memory_space=pl.ANY)
VMEM = pl.BlockSpec(memory_space=pltpu.VMEM)
SMEM = pl.BlockSpec(memory_space=pltpu.SMEM)


def dot(left, right, left_dim, right_dim):
    return lax.dot_general(
        left, right, (((left_dim,), (right_dim,)), ((), ())), preferred_element_type=f32
    )


def rope_tables(seq_len):
    frequency = (THETA ** (-np.arange(HALF_DIM, dtype=np.float32) / HALF_DIM)).astype(np.float32)
    angles = np.arange(seq_len, dtype=np.float32)[:, None] * frequency[None, :]
    cosine, sine = np.cos(angles), np.sin(angles)
    return np.concatenate([cosine, cosine, -sine, sine], axis=-1).astype(np.float32)


def turn_halves(values):
    return jnp.concatenate([values[:, HALF_DIM:], values[:, :HALF_DIM]], axis=1)


class Place:
    def __init__(self, ranks, planes):
        self.s = lax.axis_index("section")
        self.t = lax.axis_index("tensor")
        self.z = lax.axis_index("dp")
        self.ranks, self.planes = ranks, planes
        self.odd = lax.rem(self.z, 2)
        self.sibling = (1 - self.s, self.t, self.z)
        self.partner = (self.s, self.t, self.z + 1 - 2 * self.odd)

    def peer(self, k):
        return lax.rem(self.t + k, self.ranks)

    def peer_id(self, k):
        return (self.s, self.peer(k), self.z)

    def plane_id(self, k):
        return (self.s, self.t, lax.rem(self.z + k, self.planes))

    def greet(self):
        barrier = pltpu.get_barrier_semaphore()
        others = [self.sibling] + [self.peer_id(k) for k in range(1, self.ranks)]
        for k in range(1, self.planes):
            _, t, z = self.plane_id(k)
            others += [(self.s, t, z), (1 - self.s, t, z)]
        for other in others:
            pl.semaphore_signal(barrier, inc=1, device_id=other, device_id_type=MESH)
        pl.semaphore_wait(barrier, len(others))


def remote(src, dst, send, recv, device):
    return pltpu.make_async_remote_copy(
        src_ref=src, dst_ref=dst, send_sem=send, recv_sem=recv, device_id=device, device_id_type=MESH
    )


def gather_rows(place, full, rows, send, recv):
    mine = full.at[pl.ds(place.t * rows, rows)]
    copies = []
    for k in range(1, place.ranks):
        copy = remote(mine, mine, send.at[k - 1], recv.at[k - 1], place.peer_id(k))
        copy.start()
        copies.append(copy)
    return copies


def scatter_block(place, stage, landing, rows, lo, width, send, recv):
    copies = []
    for k in range(1, place.ranks):
        src = stage.at[pl.ds(place.peer(k) * rows, rows), pl.ds(lo, width)]
        dst = landing.at[k - 1, :, pl.ds(lo, width)]
        copy = remote(src, dst, send.at[k - 1], recv.at[k - 1], place.peer_id(k))
        copy.start()
        copies.append(copy)
    return copies


def landed_sum(own, landing, ranks):
    total = own
    for k in range(ranks - 1):
        total = total + landing[k].astype(f32)
    return total


def rms_rows(values, gain):
    return values * lax.rsqrt(jnp.mean(values * values, axis=-1, keepdims=True) + EPSILON) * gain


def rms_back(values, gain, grad):
    r = lax.rsqrt(jnp.mean(values * values, axis=-1, keepdims=True) + EPSILON)
    normed = values * r
    scaled = grad * gain
    inner = jnp.mean(scaled * normed, axis=-1, keepdims=True)
    return r * (scaled - normed * inner), jnp.sum(grad * normed, axis=0, keepdims=True)


def name_rows(routes):
    expert = lax.broadcasted_iota(jnp.int32, (8, routes.shape[1]), 0)
    named = routes[0:1] == expert
    for j in range(1, routes.shape[0]):
        named = named | (routes[j : j + 1] == expert)
    return named.astype(f32)


def column(matrix, index):
    lane = lax.broadcasted_iota(jnp.int32, matrix.shape, 1)
    return jnp.sum(jnp.where(lane == index, matrix, 0.0), axis=1, keepdims=True)


def load_choice(first, pairs, sems):
    for i, (own, other, dst) in enumerate(pairs):

        @pl.when(first)
        def _(own=own, dst=dst, i=i):
            pltpu.make_async_copy(own, dst, sems.at[i]).start()

        @pl.when(jnp.logical_not(first))
        def _(other=other, dst=dst, i=i):
            pltpu.make_async_copy(other, dst, sems.at[i]).start()

    return [pltpu.make_async_copy(own, dst, sems.at[i]) for i, (own, other, dst) in enumerate(pairs)]


N_ATTN = 4
N_FFN = 6
SENT_AT_ONCE = 3


def attn_targets(w_in, w_out, heads_width):
    return [w_in.at[pl.ds(i * heads_width, heads_width)] for i in range(3)] + [w_out]


def ffn_targets(wg, wu, wd):
    experts = wg.shape[0] - 1
    first = pl.ds(0, experts)
    return [wg.at[first], wu.at[first], wd.at[first], wg.at[experts], wu.at[experts], wd.at[experts]]


def both_kernel(ranks, planes, top, *refs):
    (lens, bnd, routes, gain_a_own, gain_f_own, router, tables), refs = refs[:7], refs[7:]
    own, refs = refs[:10], refs[10:]
    other, refs = refs[:10], refs[10:]
    (nf_o, q_o, k_o, v_o, p_o, mx_o, hf_o, g_o, u_o, hp_o, land, land_z), refs = refs[:12], refs[12:]
    (out_rows, in_grads, gain_a_out, gain_f_out, router_out, balance), refs = refs[:6], refs[6:]
    (nf, qs, ks, vs, ps, mx, hf, gs, us, hp), refs = refs[:10], refs[10:]
    (w_in, wo, wg, wu, wd), refs = refs[:5], refs[5:]
    (dyf, dyp, acts, gp, up, ap, coef, gate_sum), refs = refs[:8], refs[8:]
    (stage, stage_y, land_a, land_f, land_y, row_buf, d_mid), refs = refs[:7], refs[7:]
    (sent, got, quarter, df, ds, dqkv, gw, got_a, half_a, pair_in), refs = refs[:10], refs[10:]
    (xs, mid, small, o_small, probs_sum, cnt, o_cnt, cnt_in), refs = refs[:8], refs[8:]
    (o_bnd, o_routes, o_gain_a, o_gain_f, o_router, y_low), refs = refs[:6], refs[6:]
    (packs, pack_t, pack_z, gain_now), refs = refs[:4], refs[4:]
    (ag_s, ag_r, rsa_s, rsa_r, rsf_s, rsf_r, rsy_s, rsy_r, ex_s, ex_r), refs = refs[:10], refs[10:]
    (hp_s, hp_r, dp_s, dp_r, cz_s, cz_r, cs_s, cs_r, row_s, row_r), refs = refs[:10], refs[10:]
    (sw_s, sw_r, zs, zr, zl, as_s, as_r, az_s, az_r, az_l), refs = refs[:10], refs[10:]
    (pr_s, pr_r, gr_s, gr_r, pk_s, pk_r, pt_s, pt_r, pz_s, pz_r, ffn_sem, attn_sem, save_sem) = refs

    place = Place(ranks, planes)
    s, t, z, odd = place.s, place.t, place.z, place.odd
    rows, width = bnd.shape[1], bnd.shape[2]
    seq_len = hf.shape[0]
    experts = wg.shape[0] - 1
    blocks = experts + 1
    inner = wg.shape[2]
    half = inner // 2
    part = half // 2
    heads = qs.shape[0]
    heads_width = heads * HEAD_DIM
    chunk = width // planes
    chunks = width // LANES
    mine = pl.ds(t * rows, rows)
    my_lanes = pl.ds(pl.multiple_of(odd * half, half), half)
    far_lanes = pl.ds(pl.multiple_of((1 - odd) * half, half), half)
    slot = s * planes + z
    scale = HEAD_DIM ** (-0.5)

    def ffn_weights(l):
        targets = ffn_targets(wg, wu, wd)
        return load_choice(s == l, [(own[4 + i], other[4 + i], targets[i]) for i in range(N_FFN)], ffn_sem)

    def attn_weights(l):
        targets = attn_targets(w_in, wo, heads_width)
        return load_choice(s == l, [(own[i], other[i], targets[i]) for i in range(N_ATTN)], attn_sem)

    ffn_state = [(gs, g_o), (us, u_o), (hf, hf_o), (hp, hp_o)]
    attn_state = [(nf, nf_o), (qs, q_o), (ks, k_o), (vs, v_o), (ps, p_o), (mx, mx_o)]

    def moves(pairs, first, back):
        copies = []
        for i, (inside, outside) in enumerate(pairs):
            src, dst = (outside, inside) if back else (inside, outside)
            copies.append(pltpu.make_async_copy(src, dst, save_sem.at[first + i]))
        return copies

    def begin(copies):
        for copy in copies:
            copy.start()
        return copies

    def finish_all(copies):
        for copy in copies:
            copy.wait()

    def gain_of(l, mine_ref, other_ref):
        return jnp.where(s == l, mine_ref[...], other_ref[...])

    def route_weights(l):
        value = jnp.where(s == l, router[...], o_router[...]).astype(f32)
        if experts < 8:
            value = jnp.concatenate([value, jnp.zeros((8 - experts, width), f32)], axis=0)
        return value.astype(bf16)

    def to_owner(l, src, dst, send, recv, local):
        for c in range(planes):
            own_copy = (z == c) & (s == l)

            @pl.when(own_copy)
            def _(c=c):
                pltpu.make_async_copy(src(c), dst, local).start()

            @pl.when(jnp.logical_not(own_copy))
            def _(c=c):
                remote(src(c), dst, send.at[c], recv.at[slot], (l, t, c)).start()

    def sent_to_owner(l, whole, dst, send, recv, local):
        for c in range(planes):
            own_copy = (z == c) & (s == l)

            @pl.when(own_copy)
            def _(c=c):
                pltpu.make_async_copy(whole.at[c], dst.at[slot], local).wait()

            @pl.when(jnp.logical_not(own_copy))
            def _(c=c):
                remote(whole.at[c], dst.at[slot], send.at[c], recv.at[slot], (l, t, c)).wait_send()

    def arrived(dst, send, recv):
        for source in range(2 * planes):

            @pl.when(source != slot)
            def _(source=source):
                remote(
                    dst.at[source], dst.at[source], send.at[0], recv.at[source], place.sibling
                ).wait_recv()

    def scatter_product(product, staged, landing, send, recv):
        copies = []
        for n in range(chunks):
            lanes = slice(n * LANES, (n + 1) * LANES)
            staged[:, lanes] = product(lanes).astype(bf16)
            copies += scatter_block(
                place, staged, landing, rows, n * LANES, LANES, send.at[n], recv.at[n]
            )
        return copies

    def share_of(l):
        return remote(half_a.at[l, 1 - odd], pair_in.at[l], pr_s.at[l], pr_r.at[l], place.partner)

    side = 2 * heads_width

    def swap_half(l):
        theirs = pl.ds(pl.multiple_of((1 - s) * side, 128), side)
        return remote(gw.at[:, theirs], got_a, as_s.at[l], as_r.at[l], place.sibling)

    def share_half(l):
        swap_half(l).wait()
        ours = pl.ds(pl.multiple_of(s * side, 128), side)
        kept = (gw[:, ours].astype(f32) + got_a[...].astype(f32)).astype(bf16)
        for side_b in range(2):
            for c in range(planes):
                lo = c * chunk + side_b * (chunk // 2)
                half_a[l, side_b, c] = kept[lo : lo + chunk // 2]
        share_of(l).start()

    def send_half(l):
        share_of(l).wait()
        half_a[l, odd] = (half_a[l, odd].astype(f32) + pair_in[l].astype(f32)).astype(bf16)
        to_owner(l, lambda c: half_a.at[l, odd, c], land_z.at[slot], az_s.at[l], az_r, az_l.at[l])

    place.greet()
    first_w = 5
    ex_pairs = [
        (bnd.at[1 - s], o_bnd),
        (gain_a_own, o_gain_a),
        (gain_f_own, o_gain_f),
        (router, o_router),
        (routes.at[1 - s], o_routes),
    ] + [(own[i], other[i]) for i in range(10)]
    exchange = [
        remote(src, dst, ex_s.at[i], ex_r.at[i], place.sibling) for i, (src, dst) in enumerate(ex_pairs)
    ]
    begin(exchange)
    row8 = lax.broadcasted_iota(jnp.int32, (8, seq_len), 0)
    token8 = lax.broadcasted_iota(jnp.int32, (8, seq_len), 1)
    length = lens[s]
    cosine, signed = tables[:, :HEAD_DIM], tables[:, HEAD_DIM:]

    def attn_begin(l):
        if l == 0:

            @pl.when(s == 0)
            def _():
                gain_now[...] = gain_a_own[...]

            @pl.when(s != 0)
            def _():
                gain_now[...] = o_gain_a[...]

        else:
            gain_now[...] = gain_of(l, gain_a_own, o_gain_a)
        nf[mine] = rms_rows(xs[l].astype(f32), gain_now[...]).astype(bf16)
        return gather_rows(place, nf, rows, ag_s.at[l, 0], ag_r.at[l, 0])

    def attn_forward(l, gathering, loads, between):
        finish_all(loads)
        finish_all(gathering)
        between()
        projected = dot(nf[...], w_in[...], 1, 1)
        for j, dst in enumerate((qs, ks, vs)):
            for h in range(heads):
                at = j * heads_width + h * HEAD_DIM
                piece = projected[:, at : at + HEAD_DIM]
                if j < 2:
                    piece = piece * cosine + turn_halves(piece) * signed
                dst[h] = piece.astype(bf16)
        place_q = lax.broadcasted_iota(jnp.int32, (seq_len, seq_len), 0)
        place_k = lax.broadcasted_iota(jnp.int32, (seq_len, seq_len), 1)
        allowed = (place_k <= place_q) & (place_k < length)
        for h in range(heads):
            scores = dot(qs[h], ks[h], 1, 1) * scale
            scores = jnp.where(allowed, scores, MASKED)
            peak = jnp.max(scores, axis=-1, keepdims=True)
            raised = jnp.exp(scores - peak)
            total = jnp.sum(raised, axis=-1, keepdims=True)
            weights = (raised / total).astype(bf16)
            ps[h] = weights
            mx[:, h * HEAD_DIM : (h + 1) * HEAD_DIM] = dot(weights, vs[h], 1, 0).astype(bf16)
        return scatter_product(
            lambda lanes: dot(mx[...], wo[:, lanes], 1, 0),
            stage,
            land_a,
            rsa_s.at[l, pl.ds(0, chunks)],
            rsa_r.at[l, pl.ds(0, chunks)],
        )

    def attn_finish(l, scattering):
        finish_all(scattering)
        middle = xs[l].astype(f32) + landed_sum(stage[mine].astype(f32), land_a, ranks)
        mid[l] = middle
        hf[mine] = rms_rows(middle, gain_of(l, gain_f_own, o_gain_f)).astype(bf16)
        return gather_rows(place, hf, rows, ag_s.at[l, 1], ag_r.at[l, 1])

    def route(l):
        names = name_rows(jnp.where(s == l, routes[s], o_routes[...]))
        logits = dot(route_weights(l), hf[...], 1, 1)
        logits = jnp.where(row8 < experts, logits, MASKED)
        raised = jnp.exp(logits - jnp.max(logits, axis=0, keepdims=True))
        raised = jnp.where(row8 < experts, raised, 0.0)
        chances = raised / jnp.sum(raised, axis=0, keepdims=True)
        per_chosen = names / jnp.sum(chances * names, axis=0, keepdims=True)
        gates = chances * per_chosen
        small[l, 0:8] = chances
        small[l, 8:16] = gates
        small[l, 16:24] = per_chosen
        remote(small.at[l], o_small.at[l], hp_s.at[l, 1], hp_r.at[l, 1], place.partner).start()
        summed = jnp.sum(jnp.where(token8 < length, chances, 0.0), axis=1, keepdims=True)
        probs_sum[l] = jnp.broadcast_to(summed, (8, 128))
        coef[...] = jnp.where(row8 == experts, 1.0, gates).T

    def split_acts(e, value):
        low, high = value[:, :half], value[:, half:]
        acts[e] = jnp.where(odd == 0, low, high).astype(bf16)
        gp[e] = jnp.where(odd == 0, high, low).astype(bf16)

    def branch_product(lanes):
        total = dot(acts[0], wd[0, my_lanes, lanes], 1, 0) + dot(gp[0], wd[0, far_lanes, lanes], 1, 0)
        for e in range(1, blocks):
            total = total + dot(acts[e], wd[e, my_lanes, lanes], 1, 0)
            total = total + dot(gp[e], wd[e, far_lanes, lanes], 1, 0)
        return total

    def output_rows(l, landing, staged):
        output = mid[l] + landed_sum(staged[mine].astype(f32), landing, ranks)
        y_low[l] = output.astype(bf16)

        @pl.when(s == l)
        def _():
            out_rows[s] = y_low[l]

        @pl.when(s != l)
        def _():
            remote(y_low.at[l], out_rows.at[s], row_s, row_r, place.sibling).start()

    @pl.when(s == 0)
    def _():
        xs[0] = bnd[0]

    @pl.when(s != 0)
    def _():
        finish_all(exchange[:first_w])
        xs[0] = o_bnd[...]
        for copy in exchange[first_w : first_w + N_ATTN]:
            copy.wait_recv()

    gathering = attn_begin(0)
    loads = attn_weights(0)
    counted = jnp.zeros((8, 1), f32)
    for q in range(2):
        live = jnp.where(token8 < lens[q], 1.0, 0.0)
        counts = jnp.where(row8 == 7, live, name_rows(routes[q]) * live)
        counted = counted + jnp.sum(counts, axis=1, keepdims=True)
    cnt[...] = jnp.broadcast_to(counted, cnt.shape)
    count_copies = begin(
        [
            remote(cnt, cnt_in.at[k - 1], cz_s.at[k - 1], cz_r.at[k - 1], place.plane_id(k))
            for k in range(1, planes)
        ]
    )

    @pl.when(s == 0)
    def _():
        finish_all(exchange[:first_w])

    cotangent = jnp.where(s == 0, o_bnd[...], bnd[1]).astype(f32)
    position = lax.broadcasted_iota(jnp.int32, (rows, width), 0) + t * rows
    dyf[mine] = jnp.where(position < length, cotangent, 0.0).astype(bf16)
    cot_gather = []

    def gather_cotangent():
        cot_gather.extend(gather_rows(place, dyf, rows, ag_s.at[1, 2], ag_r.at[1, 2]))

    scattering = attn_forward(0, gathering, loads, gather_cotangent)

    @pl.when(s != 0)
    def _():
        for copy in exchange[first_w + N_ATTN :]:
            copy.wait_recv()

    ffn_loads = ffn_weights(0)
    attn_saves = begin(moves(attn_state, 4, False))
    gathering = attn_finish(0, scattering)

    @pl.when(s == 0)
    def _():
        for copy in exchange[first_w : first_w + N_ATTN]:
            copy.wait_recv()

    attn_w = attn_weights(1)
    finish_all(count_copies)
    total = cnt[...]
    for k in range(planes - 1):
        total = total + cnt_in[k]
    cnt[...] = total
    share_counts = remote(cnt, o_cnt, cs_s, cs_r, place.sibling)
    share_counts.start()
    finish_all(ffn_loads)
    finish_all(gathering)
    ffn_saves = begin(moves(ffn_state[2:3], 2, False))
    hidden_sent = [remote(hf, hp_o, hp_s.at[0, 0], hp_r.at[0, 0], place.partner)]
    begin(hidden_sent)
    route(0)

    def forward_expert(e, carry):
        gate_h = dot(hf[...], wg[e], 1, 0)
        up_h = dot(hf[...], wu[e], 1, 0)
        gs[e] = gate_h.astype(bf16)
        us[e] = up_h.astype(bf16)
        split_acts(e, gate_h * jax.nn.sigmoid(gate_h) * up_h * column(coef[...], e))
        return carry

    lax.fori_loop(0, blocks, forward_expert, 0)
    ffn_saves += begin(moves(ffn_state[:2], 0, False))
    finish_all(attn_saves)
    scat = scatter_product(branch_product, stage, land_f, rsf_s.at[0, 0], rsf_r.at[0, 0])

    @pl.when(s == 0)
    def _():
        for copy in exchange[first_w + N_ATTN :]:
            copy.wait_recv()

    ffn_loads = ffn_weights(1)
    finish_all(cot_gather)
    cot_sent = remote(dyf, dyp.at[1], dp_s.at[1, 0], dp_r.at[1, 0], place.partner)
    cot_sent.start()
    finish_all(scat)
    output_rows(0, land_f, stage)
    xs[1] = y_low[0]

    gathering = attn_begin(1)
    finish_all(hidden_sent)
    finish_all(ffn_saves)
    scattering = attn_forward(1, gathering, attn_w, lambda: None)
    gathering = attn_finish(1, scattering)
    finish_all(ffn_loads)
    finish_all(gathering)
    hidden_sent = [remote(hf, hp, hp_s.at[1, 0], hp_r.at[1, 0], place.partner)]
    begin(hidden_sent)
    route(1)
    gate_sum[...] = jnp.zeros_like(gate_sum)
    lane8 = lax.broadcasted_iota(jnp.int32, gate_sum.shape, 1)

    def expert_grads(e, gate_h, up_h, raw):
        sig = jax.nn.sigmoid(gate_h)
        silu = gate_h * sig
        acted = silu * up_h
        inner_sum = jnp.sum(acted * raw, axis=1, keepdims=True)
        gate_sum[...] = jnp.where(lane8 == e, inner_sum, gate_sum[...])
        weight = column(coef[...], e)
        d_acted = raw * weight
        gs[e] = (d_acted * up_h * (sig + silu * (1.0 - sig))).astype(bf16)
        us[e] = (d_acted * silu).astype(bf16)
        return acted * weight

    def both_expert(e, carry):
        gate_h = dot(hf[...], wg[e], 1, 0)
        up_h = dot(hf[...], wu[e], 1, 0)
        raw = dot(dyf[...], wd[e], 1, 1)
        split_acts(e, expert_grads(e, gate_h, up_h, raw))
        return carry

    def back_expert(e, carry):
        raw = dot(dyf[...], wd[e], 1, 1)
        value = expert_grads(e, gs[e].astype(f32), us[e].astype(f32), raw)
        acts[e] = jnp.where(odd == 0, value[:, :half], value[:, half:]).astype(bf16)
        return carry

    lax.fori_loop(0, blocks, both_expert, 0)
    share_counts.wait()
    y_scat = []

    for l in (1, 0):
        here = s == l
        if l == 0:
            finish_all(ffn_loads)
            finish_all(ffn_back)
            coef[...] = jnp.where(row8 == experts, 1.0, small[l, 8:16]).T
            gate_sum[...] = jnp.zeros_like(gate_sum)
            to_partner = [remote(dyf.at[mine], dyp.at[l, mine], dp_s.at[l, 0], dp_r.at[l, 0], place.partner)]
            begin(to_partner)
            for k, copy in enumerate(gathering, 1):
                copy.wait()
                they = pl.ds(place.peer(ranks - k) * rows, rows)
                to_partner += begin(
                    [remote(dyf.at[they], dyp.at[l, they], dp_s.at[l, k], dp_r.at[l, k], place.partner)]
                )
            share_half(1)
            for e in range(SENT_AT_ONCE, blocks):
                send_later(e)
            lax.fori_loop(0, blocks, back_expert, 0)
        else:
            to_partner = [cot_sent]
        chances, gates, per_chosen = small[l, 0:8], small[l, 8:16], small[l, 16:24]
        totals = jnp.where(here, cnt[...], o_cnt[...])
        tokens_all = totals[7:8, 0:1]
        share = totals[:, 0:1] / (top * tokens_all)
        aux = jnp.where((token8 < length) & (t == 0), ALPHA * experts * share / tokens_all, 0.0)
        d_gates = gate_sum[...].T
        common = jnp.sum(d_gates * gates, axis=0, keepdims=True)
        d_chances = per_chosen * (d_gates - common) + aux
        d_logits = chances * (d_chances - jnp.sum(chances * d_chances, axis=0, keepdims=True))
        d_logits = d_logits.astype(bf16)
        router_grad = dot(d_logits, hf[...], 1, 0)
        route_w = route_weights(l)

        def hidden_product(lanes, d_logits=d_logits, route_w=route_w):
            total = dot(d_logits, route_w[:, lanes], 0, 0)
            for e in range(blocks):
                total = total + dot(gs[e], wg[e, lanes], 1, 1)
                total = total + dot(us[e], wu[e, lanes], 1, 1)
            return total

        scat = scatter_product(hidden_product, stage, land_f, rsf_s.at[l, 1], rsf_r.at[l, 1])
        if l == 1:
            y_scat = scatter_product(branch_product, stage_y, land_y, rsy_s, rsy_r)
        finish_all(to_partner)
        if l == 1:
            finish_all(hidden_sent)
        remote(small.at[l], o_small.at[l], hp_s.at[l, 1], hp_r.at[l, 1], place.partner).wait()
        coef[...] = jnp.where(row8 == experts, 1.0, o_small[l, 8:16]).T

        def partner_expert(e, carry, l=l):
            gate_h = dot(hp[...], wg[e, :, my_lanes], 1, 0)
            up_h = dot(hp[...], wu[e, :, my_lanes], 1, 0)
            raw = dot(dyp[l], wd[e, my_lanes], 1, 1)
            sig = jax.nn.sigmoid(gate_h)
            silu = gate_h * sig
            weight = column(coef[...], e)
            ap[e] = (silu * up_h * weight).astype(bf16)
            d_acted = raw * weight
            gp[e] = (d_acted * up_h * (sig + silu * (1.0 - sig))).astype(bf16)
            up[e] = (d_acted * silu).astype(bf16)
            return carry

        lax.fori_loop(0, blocks, partner_expert, 0)
        finish_all(scat)
        d_hidden = landed_sum(stage[mine].astype(f32), land_f, ranks)
        d_norm, gain_f_grad = rms_back(mid[l], gain_of(l, gain_f_own, o_gain_f), d_hidden)
        d_mid[...] = dyf[mine].astype(f32) + d_norm
        df[mine] = d_mid[...].astype(bf16)
        gathering = gather_rows(place, df, rows, ag_s.at[l, 3], ag_r.at[l, 3])

        def swap_of(e, l=l):
            return remote(sent.at[e], got.at[e], sw_s.at[e], sw_r.at[e], place.sibling)

        def send_grads(e, l=l):
            three = pl.ds(e * 3, 3)
            to_owner(l, lambda c: quarter.at[l, c, three], land.at[slot, three], zs.at[l], zr, zl.at[l])

        def finish(e, l=l, send_grads=send_grads):
            swap_of(e).wait()
            for j in range(3):
                at = e * 3 + j
                for c in range(planes):
                    quarter[l, c, at] = (
                        quarter[l, c, at].astype(f32) + got[e, j, c].astype(f32)
                    ).astype(bf16)

            @pl.when(jnp.logical_or(l == 0, e < SENT_AT_ONCE))
            def _():
                send_grads(e)

        def weight_grads(e, carry, l=l):
            sources = ((hf, gs, hp, gp), (hf, us, hp, up))
            for j in range(3):
                if j < 2:
                    left, right, left_p, right_p = sources[j]
                    value = dot(left[...], right[e, :, my_lanes], 0, 0) + dot(left_p[...], right_p[e], 0, 0)
                else:
                    value = dot(dyf[...], acts[e], 0, 0) + dot(dyp[l], ap[e], 0, 0)
                low, high = value[:, :part], value[:, part:]
                kept = jnp.where(s == 0, low, high).astype(bf16)
                given = jnp.where(s == 0, high, low).astype(bf16)
                for c in range(planes):
                    quarter[l, c, e * 3 + j] = kept[c * chunk : (c + 1) * chunk]
                    sent[e, j, c] = given[c * chunk : (c + 1) * chunk]
            swap_of(e).start()

            @pl.when((e > 0) & (s == 1))
            def _():
                finish(e - 1)

            return carry

        if l == 1:
            send_later = send_grads
        else:
            send_half(1)
        lax.fori_loop(0, blocks, weight_grads, 0)

        @pl.when(s == 1)
        def _(finish=finish):
            finish(blocks - 1)

        if l == 1:
            ffn_loads = ffn_weights(0)
            ffn_back = begin(moves(ffn_state, 0, True))
        else:
            finish_all(attn_w)
            finish_all(attn_back)
        finish_all(gathering)
        for h in range(heads):
            span = slice(h * HEAD_DIM, (h + 1) * HEAD_DIM)
            d_mixed = dot(df[...], wo[span], 1, 1).astype(bf16)
            for lo in range(0, seq_len, LANES):
                reach = lo + LANES
                weights = ps[h, lo:reach, 0:reach].astype(f32)
                d_probs = dot(d_mixed[lo:reach], vs[h, 0:reach], 1, 1)
                total = jnp.sum(weights * d_probs, axis=-1, keepdims=True)
                ds[lo:reach, 0:reach] = (weights * (d_probs - total)).astype(bf16)
                if reach < seq_len:
                    ds[lo:reach, reach:] = jnp.zeros((LANES, seq_len - reach), bf16)
            d_value = dot(ps[h], d_mixed, 0, 0)
            d_query = dot(ds[...], ks[h], 1, 0) * scale
            d_key = dot(ds[...], qs[h], 0, 0) * scale
            d_query = d_query * cosine - turn_halves(d_query) * signed
            d_key = d_key * cosine - turn_halves(d_key) * signed
            for j, value in enumerate((d_query, d_key, d_value)):
                at = j * heads_width + h * HEAD_DIM
                dqkv[:, at : at + HEAD_DIM] = value.astype(bf16)
        scat = scatter_product(
            lambda lanes: dot(dqkv[...], w_in[:, lanes], 1, 0), stage, land_a, rsa_s.at[l, pl.ds(chunks, chunks)], rsa_r.at[l, pl.ds(chunks, chunks)]
        )

        @pl.when(s == 0)
        def _(finish=finish):
            def each(e, carry):
                finish(e)
                return carry

            lax.fori_loop(0, blocks, each, 0)

        three_widths = 3 * heads_width
        gw[:, :three_widths] = dot(nf[...], dqkv[...], 0, 0).astype(bf16)
        gw[:, three_widths:] = dot(df[...], mx[...], 0, 0).astype(bf16)
        swap_half(l).start()
        finish_all(scat)
        d_normed = landed_sum(stage[mine].astype(f32), land_a, ranks)
        d_norm, gain_a_grad = rms_back(xs[l].astype(f32), gain_of(l, gain_a_own, o_gain_a), d_normed)
        dx = d_mid[...] + d_norm
        if l == 1:
            low_dx = dx.astype(bf16)
            dyf[mine] = low_dx
            gathering = gather_rows(place, dyf, rows, ag_s.at[0, 2], ag_r.at[0, 2])
            dx = low_dx.astype(f32)
            attn_w = attn_weights(0)
            attn_back = begin(moves(attn_state, 4, True))
            finish_all(y_scat)
            output_rows(1, land_y, stage_y)
        pack = jnp.concatenate(
            [
                jnp.concatenate([gain_a_grad, gain_f_grad, router_grad[:6]], axis=0),
                jnp.concatenate(
                    [jnp.zeros((2, 128), f32), jnp.where(t == 0, probs_sum[l, 0:6], 0.0)], axis=0
                ),
            ],
            axis=1,
        )

        @pl.when(here)
        def _(dx=dx, pack=pack):
            in_grads[s] = dx
            packs[0] = pack

        @pl.when(jnp.logical_not(here))
        def _(dx=dx, pack=pack):
            row_buf[...] = dx
            packs[1] = pack
            remote(row_buf, in_grads.at[s], gr_s, gr_r, place.sibling).start()
            remote(packs.at[1], packs.at[2], pk_s, pk_r, place.sibling).start()

    share_half(0)
    send_half(0)
    remote(packs.at[1], packs.at[2], pk_s, pk_r, place.sibling).wait()
    packs[0] = packs[0] + packs[2]
    finish_all(
        begin(
            [
                remote(packs.at[0], pack_t.at[k - 1], pt_s.at[k - 1], pt_r.at[k - 1], place.peer_id(k))
                for k in range(1, ranks)
            ]
        )
    )
    total = packs[0]
    for k in range(ranks - 1):
        total = total + pack_t[k]
    packs[0] = total
    finish_all(
        begin(
            [
                remote(packs.at[0], pack_z.at[k - 1], pz_s.at[k - 1], pz_r.at[k - 1], place.plane_id(k))
                for k in range(1, planes)
            ]
        )
    )
    total = packs[0]
    for k in range(planes - 1):
        total = total + pack_z[k]
    gain_a_out[...] = total[0:1, :width]
    gain_f_out[...] = total[1:2, :width]
    router_out[...] = total[2 : 2 + experts, :width]
    tokens_all = cnt[7:8, 0:1]
    products = cnt[0:experts, 0:1] / (top * tokens_all) * total[2 : 2 + experts, width : width + 1]
    balance[...] = experts * jnp.sum(products, axis=0, keepdims=True) / tokens_all

    for copy in exchange[first_w:]:
        copy.wait_send()
    remote(y_low.at[1 - s], out_rows.at[s], row_s, row_r, place.sibling).wait_send()
    remote(y_low.at[1 - s], out_rows.at[1 - s], row_s, row_r, place.sibling).wait_recv()
    remote(row_buf, in_grads.at[s], gr_s, gr_r, place.sibling).wait_send()
    remote(row_buf, in_grads.at[1 - s], gr_s, gr_r, place.sibling).wait_recv()
    for l in (1, 0):
        sent_to_owner(l, quarter.at[l], land, zs.at[l], zr, zl.at[l])
        sent_to_owner(l, half_a.at[l, odd], land_z, az_s.at[l], az_r, az_l.at[l])
    arrived(land, zs.at[0], zr)
    arrived(land_z, az_s.at[0], az_r)


def finish_kernel(planes, land, land_z, *refs):
    ins, outs, refs = refs[:6], refs[6:12], refs[12:]
    g_gate, g_up, g_down, s_gate, s_up, s_down, wq_out, wk_out, wv_out, wo_out = refs
    e = pl.program_id(0)
    experts = pl.num_programs(0) - 1
    part = land.shape[3]
    heads_width = wq_out.shape[1]
    for j, (routed, common) in enumerate(((g_gate, s_gate), (g_up, s_up), (g_down, s_down))):
        for core in range(2):
            for parity in range(2):
                value = land[core * planes + parity, j].astype(f32)
                for pair in range(1, planes // 2):
                    value = value + land[core * planes + 2 * pair + parity, j].astype(f32)
                lo = (2 * parity + core) * part

                @pl.when(e < experts)
                def _(value=value, lo=lo, routed=routed):
                    routed[0, :, lo : lo + part] = value

                @pl.when(e == experts)
                def _(value=value, lo=lo, common=common):
                    common[:, lo : lo + part] = value

    @pl.when(e == 1)
    def _():
        for src, dst in zip(ins, outs):
            dst[...] = src[...]
        sides = []
        for core in range(2):
            halves = []
            for parity in range(2):
                value = land_z[core * planes + parity].astype(f32)
                for pair in range(1, planes // 2):
                    value = value + land_z[core * planes + 2 * pair + parity].astype(f32)
                halves.append(value)
            sides.append(jnp.concatenate(halves, axis=0))
        wq_out[...] = sides[0][:, :heads_width]
        wk_out[...] = sides[0][:, heads_width:]
        wv_out[...] = sides[1][:, :heads_width]
        wo_out[...] = sides[1][:, heads_width:].T


def params(collective_id):
    return pltpu.CompilerParams(
        collective_id=collective_id, has_side_effects=True, vmem_limit_bytes=VMEM_LIMIT
    )


def shape_of(*dims, dtype=bf16):
    return jax.ShapeDtypeStruct(dims, dtype)


def on_device(ranks, planes, *args):
    (boundary, lengths, routes, attn_gain, w_query, w_key, w_value, w_out, ffn_gain, router) = args[:10]
    ffn_own = tuple(a[0] for a in args[10:])
    attn_own = (w_query[0].T, w_key[0].T, w_value[0].T, w_out[0])
    rows, width = boundary.shape[2:]
    seqs, seq_len = routes.shape[1:3]
    top = routes.shape[3]
    experts, _, inner = ffn_own[0].shape
    blocks = experts + 1
    heads_width = w_query.shape[2]
    heads = heads_width // HEAD_DIM
    chunks = width // LANES
    half, part = inner // 2, inner // 4
    chunk = width // planes
    peers = ranks - 1
    dma = pltpu.SemaphoreType.DMA

    def vmem(*dims, dtype=bf16):
        return pltpu.VMEM(dims, dtype)

    routes_t = jnp.swapaxes(routes[0], 1, 2)
    router_t = router[0].T
    tables = jnp.asarray(rope_tables(seq_len))
    head_shape = (heads, seq_len, HEAD_DIM)
    states = [
        (seq_len, width),
        head_shape,
        head_shape,
        head_shape,
        (heads, seq_len, seq_len),
        (seq_len, heads_width),
        (seq_len, width),
        (blocks, seq_len, inner),
        (blocks, seq_len, inner),
        (seq_len, width),
    ]
    weights = attn_own + ffn_own
    small_outs = [
        shape_of(2, rows, width),
        shape_of(seqs, rows, width, dtype=f32),
        shape_of(1, width, dtype=f32),
        shape_of(1, width, dtype=f32),
        shape_of(experts, width, dtype=f32),
        shape_of(1, 1, dtype=f32),
    ]
    result = pl.pallas_call(
        functools.partial(both_kernel, ranks, planes, top),
        out_shape=[shape_of(*w.shape) for w in weights]
        + [shape_of(*dims) for dims in states]
        + [
            shape_of(2 * planes, 3 * blocks, chunk, part),
            shape_of(2 * planes, chunk // 2, 2 * heads_width),
        ]
        + small_outs,
        in_specs=[SMEM] + [VMEM] * 6 + [ANY] * 10,
        out_specs=[ANY] * 22 + [VMEM] * 6,
        scratch_shapes=[vmem(*dims) for dims in states]
        + [
            vmem(3 * heads_width, width),
            vmem(heads_width, width),
            vmem(blocks, width, inner),
            vmem(blocks, width, inner),
            vmem(blocks, inner, width),
        ]
        + [vmem(seq_len, width), vmem(2, seq_len, width)]
        + [vmem(blocks, seq_len, half)] * 4
        + [vmem(seq_len, 8, dtype=f32)] * 2
        + [vmem(seq_len, width)] * 2
        + [vmem(peers, rows, width)] * 3
        + [vmem(rows, width, dtype=f32)] * 2
        + [
            vmem(blocks, 3, planes, chunk, part),
            vmem(blocks, 3, planes, chunk, part),
            vmem(2, planes, 3 * blocks, chunk, part),
            vmem(seq_len, width),
            vmem(seq_len, seq_len),
            vmem(seq_len, 3 * heads_width),
            vmem(width, 4 * heads_width),
            vmem(width, 2 * heads_width),
            vmem(2, 2, planes, chunk // 2, 2 * heads_width),
            vmem(2, planes, chunk // 2, 2 * heads_width),
        ]
        + [
            vmem(2, rows, width),
            vmem(2, rows, width, dtype=f32),
            vmem(2, 24, seq_len, dtype=f32),
            vmem(2, 24, seq_len, dtype=f32),
            vmem(2, 8, 128, dtype=f32),
            vmem(8, 128, dtype=f32),
            vmem(8, 128, dtype=f32),
            vmem(planes - 1, 8, 128, dtype=f32),
        ]
        + [
            vmem(rows, width),
            vmem(top, seq_len, dtype=jnp.int32),
            vmem(1, width, dtype=f32),
            vmem(1, width, dtype=f32),
            vmem(*router_t.shape),
            vmem(2, rows, width),
        ]
        + [
            vmem(3, 8, width + 128, dtype=f32),
            vmem(peers, 8, width + 128, dtype=f32),
            vmem(planes - 1, 8, width + 128, dtype=f32),
            vmem(1, width, dtype=f32),
        ]
        + [dma((2, 4, peers))] * 2
        + [dma((2, 2 * chunks, peers))] * 2
        + [dma((2, 2, chunks, peers))] * 2
        + [dma((chunks, peers))] * 2
        + [dma((15,))] * 2
        + [dma((2, 2))] * 2
        + [dma((2, ranks))] * 2
        + [dma((planes - 1,))] * 2
        + [dma] * 4
        + [dma((blocks,))] * 2
        + [dma((2, planes)), dma((2 * planes,)), dma((2,))]
        + [dma((2,))] * 2
        + [dma((2, planes)), dma((2 * planes,)), dma((2,))]
        + [dma((2,))] * 2
        + [dma] * 4
        + [dma((peers,))] * 2
        + [dma((planes - 1,))] * 2
        + [dma((N_FFN,)), dma((N_ATTN,)), dma((10,))],
        compiler_params=params(0),
        name="forward_backward",
    )(lengths, boundary[0], routes_t, attn_gain, ffn_gain, router_t, tables, *weights)
    land, land_z, *small_results = result[20:]

    def whole(shape):
        return pl.BlockSpec(shape, lambda e: (0,) * len(shape))

    routed = shape_of(experts, chunk, inner, dtype=f32)
    common = shape_of(chunk, inner, dtype=f32)
    square = shape_of(chunk, heads_width, dtype=f32)
    turned = shape_of(heads_width, chunk, dtype=f32)
    last = experts - 1
    done = pl.pallas_call(
        functools.partial(finish_kernel, planes),
        grid=(blocks,),
        out_shape=small_outs + [routed] * 3 + [common] * 3 + [square] * 3 + [turned],
        in_specs=[
            pl.BlockSpec((2 * planes, 3, chunk, part), lambda e: (0, e, 0, 0)),
            whole(land_z.shape),
        ]
        + [whole(o.shape) for o in small_outs],
        out_specs=[whole(o.shape) for o in small_outs]
        + [pl.BlockSpec((1, chunk, inner), lambda e: (jnp.minimum(e, last), 0, 0))] * 3
        + [whole(common.shape)] * 3
        + [whole(square.shape)] * 3
        + [whole(turned.shape)],
        compiler_params=pltpu.CompilerParams(vmem_limit_bytes=VMEM_LIMIT),
        name="finish",
    )(land, land_z, *small_results)
    (out_rows, in_grads, g_gain_a, g_gain_f, g_router, balance), done = done[:6], done[6:]
    g_eg, g_eu, g_ed, g_sg, g_su, g_sd, g_q, g_k, g_v, g_o = done
    return (
        out_rows[None],
        in_grads[None],
        g_gain_a,
        g_q[None],
        g_k[None],
        g_v[None],
        g_o[None],
        g_gain_f,
        g_router.T[None],
        g_eg[None],
        g_eu[None],
        jnp.swapaxes(g_ed, 1, 2)[None],
        g_sg[None],
        g_su[None],
        g_sd.T[None],
        balance.reshape(1),
    )


def solution(mesh):
    placed = (
        P("section", "dp", "tensor", None),
        P("dp"),
        P("section", "dp", None, None),
        P("section", None),
        P("section", None, "tensor"),
        P("section", None, "tensor"),
        P("section", None, "tensor"),
        P("section", "tensor", None),
        P("section", None),
        P("section", None, None),
        P("section", None, None, "tensor"),
        P("section", None, None, "tensor"),
        P("section", None, "tensor", None),
        P("section", None, "tensor"),
        P("section", None, "tensor"),
        P("section", "tensor", None),
    )
    return jax.shard_map(
        functools.partial(on_device, mesh.shape["tensor"], mesh.shape["dp"]),
        mesh=mesh,
        in_specs=placed,
        out_specs=(
            P("section", "dp", "tensor", None),
            P("section", "dp", "tensor", None),
            P("section", None),
            P("section", "dp", "tensor"),
            P("section", "dp", "tensor"),
            P("section", "dp", "tensor"),
            P("section", "tensor", "dp"),
            P("section", None),
            P("section", None, None),
            P("section", None, "dp", "tensor"),
            P("section", None, "dp", "tensor"),
            P("section", None, "tensor", "dp"),
            P("section", "dp", "tensor"),
            P("section", "dp", "tensor"),
            P("section", "tensor", "dp"),
            P("section"),
        ),
        check_vma=False,
    )
```

```python
import functools

import jax
import jax.numpy as jnp
import numpy as np
from jax import lax
from jax.experimental import pallas as pl
from jax.experimental.pallas import tpu as pltpu
from jax.sharding import PartitionSpec as P

HEAD_DIM = 64
HALF_DIM = HEAD_DIM // 2
EPSILON = 1e-06
ALPHA = 0.01
THETA = 10000.0
MASKED = -1e30
LANES = 256
VMEM_LIMIT = 63 * 2**20 + 2**19

f32 = jnp.float32
bf16 = jnp.bfloat16
MESH = pl.DeviceIdType.MESH
ANY = pl.BlockSpec(memory_space=pl.ANY)
VMEM = pl.BlockSpec(memory_space=pltpu.VMEM)
SMEM = pl.BlockSpec(memory_space=pltpu.SMEM)


def dot(left, right, left_dim, right_dim):
    return lax.dot_general(
        left, right, (((left_dim,), (right_dim,)), ((), ())), preferred_element_type=f32
    )


def rope_tables(seq_len):
    frequency = (THETA ** (-np.arange(HALF_DIM, dtype=np.float32) / HALF_DIM)).astype(np.float32)
    angles = np.arange(seq_len, dtype=np.float32)[:, None] * frequency[None, :]
    cosine, sine = np.cos(angles), np.sin(angles)
    return np.concatenate([cosine, cosine, -sine, sine], axis=-1).astype(np.float32)


def turn_halves(values):
    return jnp.concatenate([values[:, HALF_DIM:], values[:, :HALF_DIM]], axis=1)


class Place:
    def __init__(self, ranks, planes):
        self.s = lax.axis_index("section")
        self.t = lax.axis_index("tensor")
        self.z = lax.axis_index("dp")
        self.ranks, self.planes = ranks, planes
        self.odd = lax.rem(self.z, 2)
        self.sibling = (1 - self.s, self.t, self.z)
        self.partner = (self.s, self.t, self.z + 1 - 2 * self.odd)

    def peer(self, k):
        return lax.rem(self.t + k, self.ranks)

    def peer_id(self, k):
        return (self.s, self.peer(k), self.z)

    def plane_id(self, k):
        return (self.s, self.t, lax.rem(self.z + k, self.planes))

    def greet(self):
        barrier = pltpu.get_barrier_semaphore()
        others = [self.sibling] + [self.peer_id(k) for k in range(1, self.ranks)]
        for k in range(1, self.planes):
            _, t, z = self.plane_id(k)
            others += [(self.s, t, z), (1 - self.s, t, z)]
        for other in others:
            pl.semaphore_signal(barrier, inc=1, device_id=other, device_id_type=MESH)
        pl.semaphore_wait(barrier, len(others))


def remote(src, dst, send, recv, device):
    return pltpu.make_async_remote_copy(
        src_ref=src, dst_ref=dst, send_sem=send, recv_sem=recv, device_id=device, device_id_type=MESH
    )


def gather_rows(place, full, rows, send, recv):
    mine = full.at[pl.ds(place.t * rows, rows)]
    copies = []
    for k in range(1, place.ranks):
        copy = remote(mine, mine, send.at[k - 1], recv.at[k - 1], place.peer_id(k))
        copy.start()
        copies.append(copy)
    return copies


def scatter_block(place, stage, landing, rows, lo, width, send, recv):
    copies = []
    for k in range(1, place.ranks):
        src = stage.at[pl.ds(place.peer(k) * rows, rows), pl.ds(lo, width)]
        dst = landing.at[k - 1, :, pl.ds(lo, width)]
        copy = remote(src, dst, send.at[k - 1], recv.at[k - 1], place.peer_id(k))
        copy.start()
        copies.append(copy)
    return copies


def landed_sum(own, landing, ranks):
    total = own
    for k in range(ranks - 1):
        total = total + landing[k].astype(f32)
    return total


def rms_rows(values, gain):
    return values * lax.rsqrt(jnp.mean(values * values, axis=-1, keepdims=True) + EPSILON) * gain


def rms_back(values, gain, grad):
    r = lax.rsqrt(jnp.mean(values * values, axis=-1, keepdims=True) + EPSILON)
    normed = values * r
    scaled = grad * gain
    inner = jnp.mean(scaled * normed, axis=-1, keepdims=True)
    return r * (scaled - normed * inner), jnp.sum(grad * normed, axis=0, keepdims=True)


def name_rows(routes):
    expert = lax.broadcasted_iota(jnp.int32, (8, routes.shape[1]), 0)
    named = routes[0:1] == expert
    for j in range(1, routes.shape[0]):
        named = named | (routes[j : j + 1] == expert)
    return named.astype(f32)


def column(matrix, index):
    lane = lax.broadcasted_iota(jnp.int32, matrix.shape, 1)
    return jnp.sum(jnp.where(lane == index, matrix, 0.0), axis=1, keepdims=True)


def load_choice(first, pairs, sems):
    for i, (own, other, dst) in enumerate(pairs):

        @pl.when(first)
        def _(own=own, dst=dst, i=i):
            pltpu.make_async_copy(own, dst, sems.at[i]).start()

        @pl.when(jnp.logical_not(first))
        def _(other=other, dst=dst, i=i):
            pltpu.make_async_copy(other, dst, sems.at[i]).start()

    return [pltpu.make_async_copy(own, dst, sems.at[i]) for i, (own, other, dst) in enumerate(pairs)]


N_ATTN = 4
N_FFN = 6
SENT_AT_ONCE = 3
GRADS_BY = ((2, 4), (1, 3))


def attn_targets(w_in, w_out, heads_width):
    return [w_in.at[pl.ds(i * heads_width, heads_width)] for i in range(3)] + [w_out]


def ffn_targets(wg, wu, wd):
    experts = wg.shape[0] - 1
    first = pl.ds(0, experts)
    return [wg.at[first], wu.at[first], wd.at[first], wg.at[experts], wu.at[experts], wd.at[experts]]


def both_kernel(ranks, planes, top, *refs):
    (lens, bnd, routes, gain_a_own, gain_f_own, router, tables), refs = refs[:7], refs[7:]
    own, refs = refs[:10], refs[10:]
    other, refs = refs[:10], refs[10:]
    (nf_o, q_o, k_o, v_o, p_o, mx_o, hf_o, g_o, u_o, hp_o, land, land_z), refs = refs[:12], refs[12:]
    (out_rows, in_grads, gain_a_out, gain_f_out, router_out, balance), refs = refs[:6], refs[6:]
    (nf, qs, ks, vs, ps, mx, hf, gs, us, hp), refs = refs[:10], refs[10:]
    (w_in, wo, wg, wu, wd), refs = refs[:5], refs[5:]
    (dyf, dyp, acts, gp, up, ap, coef, gate_sum), refs = refs[:8], refs[8:]
    (stage, stage_y, land_a, land_f, land_y, row_buf, d_mid), refs = refs[:7], refs[7:]
    (sent, got, quarter, df, ds, dqkv, gw, got_a, half_a, pair_in), refs = refs[:10], refs[10:]
    (xs, mid, small, o_small, probs_sum, cnt, o_cnt, cnt_in), refs = refs[:8], refs[8:]
    (o_bnd, o_routes, o_gain_a, o_gain_f, o_router, y_low), refs = refs[:6], refs[6:]
    (packs, pack_t, pack_z, gain_now), refs = refs[:4], refs[4:]
    (ag_s, ag_r, rsa_s, rsa_r, rsf_s, rsf_r, rsy_s, rsy_r, ex_s, ex_r), refs = refs[:10], refs[10:]
    (hp_s, hp_r, hq_s, hq_r, dp_s, dp_r, cz_s, cz_r, cs_s, cs_r, row_s, row_r), refs = refs[:12], refs[12:]
    (sw_s, sw_r, zs, zr, zl, as_s, as_r, az_s, az_r, az_l), refs = refs[:10], refs[10:]
    (pr_s, pr_r, gr_s, gr_r, pk_s, pk_r, pt_s, pt_r, pz_s, pz_r, ffn_sem, attn_sem, save_sem) = refs

    place = Place(ranks, planes)
    s, t, z, odd = place.s, place.t, place.z, place.odd
    rows, width = bnd.shape[1], bnd.shape[2]
    seq_len = hf.shape[0]
    experts = wg.shape[0] - 1
    blocks = experts + 1
    inner = wg.shape[2]
    half = inner // 2
    part = half // 2
    heads = qs.shape[0]
    heads_width = heads * HEAD_DIM
    chunk = width // planes
    chunks = width // LANES
    mine = pl.ds(t * rows, rows)
    my_lanes = pl.ds(pl.multiple_of(odd * half, half), half)
    far_lanes = pl.ds(pl.multiple_of((1 - odd) * half, half), half)
    slot = s * planes + z
    scale = HEAD_DIM ** (-0.5)

    def ffn_weights(l):
        targets = ffn_targets(wg, wu, wd)
        return load_choice(s == l, [(own[4 + i], other[4 + i], targets[i]) for i in range(N_FFN)], ffn_sem)

    def attn_weights(l):
        targets = attn_targets(w_in, wo, heads_width)
        return load_choice(s == l, [(own[i], other[i], targets[i]) for i in range(N_ATTN)], attn_sem)

    ffn_state = [(gs, g_o), (us, u_o), (hf, hf_o), (hp, hp_o)]
    attn_state = [(nf, nf_o), (qs, q_o), (ks, k_o), (vs, v_o), (ps, p_o), (mx, mx_o)]

    def moves(pairs, first, back):
        copies = []
        for i, (inside, outside) in enumerate(pairs):
            src, dst = (outside, inside) if back else (inside, outside)
            copies.append(pltpu.make_async_copy(src, dst, save_sem.at[first + i]))
        return copies

    def begin(copies):
        for copy in copies:
            copy.start()
        return copies

    def finish_all(copies):
        for copy in copies:
            copy.wait()

    class RelayGather:
        def __init__(self, full, send, recv):
            near = t + 1 - 2 * lax.rem(t, 2)
            far = lax.rem(t + 2, ranks)
            side = rows // 2

            def copy(owner, upper, at, to):
                piece = full.at[pl.ds(owner * rows + upper * side, side)]
                return remote(piece, piece, send.at[at], recv.at[at], (s, to, z))

            self.near, self.far = near, far
            self.diagonal = lax.rem(near + 2, ranks)
            self.first = [copy(t, 0, 0, near), copy(t, 1, 2, far), copy(t, 1, 1, near), copy(t, 0, 3, far)]
            self.relays = [copy(near, 0, 4, far), copy(far, 1, 5, near)]
            begin(self.first)

        def wait(self, arrived=lambda rank: None):
            for copy, relay in zip(self.first[:2], self.relays):
                copy.wait_recv()
                relay.start()
            for copy, rank in zip(self.first[2:], (self.near, self.far)):
                copy.wait_recv()
                arrived(rank)
            for relay in self.relays:
                relay.wait_recv()
            arrived(self.diagonal)
            for copy in self.first + self.relays:
                copy.wait_send()

    def gather_now(full, send, recv):
        if ranks == 4:
            return [RelayGather(full, send, recv)]
        return gather_rows(place, full, rows, send, recv)

    def gain_of(l, mine_ref, other_ref):
        return jnp.where(s == l, mine_ref[...], other_ref[...])

    def route_weights(l):
        value = jnp.where(s == l, router[...], o_router[...]).astype(f32)
        if experts < 8:
            value = jnp.concatenate([value, jnp.zeros((8 - experts, width), f32)], axis=0)
        return value.astype(bf16)

    def to_owner(l, src, dst, send, recv, local):
        for c in range(planes):
            own_copy = (z == c) & (s == l)

            @pl.when(own_copy)
            def _(c=c):
                pltpu.make_async_copy(src(c), dst, local).start()

            @pl.when(jnp.logical_not(own_copy))
            def _(c=c):
                remote(src(c), dst, send.at[c], recv.at[slot], (l, t, c)).start()

    def sent_to_owner(l, whole, dst, send, recv, local):
        for c in range(planes):
            own_copy = (z == c) & (s == l)

            @pl.when(own_copy)
            def _(c=c):
                pltpu.make_async_copy(whole.at[c], dst.at[slot], local).wait()

            @pl.when(jnp.logical_not(own_copy))
            def _(c=c):
                remote(whole.at[c], dst.at[slot], send.at[c], recv.at[slot], (l, t, c)).wait_send()

    def arrived(dst, send, recv):
        for source in range(2 * planes):

            @pl.when(source != slot)
            def _(source=source):
                remote(
                    dst.at[source], dst.at[source], send.at[0], recv.at[source], place.sibling
                ).wait_recv()

    def scatter_product(product, staged, landing, send, recv):
        copies = []
        for n in range(chunks):
            lanes = slice(n * LANES, (n + 1) * LANES)
            staged[:, lanes] = product(lanes).astype(bf16)
            copies += scatter_block(
                place, staged, landing, rows, n * LANES, LANES, send.at[n], recv.at[n]
            )
        return copies

    def share_of(l):
        return remote(half_a.at[l, 1 - odd], pair_in.at[l], pr_s.at[l], pr_r.at[l], place.partner)

    side = 2 * heads_width

    def swap_half(l):
        theirs = pl.ds(pl.multiple_of((1 - s) * side, 128), side)
        return remote(gw.at[:, theirs], got_a, as_s.at[l], as_r.at[l], place.sibling)

    def share_half(l):
        swap_half(l).wait()
        ours = pl.ds(pl.multiple_of(s * side, 128), side)
        kept = (gw[:, ours].astype(f32) + got_a[...].astype(f32)).astype(bf16)
        for side_b in range(2):
            for c in range(planes):
                lo = c * chunk + side_b * (chunk // 2)
                half_a[l, side_b, c] = kept[lo : lo + chunk // 2]
        share_of(l).start()

    def send_half(l):
        share_of(l).wait()
        half_a[l, odd] = (half_a[l, odd].astype(f32) + pair_in[l].astype(f32)).astype(bf16)
        to_owner(l, lambda c: half_a.at[l, odd, c], land_z.at[slot], az_s.at[l], az_r, az_l.at[l])

    def forward_chunks(gathering, full, landing, send, recv):
        copies = begin([remote(full.at[mine], landing.at[mine], send.at[0], recv.at[0], place.partner)])

        def onward(rank):
            they = pl.ds(rank * rows, rows)
            at = len(copies)
            copies.extend(
                begin([remote(full.at[they], landing.at[they], send.at[at], recv.at[at], place.partner)])
            )

        if ranks == 4:
            gathering[0].wait(onward)
        else:
            for k, copy in enumerate(gathering, 1):
                copy.wait()
                onward(place.peer(ranks - k))
        return copies

    place.greet()
    first_w = 5
    ex_pairs = [
        (bnd.at[1 - s], o_bnd),
        (gain_a_own, o_gain_a),
        (gain_f_own, o_gain_f),
        (router, o_router),
        (routes.at[1 - s], o_routes),
    ] + [(own[i], other[i]) for i in range(10)]
    exchange = [
        remote(src, dst, ex_s.at[i], ex_r.at[i], place.sibling) for i, (src, dst) in enumerate(ex_pairs)
    ]
    begin(exchange)
    row8 = lax.broadcasted_iota(jnp.int32, (8, seq_len), 0)
    token8 = lax.broadcasted_iota(jnp.int32, (8, seq_len), 1)
    length = lens[s]
    cosine, signed = tables[:, :HEAD_DIM], tables[:, HEAD_DIM:]

    def attn_begin(l):
        if l == 0:

            @pl.when(s == 0)
            def _():
                gain_now[...] = gain_a_own[...]

            @pl.when(s != 0)
            def _():
                gain_now[...] = o_gain_a[...]

        else:
            gain_now[...] = gain_of(l, gain_a_own, o_gain_a)
        nf[mine] = rms_rows(xs[l].astype(f32), gain_now[...]).astype(bf16)
        return gather_now(nf, ag_s.at[l, 0], ag_r.at[l, 0])

    def attn_forward(l, gathering, loads, between):
        finish_all(loads)
        finish_all(gathering)
        between()
        projected = dot(nf[...], w_in[...], 1, 1)
        for j, dst in enumerate((qs, ks, vs)):
            for h in range(heads):
                at = j * heads_width + h * HEAD_DIM
                piece = projected[:, at : at + HEAD_DIM]
                if j < 2:
                    piece = piece * cosine + turn_halves(piece) * signed
                dst[h] = piece.astype(bf16)
        place_q = lax.broadcasted_iota(jnp.int32, (seq_len, seq_len), 0)
        place_k = lax.broadcasted_iota(jnp.int32, (seq_len, seq_len), 1)
        allowed = (place_k <= place_q) & (place_k < length)
        for h in range(heads):
            scores = dot(qs[h], ks[h], 1, 1) * scale
            scores = jnp.where(allowed, scores, MASKED)
            peak = jnp.max(scores, axis=-1, keepdims=True)
            raised = jnp.exp(scores - peak)
            total = jnp.sum(raised, axis=-1, keepdims=True)
            weights = (raised / total).astype(bf16)
            ps[h] = weights
            mx[:, h * HEAD_DIM : (h + 1) * HEAD_DIM] = dot(weights, vs[h], 1, 0).astype(bf16)
        return scatter_product(
            lambda lanes: dot(mx[...], wo[:, lanes], 1, 0),
            stage,
            land_a,
            rsa_s.at[l, pl.ds(0, chunks)],
            rsa_r.at[l, pl.ds(0, chunks)],
        )

    def attn_finish(l, scattering):
        finish_all(scattering)
        middle = xs[l].astype(f32) + landed_sum(stage[mine].astype(f32), land_a, ranks)
        mid[l] = middle
        hf[mine] = rms_rows(middle, gain_of(l, gain_f_own, o_gain_f)).astype(bf16)
        return gather_now(hf, ag_s.at[l, 1], ag_r.at[l, 1])

    def route(l):
        names = name_rows(jnp.where(s == l, routes[s], o_routes[...]))
        logits = dot(route_weights(l), hf[...], 1, 1)
        logits = jnp.where(row8 < experts, logits, MASKED)
        raised = jnp.exp(logits - jnp.max(logits, axis=0, keepdims=True))
        raised = jnp.where(row8 < experts, raised, 0.0)
        chances = raised / jnp.sum(raised, axis=0, keepdims=True)
        per_chosen = names / jnp.sum(chances * names, axis=0, keepdims=True)
        gates = chances * per_chosen
        small[l, 0:8] = chances
        small[l, 8:16] = gates
        small[l, 16:24] = per_chosen
        remote(small.at[l], o_small.at[l], hp_s.at[l, 1], hp_r.at[l, 1], place.partner).start()
        summed = jnp.sum(jnp.where(token8 < length, chances, 0.0), axis=1, keepdims=True)
        probs_sum[l] = jnp.broadcast_to(summed, (8, 128))
        coef[...] = jnp.where(row8 == experts, 1.0, gates).T

    def split_acts(e, value):
        low, high = value[:, :half], value[:, half:]
        acts[e] = jnp.where(odd == 0, low, high).astype(bf16)
        gp[e] = jnp.where(odd == 0, high, low).astype(bf16)

    def branch_product(lanes):
        total = dot(acts[0], wd[0, my_lanes, lanes], 1, 0) + dot(gp[0], wd[0, far_lanes, lanes], 1, 0)
        for e in range(1, blocks):
            total = total + dot(acts[e], wd[e, my_lanes, lanes], 1, 0)
            total = total + dot(gp[e], wd[e, far_lanes, lanes], 1, 0)
        return total

    def output_rows(l, landing, staged):
        output = mid[l] + landed_sum(staged[mine].astype(f32), landing, ranks)
        y_low[l] = output.astype(bf16)

        @pl.when(s == l)
        def _():
            out_rows[s] = y_low[l]

        @pl.when(s != l)
        def _():
            remote(y_low.at[l], out_rows.at[s], row_s, row_r, place.sibling).start()

    @pl.when(s == 0)
    def _():
        xs[0] = bnd[0]

    @pl.when(s != 0)
    def _():
        finish_all(exchange[:first_w])
        xs[0] = o_bnd[...]

    gathering = attn_begin(0)

    @pl.when(s != 0)
    def _():
        for copy in exchange[first_w : first_w + N_ATTN]:
            copy.wait_recv()

    loads = attn_weights(0)
    counted = jnp.zeros((8, 1), f32)
    for q in range(2):
        live = jnp.where(token8 < lens[q], 1.0, 0.0)
        counts = jnp.where(row8 == 7, live, name_rows(routes[q]) * live)
        counted = counted + jnp.sum(counts, axis=1, keepdims=True)
    cnt[...] = jnp.broadcast_to(counted, cnt.shape)
    count_copies = begin(
        [
            remote(cnt, cnt_in.at[k - 1], cz_s.at[k - 1], cz_r.at[k - 1], place.plane_id(k))
            for k in range(1, planes)
        ]
    )

    @pl.when(s == 0)
    def _():
        finish_all(exchange[:first_w])

    cotangent = jnp.where(s == 0, o_bnd[...], bnd[1]).astype(f32)
    position = lax.broadcasted_iota(jnp.int32, (rows, width), 0) + t * rows
    dyf[mine] = jnp.where(position < length, cotangent, 0.0).astype(bf16)
    cot_gather = []

    def gather_cotangent():
        cot_gather.extend(gather_rows(place, dyf, rows, ag_s.at[1, 2], ag_r.at[1, 2]))

    scattering = attn_forward(0, gathering, loads, gather_cotangent)

    @pl.when(s != 0)
    def _():
        for copy in exchange[first_w + N_ATTN :]:
            copy.wait_recv()

    ffn_loads = ffn_weights(0)
    attn_saves = begin(moves(attn_state, 4, False))
    gathering = attn_finish(0, scattering)

    @pl.when(s == 0)
    def _():
        for copy in exchange[first_w : first_w + N_ATTN]:
            copy.wait_recv()

    attn_w = attn_weights(1)
    finish_all(count_copies)
    total = cnt[...]
    for k in range(planes - 1):
        total = total + cnt_in[k]
    cnt[...] = total
    share_counts = remote(cnt, o_cnt, cs_s, cs_r, place.sibling)
    share_counts.start()
    finish_all(ffn_loads)
    finish_all(gathering)
    ffn_saves = begin(moves(ffn_state[2:3], 2, False))
    hidden_sent = [remote(hf, hp_o, hp_s.at[0, 0], hp_r.at[0, 0], place.partner)]
    begin(hidden_sent)
    route(0)

    def forward_expert(e, carry):
        gate_h = dot(hf[...], wg[e], 1, 0)
        up_h = dot(hf[...], wu[e], 1, 0)
        gs[e] = gate_h.astype(bf16)
        us[e] = up_h.astype(bf16)
        split_acts(e, gate_h * jax.nn.sigmoid(gate_h) * up_h * column(coef[...], e))
        return carry

    lax.fori_loop(0, blocks, forward_expert, 0)
    ffn_saves += begin(moves(ffn_state[:2], 0, False))
    finish_all(attn_saves)
    scat = scatter_product(branch_product, stage, land_f, rsf_s.at[0, 0], rsf_r.at[0, 0])

    @pl.when(s == 0)
    def _():
        for copy in exchange[first_w + N_ATTN :]:
            copy.wait_recv()

    ffn_loads = ffn_weights(1)
    finish_all(cot_gather)
    cot_sent = remote(dyf, dyp.at[1], dp_s.at[1, 0], dp_r.at[1, 0], place.partner)
    cot_sent.start()
    finish_all(scat)
    output_rows(0, land_f, stage)
    xs[1] = y_low[0]

    gathering = attn_begin(1)
    finish_all(hidden_sent)
    finish_all(ffn_saves)
    scattering = attn_forward(1, gathering, attn_w, lambda: None)
    gathering = attn_finish(1, scattering)
    hidden_sent = forward_chunks(gathering, hf, hp, hq_s, hq_r)
    finish_all(ffn_loads)
    route(1)
    gate_sum[...] = jnp.zeros_like(gate_sum)
    lane8 = lax.broadcasted_iota(jnp.int32, gate_sum.shape, 1)

    def expert_grads(e, gate_h, up_h, raw):
        sig = jax.nn.sigmoid(gate_h)
        silu = gate_h * sig
        acted = silu * up_h
        inner_sum = jnp.sum(acted * raw, axis=1, keepdims=True)
        gate_sum[...] = jnp.where(lane8 == e, inner_sum, gate_sum[...])
        weight = column(coef[...], e)
        d_acted = raw * weight
        gs[e] = (d_acted * up_h * (sig + silu * (1.0 - sig))).astype(bf16)
        us[e] = (d_acted * silu).astype(bf16)
        return acted * weight

    def both_expert(e, carry):
        gate_h = dot(hf[...], wg[e], 1, 0)
        up_h = dot(hf[...], wu[e], 1, 0)
        raw = dot(dyf[...], wd[e], 1, 1)
        split_acts(e, expert_grads(e, gate_h, up_h, raw))
        return carry

    def back_expert(e, carry):
        raw = dot(dyf[...], wd[e], 1, 1)
        value = expert_grads(e, gs[e].astype(f32), us[e].astype(f32), raw)
        acts[e] = jnp.where(odd == 0, value[:, :half], value[:, half:]).astype(bf16)
        return carry

    lax.fori_loop(0, blocks, both_expert, 0)
    share_counts.wait()
    y_scat = []

    for l in (1, 0):
        here = s == l
        if l == 0:
            finish_all(ffn_loads)
            finish_all(ffn_back)
            coef[...] = jnp.where(row8 == experts, 1.0, small[l, 8:16]).T
            gate_sum[...] = jnp.zeros_like(gate_sum)
            to_partner = forward_chunks(gathering, dyf, dyp.at[l], dp_s.at[l], dp_r.at[l])
            share_half(1)
            for e in range(SENT_AT_ONCE, blocks):
                send_later(e)
            lax.fori_loop(0, blocks, back_expert, 0)
        else:
            to_partner = [cot_sent]
        if l == 1:
            y_scat = scatter_product(branch_product, stage_y, land_y, rsy_s, rsy_r)
        finish_all(to_partner)
        if l == 1:
            finish_all(hidden_sent)
        remote(small.at[l], o_small.at[l], hp_s.at[l, 1], hp_r.at[l, 1], place.partner).wait()
        coef[...] = jnp.where(row8 == experts, 1.0, o_small[l, 8:16]).T

        def partner_expert(e, carry, l=l):
            gate_h = dot(hp[...], wg[e, :, my_lanes], 1, 0)
            up_h = dot(hp[...], wu[e, :, my_lanes], 1, 0)
            raw = dot(dyp[l], wd[e, my_lanes], 1, 1)
            sig = jax.nn.sigmoid(gate_h)
            silu = gate_h * sig
            weight = column(coef[...], e)
            ap[e] = (silu * up_h * weight).astype(bf16)
            d_acted = raw * weight
            gp[e] = (d_acted * up_h * (sig + silu * (1.0 - sig))).astype(bf16)
            up[e] = (d_acted * silu).astype(bf16)
            return carry

        lax.fori_loop(0, blocks, partner_expert, 0)
        def swap_of(e, l=l):
            return remote(sent.at[e], got.at[e], sw_s.at[e], sw_r.at[e], place.sibling)

        def send_grads(e, l=l):
            three = pl.ds(e * 3, 3)
            to_owner(l, lambda c: quarter.at[l, c, three], land.at[slot, three], zs.at[l], zr, zl.at[l])

        def finish(e, l=l, send_grads=send_grads):
            swap_of(e).wait()
            for j in range(3):
                at = e * 3 + j
                for c in range(planes):
                    quarter[l, c, at] = (
                        quarter[l, c, at].astype(f32) + got[e, j, c].astype(f32)
                    ).astype(bf16)

            @pl.when(jnp.logical_or(l == 0, e < SENT_AT_ONCE))
            def _():
                send_grads(e)

        def weight_grads(e, carry, l=l, finish=finish):
            sources = ((hf, gs, hp, gp), (hf, us, hp, up))
            for j in range(3):
                if j < 2:
                    left, right, left_p, right_p = sources[j]
                    value = dot(left[...], right[e, :, my_lanes], 0, 0) + dot(left_p[...], right_p[e], 0, 0)
                else:
                    value = dot(dyf[...], acts[e], 0, 0) + dot(dyp[l], ap[e], 0, 0)
                low, high = value[:, :part], value[:, part:]
                kept = jnp.where(s == 0, low, high).astype(bf16)
                given = jnp.where(s == 0, high, low).astype(bf16)
                for c in range(planes):
                    quarter[l, c, e * 3 + j] = kept[c * chunk : (c + 1) * chunk]
                    sent[e, j, c] = given[c * chunk : (c + 1) * chunk]
            swap_of(e).start()

            @pl.when(e > 0)
            def _():
                finish(e - 1)

            return carry

        early, middle = GRADS_BY[l]
        if l == 1:
            send_later = send_grads
        lax.fori_loop(0, early, weight_grads, 0)
        chances, gates, per_chosen = small[l, 0:8], small[l, 8:16], small[l, 16:24]
        totals = jnp.where(here, cnt[...], o_cnt[...])
        tokens_all = totals[7:8, 0:1]
        share = totals[:, 0:1] / (top * tokens_all)
        aux = jnp.where((token8 < length) & (t == 0), ALPHA * experts * share / tokens_all, 0.0)
        d_gates = gate_sum[...].T
        common = jnp.sum(d_gates * gates, axis=0, keepdims=True)
        d_chances = per_chosen * (d_gates - common) + aux
        d_logits = chances * (d_chances - jnp.sum(chances * d_chances, axis=0, keepdims=True))
        d_logits = d_logits.astype(bf16)
        router_grad = dot(d_logits, hf[...], 1, 0)
        route_w = route_weights(l)

        def hidden_product(lanes, d_logits=d_logits, route_w=route_w):
            total = dot(d_logits, route_w[:, lanes], 0, 0)
            for e in range(blocks):
                total = total + dot(gs[e], wg[e, lanes], 1, 1)
                total = total + dot(us[e], wu[e, lanes], 1, 1)
            return total

        scat = scatter_product(hidden_product, stage, land_f, rsf_s.at[l, 1], rsf_r.at[l, 1])
        lax.fori_loop(early, middle, weight_grads, 0)
        finish_all(scat)
        d_hidden = landed_sum(stage[mine].astype(f32), land_f, ranks)
        d_norm, gain_f_grad = rms_back(mid[l], gain_of(l, gain_f_own, o_gain_f), d_hidden)
        d_mid[...] = dyf[mine].astype(f32) + d_norm
        df[mine] = d_mid[...].astype(bf16)
        gathering = gather_rows(place, df, rows, ag_s.at[l, 3], ag_r.at[l, 3])

        if l == 0:
            send_half(1)
        lax.fori_loop(middle, blocks, weight_grads, 0)
        finish(blocks - 1)
        if l == 1:
            ffn_loads = ffn_weights(0)
            ffn_back = begin(moves(ffn_state, 0, True))
        else:
            finish_all(attn_w)
            finish_all(attn_back)
        finish_all(gathering)
        for h in range(heads):
            span = slice(h * HEAD_DIM, (h + 1) * HEAD_DIM)
            d_mixed = dot(df[...], wo[span], 1, 1).astype(bf16)
            for lo in range(0, seq_len, LANES):
                reach = lo + LANES
                weights = ps[h, lo:reach, 0:reach].astype(f32)
                d_probs = dot(d_mixed[lo:reach], vs[h, 0:reach], 1, 1)
                total = jnp.sum(weights * d_probs, axis=-1, keepdims=True)
                ds[lo:reach, 0:reach] = (weights * (d_probs - total)).astype(bf16)
                if reach < seq_len:
                    ds[lo:reach, reach:] = jnp.zeros((LANES, seq_len - reach), bf16)
            d_value = dot(ps[h], d_mixed, 0, 0)
            d_query = dot(ds[...], ks[h], 1, 0) * scale
            d_key = dot(ds[...], qs[h], 0, 0) * scale
            d_query = d_query * cosine - turn_halves(d_query) * signed
            d_key = d_key * cosine - turn_halves(d_key) * signed
            for j, value in enumerate((d_query, d_key, d_value)):
                at = j * heads_width + h * HEAD_DIM
                dqkv[:, at : at + HEAD_DIM] = value.astype(bf16)
        scat = scatter_product(
            lambda lanes: dot(dqkv[...], w_in[:, lanes], 1, 0), stage, land_a, rsa_s.at[l, pl.ds(chunks, chunks)], rsa_r.at[l, pl.ds(chunks, chunks)]
        )

        three_widths = 3 * heads_width
        gw[:, :three_widths] = dot(nf[...], dqkv[...], 0, 0).astype(bf16)
        gw[:, three_widths:] = dot(df[...], mx[...], 0, 0).astype(bf16)
        swap_half(l).start()
        finish_all(scat)
        d_normed = landed_sum(stage[mine].astype(f32), land_a, ranks)
        d_norm, gain_a_grad = rms_back(xs[l].astype(f32), gain_of(l, gain_a_own, o_gain_a), d_normed)
        dx = d_mid[...] + d_norm
        if l == 1:
            low_dx = dx.astype(bf16)
            dyf[mine] = low_dx
            gathering = gather_now(dyf, ag_s.at[0, 2], ag_r.at[0, 2])
            dx = low_dx.astype(f32)
            attn_w = attn_weights(0)
            attn_back = begin(moves(attn_state, 4, True))
            finish_all(y_scat)
            output_rows(1, land_y, stage_y)
        pack = jnp.concatenate(
            [
                jnp.concatenate([gain_a_grad, gain_f_grad, router_grad[:6]], axis=0),
                jnp.concatenate(
                    [jnp.zeros((2, 128), f32), jnp.where(t == 0, probs_sum[l, 0:6], 0.0)], axis=0
                ),
            ],
            axis=1,
        )

        @pl.when(here)
        def _(dx=dx, pack=pack):
            in_grads[s] = dx
            packs[0] = pack

        @pl.when(jnp.logical_not(here))
        def _(dx=dx, pack=pack):
            row_buf[...] = dx
            packs[1] = pack
            remote(row_buf, in_grads.at[s], gr_s, gr_r, place.sibling).start()
            remote(packs.at[1], packs.at[2], pk_s, pk_r, place.sibling).start()

    share_half(0)
    send_half(0)
    remote(packs.at[1], packs.at[2], pk_s, pk_r, place.sibling).wait()
    packs[0] = packs[0] + packs[2]
    finish_all(
        begin(
            [
                remote(packs.at[0], pack_t.at[k - 1], pt_s.at[k - 1], pt_r.at[k - 1], place.peer_id(k))
                for k in range(1, ranks)
            ]
        )
    )
    total = packs[0]
    for k in range(ranks - 1):
        total = total + pack_t[k]
    packs[0] = total
    finish_all(
        begin(
            [
                remote(packs.at[0], pack_z.at[k - 1], pz_s.at[k - 1], pz_r.at[k - 1], place.plane_id(k))
                for k in range(1, planes)
            ]
        )
    )
    total = packs[0]
    for k in range(planes - 1):
        total = total + pack_z[k]
    gain_a_out[...] = total[0:1, :width]
    gain_f_out[...] = total[1:2, :width]
    router_out[...] = total[2 : 2 + experts, :width]
    tokens_all = cnt[7:8, 0:1]
    products = cnt[0:experts, 0:1] / (top * tokens_all) * total[2 : 2 + experts, width : width + 1]
    balance[...] = experts * jnp.sum(products, axis=0, keepdims=True) / tokens_all

    for copy in exchange[first_w:]:
        copy.wait_send()
    remote(y_low.at[1 - s], out_rows.at[s], row_s, row_r, place.sibling).wait_send()
    remote(y_low.at[1 - s], out_rows.at[1 - s], row_s, row_r, place.sibling).wait_recv()
    remote(row_buf, in_grads.at[s], gr_s, gr_r, place.sibling).wait_send()
    remote(row_buf, in_grads.at[1 - s], gr_s, gr_r, place.sibling).wait_recv()
    for l in (1, 0):
        sent_to_owner(l, quarter.at[l], land, zs.at[l], zr, zl.at[l])
        sent_to_owner(l, half_a.at[l, odd], land_z, az_s.at[l], az_r, az_l.at[l])
    arrived(land, zs.at[0], zr)
    arrived(land_z, az_s.at[0], az_r)


def finish_kernel(planes, land, land_z, *refs):
    ins, outs, refs = refs[:6], refs[6:12], refs[12:]
    g_gate, g_up, g_down, s_gate, s_up, s_down, wq_out, wk_out, wv_out, wo_out = refs
    e = pl.program_id(0)
    experts = pl.num_programs(0) - 1
    part = land.shape[3]
    heads_width = wq_out.shape[1]
    for j, (routed, common) in enumerate(((g_gate, s_gate), (g_up, s_up), (g_down, s_down))):
        for core in range(2):
            for parity in range(2):
                value = land[core * planes + parity, j].astype(f32)
                for pair in range(1, planes // 2):
                    value = value + land[core * planes + 2 * pair + parity, j].astype(f32)
                lo = (2 * parity + core) * part

                @pl.when(e < experts)
                def _(value=value, lo=lo, routed=routed):
                    routed[0, :, lo : lo + part] = value

                @pl.when(e == experts)
                def _(value=value, lo=lo, common=common):
                    common[:, lo : lo + part] = value

    @pl.when(e == 1)
    def _():
        for src, dst in zip(ins, outs):
            dst[...] = src[...]
        sides = []
        for core in range(2):
            halves = []
            for parity in range(2):
                value = land_z[core * planes + parity].astype(f32)
                for pair in range(1, planes // 2):
                    value = value + land_z[core * planes + 2 * pair + parity].astype(f32)
                halves.append(value)
            sides.append(jnp.concatenate(halves, axis=0))
        wq_out[...] = sides[0][:, :heads_width]
        wk_out[...] = sides[0][:, heads_width:]
        wv_out[...] = sides[1][:, :heads_width]
        wo_out[...] = sides[1][:, heads_width:].T


def params(collective_id):
    return pltpu.CompilerParams(
        collective_id=collective_id, has_side_effects=True, vmem_limit_bytes=VMEM_LIMIT
    )


def shape_of(*dims, dtype=bf16):
    return jax.ShapeDtypeStruct(dims, dtype)


def on_device(ranks, planes, *args):
    (boundary, lengths, routes, attn_gain, w_query, w_key, w_value, w_out, ffn_gain, router) = args[:10]
    ffn_own = tuple(a[0] for a in args[10:])
    attn_own = (w_query[0].T, w_key[0].T, w_value[0].T, w_out[0])
    rows, width = boundary.shape[2:]
    seqs, seq_len = routes.shape[1:3]
    top = routes.shape[3]
    experts, _, inner = ffn_own[0].shape
    blocks = experts + 1
    heads_width = w_query.shape[2]
    heads = heads_width // HEAD_DIM
    chunks = width // LANES
    half, part = inner // 2, inner // 4
    chunk = width // planes
    peers = ranks - 1
    dma = pltpu.SemaphoreType.DMA

    def vmem(*dims, dtype=bf16):
        return pltpu.VMEM(dims, dtype)

    routes_t = jnp.swapaxes(routes[0], 1, 2)
    router_t = router[0].T
    tables = jnp.asarray(rope_tables(seq_len))
    head_shape = (heads, seq_len, HEAD_DIM)
    states = [
        (seq_len, width),
        head_shape,
        head_shape,
        head_shape,
        (heads, seq_len, seq_len),
        (seq_len, heads_width),
        (seq_len, width),
        (blocks, seq_len, inner),
        (blocks, seq_len, inner),
        (seq_len, width),
    ]
    weights = attn_own + ffn_own
    small_outs = [
        shape_of(2, rows, width),
        shape_of(seqs, rows, width, dtype=f32),
        shape_of(1, width, dtype=f32),
        shape_of(1, width, dtype=f32),
        shape_of(experts, width, dtype=f32),
        shape_of(1, 1, dtype=f32),
    ]
    result = pl.pallas_call(
        functools.partial(both_kernel, ranks, planes, top),
        out_shape=[shape_of(*w.shape) for w in weights]
        + [shape_of(*dims) for dims in states]
        + [
            shape_of(2 * planes, 3 * blocks, chunk, part),
            shape_of(2 * planes, chunk // 2, 2 * heads_width),
        ]
        + small_outs,
        in_specs=[SMEM] + [VMEM] * 6 + [ANY] * 10,
        out_specs=[ANY] * 22 + [VMEM] * 6,
        scratch_shapes=[vmem(*dims) for dims in states]
        + [
            vmem(3 * heads_width, width),
            vmem(heads_width, width),
            vmem(blocks, width, inner),
            vmem(blocks, width, inner),
            vmem(blocks, inner, width),
        ]
        + [vmem(seq_len, width), vmem(2, seq_len, width)]
        + [vmem(blocks, seq_len, half)] * 4
        + [vmem(seq_len, 8, dtype=f32)] * 2
        + [vmem(seq_len, width)] * 2
        + [vmem(peers, rows, width)] * 3
        + [vmem(rows, width, dtype=f32)] * 2
        + [
            vmem(blocks, 3, planes, chunk, part),
            vmem(blocks, 3, planes, chunk, part),
            vmem(2, planes, 3 * blocks, chunk, part),
            vmem(seq_len, width),
            vmem(seq_len, seq_len),
            vmem(seq_len, 3 * heads_width),
            vmem(width, 4 * heads_width),
            vmem(width, 2 * heads_width),
            vmem(2, 2, planes, chunk // 2, 2 * heads_width),
            vmem(2, planes, chunk // 2, 2 * heads_width),
        ]
        + [
            vmem(2, rows, width),
            vmem(2, rows, width, dtype=f32),
            vmem(2, 24, seq_len, dtype=f32),
            vmem(2, 24, seq_len, dtype=f32),
            vmem(2, 8, 128, dtype=f32),
            vmem(8, 128, dtype=f32),
            vmem(8, 128, dtype=f32),
            vmem(planes - 1, 8, 128, dtype=f32),
        ]
        + [
            vmem(rows, width),
            vmem(top, seq_len, dtype=jnp.int32),
            vmem(1, width, dtype=f32),
            vmem(1, width, dtype=f32),
            vmem(*router_t.shape),
            vmem(2, rows, width),
        ]
        + [
            vmem(3, 8, width + 128, dtype=f32),
            vmem(peers, 8, width + 128, dtype=f32),
            vmem(planes - 1, 8, width + 128, dtype=f32),
            vmem(1, width, dtype=f32),
        ]
        + [dma((2, 4, max(peers, 6)))] * 2
        + [dma((2, 2 * chunks, peers))] * 2
        + [dma((2, 2, chunks, peers))] * 2
        + [dma((chunks, peers))] * 2
        + [dma((15,))] * 2
        + [dma((2, 2))] * 2
        + [dma((ranks,))] * 2
        + [dma((2, ranks))] * 2
        + [dma((planes - 1,))] * 2
        + [dma] * 4
        + [dma((blocks,))] * 2
        + [dma((2, planes)), dma((2 * planes,)), dma((2,))]
        + [dma((2,))] * 2
        + [dma((2, planes)), dma((2 * planes,)), dma((2,))]
        + [dma((2,))] * 2
        + [dma] * 4
        + [dma((peers,))] * 2
        + [dma((planes - 1,))] * 2
        + [dma((N_FFN,)), dma((N_ATTN,)), dma((10,))],
        compiler_params=params(0),
        name="forward_backward",
    )(lengths, boundary[0], routes_t, attn_gain, ffn_gain, router_t, tables, *weights)
    land, land_z, *small_results = result[20:]

    def whole(shape):
        return pl.BlockSpec(shape, lambda e: (0,) * len(shape))

    routed = shape_of(experts, chunk, inner, dtype=f32)
    common = shape_of(chunk, inner, dtype=f32)
    square = shape_of(chunk, heads_width, dtype=f32)
    turned = shape_of(heads_width, chunk, dtype=f32)
    last = experts - 1
    done = pl.pallas_call(
        functools.partial(finish_kernel, planes),
        grid=(blocks,),
        out_shape=small_outs + [routed] * 3 + [common] * 3 + [square] * 3 + [turned],
        in_specs=[
            pl.BlockSpec((2 * planes, 3, chunk, part), lambda e: (0, e, 0, 0)),
            whole(land_z.shape),
        ]
        + [whole(o.shape) for o in small_outs],
        out_specs=[whole(o.shape) for o in small_outs]
        + [pl.BlockSpec((1, chunk, inner), lambda e: (jnp.minimum(e, last), 0, 0))] * 3
        + [whole(common.shape)] * 3
        + [whole(square.shape)] * 3
        + [whole(turned.shape)],
        compiler_params=pltpu.CompilerParams(vmem_limit_bytes=VMEM_LIMIT),
        name="finish",
    )(land, land_z, *small_results)
    (out_rows, in_grads, g_gain_a, g_gain_f, g_router, balance), done = done[:6], done[6:]
    g_eg, g_eu, g_ed, g_sg, g_su, g_sd, g_q, g_k, g_v, g_o = done
    return (
        out_rows[None],
        in_grads[None],
        g_gain_a,
        g_q[None],
        g_k[None],
        g_v[None],
        g_o[None],
        g_gain_f,
        g_router.T[None],
        g_eg[None],
        g_eu[None],
        jnp.swapaxes(g_ed, 1, 2)[None],
        g_sg[None],
        g_su[None],
        g_sd.T[None],
        balance.reshape(1),
    )


def solution(mesh):
    placed = (
        P("section", "dp", "tensor", None),
        P("dp"),
        P("section", "dp", None, None),
        P("section", None),
        P("section", None, "tensor"),
        P("section", None, "tensor"),
        P("section", None, "tensor"),
        P("section", "tensor", None),
        P("section", None),
        P("section", None, None),
        P("section", None, None, "tensor"),
        P("section", None, None, "tensor"),
        P("section", None, "tensor", None),
        P("section", None, "tensor"),
        P("section", None, "tensor"),
        P("section", "tensor", None),
    )
    return jax.shard_map(
        functools.partial(on_device, mesh.shape["tensor"], mesh.shape["dp"]),
        mesh=mesh,
        in_specs=placed,
        out_specs=(
            P("section", "dp", "tensor", None),
            P("section", "dp", "tensor", None),
            P("section", None),
            P("section", "dp", "tensor"),
            P("section", "dp", "tensor"),
            P("section", "dp", "tensor"),
            P("section", "tensor", "dp"),
            P("section", None),
            P("section", None, None),
            P("section", None, "dp", "tensor"),
            P("section", None, "dp", "tensor"),
            P("section", None, "tensor", "dp"),
            P("section", "dp", "tensor"),
            P("section", "dp", "tensor"),
            P("section", "tensor", "dp"),
            P("section"),
        ),
        check_vma=False,
    )
```

```python
import functools

import jax
import jax.numpy as jnp
import numpy as np
from jax import lax
from jax.experimental import pallas as pl
from jax.experimental.pallas import tpu as pltpu
from jax.sharding import PartitionSpec as P

HEAD_DIM = 64
HALF_DIM = HEAD_DIM // 2
EPSILON = 1e-06
ALPHA = 0.01
THETA = 10000.0
MASKED = -1e30
LANES = 256
VMEM_LIMIT = 63 * 2**20 + 2**19

f32 = jnp.float32
bf16 = jnp.bfloat16
MESH = pl.DeviceIdType.MESH
ANY = pl.BlockSpec(memory_space=pl.ANY)
VMEM = pl.BlockSpec(memory_space=pltpu.VMEM)
SMEM = pl.BlockSpec(memory_space=pltpu.SMEM)


def dot(left, right, left_dim, right_dim):
    return lax.dot_general(
        left, right, (((left_dim,), (right_dim,)), ((), ())), preferred_element_type=f32
    )


def rope_tables(seq_len):
    frequency = (THETA ** (-np.arange(HALF_DIM, dtype=np.float32) / HALF_DIM)).astype(np.float32)
    angles = np.arange(seq_len, dtype=np.float32)[:, None] * frequency[None, :]
    cosine, sine = np.cos(angles), np.sin(angles)
    return np.concatenate([cosine, cosine, -sine, sine], axis=-1).astype(np.float32)


def turn_halves(values):
    return jnp.concatenate([values[:, HALF_DIM:], values[:, :HALF_DIM]], axis=1)


class Place:
    def __init__(self, ranks, planes):
        self.s = lax.axis_index("section")
        self.t = lax.axis_index("tensor")
        self.z = lax.axis_index("dp")
        self.ranks, self.planes = ranks, planes
        self.odd = lax.rem(self.z, 2)
        self.sibling = (1 - self.s, self.t, self.z)
        self.partner = (self.s, self.t, self.z + 1 - 2 * self.odd)

    def peer(self, k):
        return lax.rem(self.t + k, self.ranks)

    def peer_id(self, k):
        return (self.s, self.peer(k), self.z)

    def plane_id(self, k):
        return (self.s, self.t, lax.rem(self.z + k, self.planes))

    def greet(self):
        barrier = pltpu.get_barrier_semaphore()
        others = [self.sibling] + [self.peer_id(k) for k in range(1, self.ranks)]
        for k in range(1, self.planes):
            _, t, z = self.plane_id(k)
            others += [(self.s, t, z), (1 - self.s, t, z)]
        for other in others:
            pl.semaphore_signal(barrier, inc=1, device_id=other, device_id_type=MESH)
        pl.semaphore_wait(barrier, len(others))


def remote(src, dst, send, recv, device):
    return pltpu.make_async_remote_copy(
        src_ref=src, dst_ref=dst, send_sem=send, recv_sem=recv, device_id=device, device_id_type=MESH
    )


def gather_rows(place, full, rows, send, recv):
    mine = full.at[pl.ds(place.t * rows, rows)]
    copies = []
    for k in range(1, place.ranks):
        copy = remote(mine, mine, send.at[k - 1], recv.at[k - 1], place.peer_id(k))
        copy.start()
        copies.append(copy)
    return copies


def scatter_block(place, stage, landing, rows, lo, width, send, recv):
    copies = []
    for k in range(1, place.ranks):
        src = stage.at[pl.ds(place.peer(k) * rows, rows), pl.ds(lo, width)]
        dst = landing.at[k - 1, :, pl.ds(lo, width)]
        copy = remote(src, dst, send.at[k - 1], recv.at[k - 1], place.peer_id(k))
        copy.start()
        copies.append(copy)
    return copies


def landed_sum(own, landing, ranks):
    total = own
    for k in range(ranks - 1):
        total = total + landing[k].astype(f32)
    return total


def rms_rows(values, gain):
    return values * lax.rsqrt(jnp.mean(values * values, axis=-1, keepdims=True) + EPSILON) * gain


def rms_back(values, gain, grad):
    r = lax.rsqrt(jnp.mean(values * values, axis=-1, keepdims=True) + EPSILON)
    normed = values * r
    scaled = grad * gain
    inner = jnp.mean(scaled * normed, axis=-1, keepdims=True)
    return r * (scaled - normed * inner), jnp.sum(grad * normed, axis=0, keepdims=True)


def name_rows(routes):
    expert = lax.broadcasted_iota(jnp.int32, (8, routes.shape[1]), 0)
    named = routes[0:1] == expert
    for j in range(1, routes.shape[0]):
        named = named | (routes[j : j + 1] == expert)
    return named.astype(f32)


def column(matrix, index):
    lane = lax.broadcasted_iota(jnp.int32, matrix.shape, 1)
    return jnp.sum(jnp.where(lane == index, matrix, 0.0), axis=1, keepdims=True)


def load_choice(first, pairs, sems):
    for i, (own, other, dst) in enumerate(pairs):

        @pl.when(first)
        def _(own=own, dst=dst, i=i):
            pltpu.make_async_copy(own, dst, sems.at[i]).start()

        @pl.when(jnp.logical_not(first))
        def _(other=other, dst=dst, i=i):
            pltpu.make_async_copy(other, dst, sems.at[i]).start()

    return [pltpu.make_async_copy(own, dst, sems.at[i]) for i, (own, other, dst) in enumerate(pairs)]


N_ATTN = 4
N_FFN = 6
SENT_AT_ONCE = 3
GRADS_BY = ((2, 4), (1, 3))


def attn_targets(w_in, w_out, heads_width):
    return [w_in.at[pl.ds(i * heads_width, heads_width)] for i in range(3)] + [w_out]


def ffn_targets(wg, wu, wd):
    experts = wg.shape[0] - 1
    first = pl.ds(0, experts)
    return [wg.at[first], wu.at[first], wd.at[first], wg.at[experts], wu.at[experts], wd.at[experts]]


def both_kernel(ranks, planes, top, *refs):
    (lens, bnd, routes, gain_a_own, gain_f_own, router, tables), refs = refs[:7], refs[7:]
    own, refs = refs[:10], refs[10:]
    other, refs = refs[:10], refs[10:]
    (nf_o, q_o, k_o, v_o, p_o, mx_o, hf_o, g_o, u_o, hp_o, land, land_z), refs = refs[:12], refs[12:]
    (out_rows, in_grads, gain_a_out, gain_f_out, router_out, balance), refs = refs[:6], refs[6:]
    (nf, qs, ks, vs, ps, mx, hf, gs, us, hp), refs = refs[:10], refs[10:]
    (w_in, wo, wg, wu, wd), refs = refs[:5], refs[5:]
    (dyf, dyp, acts, gp, up, ap, coef, gate_sum), refs = refs[:8], refs[8:]
    (stage, stage_y, land_a, land_f, land_y, row_buf, d_mid), refs = refs[:7], refs[7:]
    (sent, got, quarter, df, ds, dqkv, gw, got_a, half_a, pair_in), refs = refs[:10], refs[10:]
    (xs, mid, small, o_small, probs_sum, cnt, o_cnt, cnt_in), refs = refs[:8], refs[8:]
    (o_bnd, o_routes, o_gain_a, o_gain_f, o_router, y_low), refs = refs[:6], refs[6:]
    (packs, pack_t, pack_z, gain_now), refs = refs[:4], refs[4:]
    (ag_s, ag_r, rsa_s, rsa_r, rsf_s, rsf_r, rsy_s, rsy_r, ex_s, ex_r), refs = refs[:10], refs[10:]
    (hp_s, hp_r, hq_s, hq_r, dp_s, dp_r, cz_s, cz_r, cs_s, cs_r, row_s, row_r), refs = refs[:12], refs[12:]
    (sw_s, sw_r, zs, zr, zl, as_s, as_r, az_s, az_r, az_l), refs = refs[:10], refs[10:]
    (pr_s, pr_r, gr_s, gr_r, pk_s, pk_r, pt_s, pt_r, pz_s, pz_r, ffn_sem, attn_sem, save_sem) = refs

    place = Place(ranks, planes)
    s, t, z, odd = place.s, place.t, place.z, place.odd
    rows, width = bnd.shape[1], bnd.shape[2]
    seq_len = hf.shape[0]
    experts = wg.shape[0] - 1
    blocks = experts + 1
    inner = wg.shape[2]
    half = inner // 2
    part = half // 2
    heads = qs.shape[0]
    heads_width = heads * HEAD_DIM
    chunk = width // planes
    chunks = width // LANES
    mine = pl.ds(t * rows, rows)
    my_lanes = pl.ds(pl.multiple_of(odd * half, half), half)
    far_lanes = pl.ds(pl.multiple_of((1 - odd) * half, half), half)
    slot = s * planes + z
    scale = HEAD_DIM ** (-0.5)

    def ffn_weights(l):
        targets = ffn_targets(wg, wu, wd)
        return load_choice(s == l, [(own[4 + i], other[4 + i], targets[i]) for i in range(N_FFN)], ffn_sem)

    def attn_weights(l):
        targets = attn_targets(w_in, wo, heads_width)
        return load_choice(s == l, [(own[i], other[i], targets[i]) for i in range(N_ATTN)], attn_sem)

    ffn_state = [(gs, g_o), (us, u_o), (hf, hf_o), (hp, hp_o)]
    attn_state = [(nf, nf_o), (qs, q_o), (ks, k_o), (vs, v_o), (ps, p_o), (mx, mx_o)]

    def moves(pairs, first, back):
        copies = []
        for i, (inside, outside) in enumerate(pairs):
            src, dst = (outside, inside) if back else (inside, outside)
            copies.append(pltpu.make_async_copy(src, dst, save_sem.at[first + i]))
        return copies

    def begin(copies):
        for copy in copies:
            copy.start()
        return copies

    def finish_all(copies):
        for copy in copies:
            copy.wait()

    class RelayGather:
        def __init__(self, full, send, recv):
            near = t + 1 - 2 * lax.rem(t, 2)
            far = lax.rem(t + 2, ranks)
            side = rows // 2

            def copy(owner, upper, at, to):
                piece = full.at[pl.ds(owner * rows + upper * side, side)]
                return remote(piece, piece, send.at[at], recv.at[at], (s, to, z))

            self.near, self.far = near, far
            self.diagonal = lax.rem(near + 2, ranks)
            self.first = [copy(t, 0, 0, near), copy(t, 1, 2, far), copy(t, 1, 1, near), copy(t, 0, 3, far)]
            self.relays = [copy(near, 0, 4, far), copy(far, 1, 5, near)]
            begin(self.first)

        def wait(self, arrived=lambda rank: None):
            for copy, relay in zip(self.first[:2], self.relays):
                copy.wait_recv()
                relay.start()
            for copy, rank in zip(self.first[2:], (self.near, self.far)):
                copy.wait_recv()
                arrived(rank)
            for relay in self.relays:
                relay.wait_recv()
            arrived(self.diagonal)
            for copy in self.first + self.relays:
                copy.wait_send()

    def gather_now(full, send, recv):
        if ranks == 4:
            return [RelayGather(full, send, recv)]
        return gather_rows(place, full, rows, send, recv)

    def gain_of(l, mine_ref, other_ref):
        return jnp.where(s == l, mine_ref[...], other_ref[...])

    def route_weights(l):
        value = jnp.where(s == l, router[...], o_router[...]).astype(f32)
        if experts < 8:
            value = jnp.concatenate([value, jnp.zeros((8 - experts, width), f32)], axis=0)
        return value.astype(bf16)

    def to_owner(l, src, dst, send, recv, local):
        for c in range(planes):
            own_copy = (z == c) & (s == l)

            @pl.when(own_copy)
            def _(c=c):
                pltpu.make_async_copy(src(c), dst, local).start()

            @pl.when(jnp.logical_not(own_copy))
            def _(c=c):
                remote(src(c), dst, send.at[c], recv.at[slot], (l, t, c)).start()

    def sent_to_owner(l, whole, dst, send, recv, local):
        for c in range(planes):
            own_copy = (z == c) & (s == l)

            @pl.when(own_copy)
            def _(c=c):
                pltpu.make_async_copy(whole.at[c], dst.at[slot], local).wait()

            @pl.when(jnp.logical_not(own_copy))
            def _(c=c):
                remote(whole.at[c], dst.at[slot], send.at[c], recv.at[slot], (l, t, c)).wait_send()

    def arrived(dst, send, recv):
        for source in range(2 * planes):

            @pl.when(source != slot)
            def _(source=source):
                remote(
                    dst.at[source], dst.at[source], send.at[0], recv.at[source], place.sibling
                ).wait_recv()

    class RelayScatter:
        def __init__(self, staged, landing, send, recv):
            self.near, self.far = t + 1 - 2 * lax.rem(t, 2), lax.rem(t + 2, ranks)
            self.diagonal = lax.rem(self.near + 2, ranks)
            self.staged, self.landing, self.send, self.recv = staged, landing, send, recv
            self.side = rows // 2
            self.first, self.relays = [], []

        def rows_of(self, rank, upper):
            return pl.ds(pl.multiple_of(rank * rows + upper * self.side, self.side), self.side)

        def add(self, n):
            lanes, side = pl.ds(n * LANES, LANES), self.side

            def copy(owner, upper, room, upper_room, at, to):
                src = self.staged.at[self.rows_of(owner, upper), lanes]
                dst = self.landing.at[room, pl.ds(upper_room * side, side), lanes]
                return remote(src, dst, self.send.at[n, at], self.recv.at[n, at], (s, to, z))

            near, far, diagonal = self.near, self.far, self.diagonal
            self.first.append(
                begin(
                    [
                        copy(diagonal, 0, 2, 0, 0, near),
                        copy(diagonal, 1, 2, 1, 1, far),
                        copy(near, 0, 0, 0, 2, near),
                        copy(far, 1, 1, 1, 3, far),
                    ]
                )
            )
            self.relays.append([copy(far, 0, 1, 0, 4, far), copy(near, 1, 0, 1, 5, near)])

        def wait(self):
            for n, (first, relays) in enumerate(zip(self.first, self.relays)):
                lanes = slice(n * LANES, (n + 1) * LANES)
                for upper, rank in enumerate((self.far, self.near)):
                    first[upper].wait_recv()
                    here_rows = self.rows_of(rank, upper)
                    passed = self.landing[2, upper * self.side : (upper + 1) * self.side, lanes]
                    summed = self.staged[here_rows, lanes].astype(f32) + passed.astype(f32)
                    self.staged[here_rows, lanes] = summed.astype(bf16)
                    relays[upper].start()
            for first, relays in zip(self.first, self.relays):
                finish_all([Half(copy.wait_recv) for copy in first[2:] + relays])
                finish_all([Half(copy.wait_send) for copy in first + relays])

    class Half:
        def __init__(self, wait):
            self.wait = wait

    def landed(staged, landing, relayed=False):
        own_rows = staged[mine].astype(f32)
        return landed_sum(own_rows, landing, 3 if relayed and ranks == 4 else ranks)

    def scatter_product(product, staged, landing, send, recv, relayed=False):
        relayed = relayed and ranks == 4
        copies = [RelayScatter(staged, landing, send, recv)] if relayed else []
        for n in range(chunks):
            lanes = slice(n * LANES, (n + 1) * LANES)
            staged[:, lanes] = product(lanes).astype(bf16)
            if relayed:
                copies[0].add(n)
            else:
                copies += scatter_block(
                    place, staged, landing, rows, n * LANES, LANES, send.at[n], recv.at[n]
                )
        return copies

    def share_of(l):
        return remote(half_a.at[l, 1 - odd], pair_in.at[l], pr_s.at[l], pr_r.at[l], place.partner)

    side = 2 * heads_width

    def swap_half(l):
        theirs = pl.ds(pl.multiple_of((1 - s) * side, 128), side)
        return remote(gw.at[:, theirs], got_a, as_s.at[l], as_r.at[l], place.sibling)

    def share_half(l):
        swap_half(l).wait()
        ours = pl.ds(pl.multiple_of(s * side, 128), side)
        kept = (gw[:, ours].astype(f32) + got_a[...].astype(f32)).astype(bf16)
        for side_b in range(2):
            for c in range(planes):
                lo = c * chunk + side_b * (chunk // 2)
                half_a[l, side_b, c] = kept[lo : lo + chunk // 2]
        share_of(l).start()

    def send_half(l):
        share_of(l).wait()
        half_a[l, odd] = (half_a[l, odd].astype(f32) + pair_in[l].astype(f32)).astype(bf16)
        to_owner(l, lambda c: half_a.at[l, odd, c], land_z.at[slot], az_s.at[l], az_r, az_l.at[l])

    def forward_chunks(gathering, full, landing, send, recv):
        copies = begin([remote(full.at[mine], landing.at[mine], send.at[0], recv.at[0], place.partner)])

        def onward(rank):
            they = pl.ds(rank * rows, rows)
            at = len(copies)
            copies.extend(
                begin([remote(full.at[they], landing.at[they], send.at[at], recv.at[at], place.partner)])
            )

        if ranks == 4:
            gathering[0].wait(onward)
        else:
            for k, copy in enumerate(gathering, 1):
                copy.wait()
                onward(place.peer(ranks - k))
        return copies

    place.greet()
    first_w = 5
    ex_pairs = [
        (bnd.at[1 - s], o_bnd),
        (gain_a_own, o_gain_a),
        (gain_f_own, o_gain_f),
        (router, o_router),
        (routes.at[1 - s], o_routes),
    ] + [(own[i], other[i]) for i in range(10)]
    exchange = [
        remote(src, dst, ex_s.at[i], ex_r.at[i], place.sibling) for i, (src, dst) in enumerate(ex_pairs)
    ]
    begin(exchange)
    row8 = lax.broadcasted_iota(jnp.int32, (8, seq_len), 0)
    token8 = lax.broadcasted_iota(jnp.int32, (8, seq_len), 1)
    length = lens[s]
    cosine, signed = tables[:, :HEAD_DIM], tables[:, HEAD_DIM:]

    def attn_begin(l):
        if l == 0:

            @pl.when(s == 0)
            def _():
                gain_now[...] = gain_a_own[...]

            @pl.when(s != 0)
            def _():
                gain_now[...] = o_gain_a[...]

        else:
            gain_now[...] = gain_of(l, gain_a_own, o_gain_a)
        nf[mine] = rms_rows(xs[l].astype(f32), gain_now[...]).astype(bf16)
        return gather_now(nf, ag_s.at[l, 0], ag_r.at[l, 0])

    def attn_forward(l, gathering, loads, between):
        finish_all(loads)
        finish_all(gathering)
        between()
        projected = dot(nf[...], w_in[...], 1, 1)
        for j, dst in enumerate((qs, ks, vs)):
            for h in range(heads):
                at = j * heads_width + h * HEAD_DIM
                piece = projected[:, at : at + HEAD_DIM]
                if j < 2:
                    piece = piece * cosine + turn_halves(piece) * signed
                dst[h] = piece.astype(bf16)
        place_q = lax.broadcasted_iota(jnp.int32, (seq_len, seq_len), 0)
        place_k = lax.broadcasted_iota(jnp.int32, (seq_len, seq_len), 1)
        allowed = (place_k <= place_q) & (place_k < length)
        for h in range(heads):
            scores = dot(qs[h], ks[h], 1, 1) * scale
            scores = jnp.where(allowed, scores, MASKED)
            peak = jnp.max(scores, axis=-1, keepdims=True)
            raised = jnp.exp(scores - peak)
            total = jnp.sum(raised, axis=-1, keepdims=True)
            weights = (raised / total).astype(bf16)
            ps[h] = weights
            mx[:, h * HEAD_DIM : (h + 1) * HEAD_DIM] = dot(weights, vs[h], 1, 0).astype(bf16)
        return scatter_product(
            lambda lanes: dot(mx[...], wo[:, lanes], 1, 0),
            stage,
            land_a,
            rsa_s.at[l, pl.ds(0, chunks)],
            rsa_r.at[l, pl.ds(0, chunks)],
            True,
        )

    def attn_finish(l, scattering):
        finish_all(scattering)
        middle = xs[l].astype(f32) + landed(stage, land_a, True)
        mid[l] = middle
        hf[mine] = rms_rows(middle, gain_of(l, gain_f_own, o_gain_f)).astype(bf16)
        return gather_now(hf, ag_s.at[l, 1], ag_r.at[l, 1])

    def route(l):
        names = name_rows(jnp.where(s == l, routes[s], o_routes[...]))
        logits = dot(route_weights(l), hf[...], 1, 1)
        logits = jnp.where(row8 < experts, logits, MASKED)
        raised = jnp.exp(logits - jnp.max(logits, axis=0, keepdims=True))
        raised = jnp.where(row8 < experts, raised, 0.0)
        chances = raised / jnp.sum(raised, axis=0, keepdims=True)
        per_chosen = names / jnp.sum(chances * names, axis=0, keepdims=True)
        gates = chances * per_chosen
        small[l, 0:8] = chances
        small[l, 8:16] = gates
        small[l, 16:24] = per_chosen
        remote(small.at[l], o_small.at[l], hp_s.at[l, 1], hp_r.at[l, 1], place.partner).start()
        summed = jnp.sum(jnp.where(token8 < length, chances, 0.0), axis=1, keepdims=True)
        probs_sum[l] = jnp.broadcast_to(summed, (8, 128))
        coef[...] = jnp.where(row8 == experts, 1.0, gates).T

    def split_acts(e, value):
        low, high = value[:, :half], value[:, half:]
        acts[e] = jnp.where(odd == 0, low, high).astype(bf16)
        gp[e] = jnp.where(odd == 0, high, low).astype(bf16)

    def branch_product(lanes):
        total = dot(acts[0], wd[0, my_lanes, lanes], 1, 0) + dot(gp[0], wd[0, far_lanes, lanes], 1, 0)
        for e in range(1, blocks):
            total = total + dot(acts[e], wd[e, my_lanes, lanes], 1, 0)
            total = total + dot(gp[e], wd[e, far_lanes, lanes], 1, 0)
        return total

    def output_rows(l, landing, staged):
        output = mid[l] + landed(staged, landing, l == 0)
        y_low[l] = output.astype(bf16)

        @pl.when(s == l)
        def _():
            out_rows[s] = y_low[l]

        @pl.when(s != l)
        def _():
            remote(y_low.at[l], out_rows.at[s], row_s, row_r, place.sibling).start()

    @pl.when(s == 0)
    def _():
        xs[0] = bnd[0]

    @pl.when(s != 0)
    def _():
        finish_all(exchange[:first_w])
        xs[0] = o_bnd[...]

    gathering = attn_begin(0)

    @pl.when(s != 0)
    def _():
        for copy in exchange[first_w : first_w + N_ATTN]:
            copy.wait_recv()

    loads = attn_weights(0)
    counted = jnp.zeros((8, 1), f32)
    for q in range(2):
        live = jnp.where(token8 < lens[q], 1.0, 0.0)
        counts = jnp.where(row8 == 7, live, name_rows(routes[q]) * live)
        counted = counted + jnp.sum(counts, axis=1, keepdims=True)
    cnt[...] = jnp.broadcast_to(counted, cnt.shape)
    count_copies = begin(
        [
            remote(cnt, cnt_in.at[k - 1], cz_s.at[k - 1], cz_r.at[k - 1], place.plane_id(k))
            for k in range(1, planes)
        ]
    )

    @pl.when(s == 0)
    def _():
        finish_all(exchange[:first_w])

    cotangent = jnp.where(s == 0, o_bnd[...], bnd[1]).astype(f32)
    position = lax.broadcasted_iota(jnp.int32, (rows, width), 0) + t * rows
    dyf[mine] = jnp.where(position < length, cotangent, 0.0).astype(bf16)
    cot_gather = []

    def gather_cotangent():
        cot_gather.extend(gather_rows(place, dyf, rows, ag_s.at[1, 2], ag_r.at[1, 2]))

    scattering = attn_forward(0, gathering, loads, gather_cotangent)

    @pl.when(s != 0)
    def _():
        for copy in exchange[first_w + N_ATTN :]:
            copy.wait_recv()

    ffn_loads = ffn_weights(0)
    attn_saves = begin(moves(attn_state, 4, False))
    gathering = attn_finish(0, scattering)

    @pl.when(s == 0)
    def _():
        for copy in exchange[first_w : first_w + N_ATTN]:
            copy.wait_recv()

    attn_w = attn_weights(1)
    finish_all(count_copies)
    total = cnt[...]
    for k in range(planes - 1):
        total = total + cnt_in[k]
    cnt[...] = total
    share_counts = remote(cnt, o_cnt, cs_s, cs_r, place.sibling)
    share_counts.start()
    finish_all(ffn_loads)
    finish_all(gathering)
    ffn_saves = begin(moves(ffn_state[2:3], 2, False))
    hidden_sent = [remote(hf, hp_o, hp_s.at[0, 0], hp_r.at[0, 0], place.partner)]
    begin(hidden_sent)
    route(0)

    def forward_expert(e, carry):
        gate_h = dot(hf[...], wg[e], 1, 0)
        up_h = dot(hf[...], wu[e], 1, 0)
        gs[e] = gate_h.astype(bf16)
        us[e] = up_h.astype(bf16)
        split_acts(e, gate_h * jax.nn.sigmoid(gate_h) * up_h * column(coef[...], e))
        return carry

    lax.fori_loop(0, blocks, forward_expert, 0)
    ffn_saves += begin(moves(ffn_state[:2], 0, False))
    finish_all(attn_saves)
    scat = scatter_product(branch_product, stage, land_f, rsf_s.at[0, 0], rsf_r.at[0, 0], True)

    @pl.when(s == 0)
    def _():
        for copy in exchange[first_w + N_ATTN :]:
            copy.wait_recv()

    ffn_loads = ffn_weights(1)
    finish_all(cot_gather)
    cot_sent = remote(dyf, dyp.at[1], dp_s.at[1, 0], dp_r.at[1, 0], place.partner)
    cot_sent.start()
    finish_all(scat)
    output_rows(0, land_f, stage)
    xs[1] = y_low[0]

    gathering = attn_begin(1)
    finish_all(hidden_sent)
    finish_all(ffn_saves)
    scattering = attn_forward(1, gathering, attn_w, lambda: None)
    gathering = attn_finish(1, scattering)
    hidden_sent = forward_chunks(gathering, hf, hp, hq_s, hq_r)
    finish_all(ffn_loads)
    route(1)
    gate_sum[...] = jnp.zeros_like(gate_sum)
    lane8 = lax.broadcasted_iota(jnp.int32, gate_sum.shape, 1)

    def expert_grads(e, gate_h, up_h, raw):
        sig = jax.nn.sigmoid(gate_h)
        silu = gate_h * sig
        acted = silu * up_h
        inner_sum = jnp.sum(acted * raw, axis=1, keepdims=True)
        gate_sum[...] = jnp.where(lane8 == e, inner_sum, gate_sum[...])
        weight = column(coef[...], e)
        d_acted = raw * weight
        gs[e] = (d_acted * up_h * (sig + silu * (1.0 - sig))).astype(bf16)
        us[e] = (d_acted * silu).astype(bf16)
        return acted * weight

    def both_expert(e, carry):
        gate_h = dot(hf[...], wg[e], 1, 0)
        up_h = dot(hf[...], wu[e], 1, 0)
        raw = dot(dyf[...], wd[e], 1, 1)
        split_acts(e, expert_grads(e, gate_h, up_h, raw))
        return carry

    def back_expert(e, carry):
        raw = dot(dyf[...], wd[e], 1, 1)
        value = expert_grads(e, gs[e].astype(f32), us[e].astype(f32), raw)
        acts[e] = jnp.where(odd == 0, value[:, :half], value[:, half:]).astype(bf16)
        return carry

    lax.fori_loop(0, blocks, both_expert, 0)
    share_counts.wait()
    y_scat = []

    for l in (1, 0):
        here = s == l
        if l == 0:
            finish_all(ffn_loads)
            finish_all(ffn_back)
            coef[...] = jnp.where(row8 == experts, 1.0, small[l, 8:16]).T
            gate_sum[...] = jnp.zeros_like(gate_sum)
            to_partner = forward_chunks(gathering, dyf, dyp.at[l], dp_s.at[l], dp_r.at[l])
            share_half(1)
            for e in range(SENT_AT_ONCE, blocks):
                send_later(e)
            lax.fori_loop(0, blocks, back_expert, 0)
        else:
            to_partner = [cot_sent]
        if l == 1:
            y_scat = scatter_product(branch_product, stage_y, land_y, rsy_s, rsy_r)
        finish_all(to_partner)
        if l == 1:
            finish_all(hidden_sent)
        remote(small.at[l], o_small.at[l], hp_s.at[l, 1], hp_r.at[l, 1], place.partner).wait()
        coef[...] = jnp.where(row8 == experts, 1.0, o_small[l, 8:16]).T

        def partner_expert(e, carry, l=l):
            gate_h = dot(hp[...], wg[e, :, my_lanes], 1, 0)
            up_h = dot(hp[...], wu[e, :, my_lanes], 1, 0)
            raw = dot(dyp[l], wd[e, my_lanes], 1, 1)
            sig = jax.nn.sigmoid(gate_h)
            silu = gate_h * sig
            weight = column(coef[...], e)
            ap[e] = (silu * up_h * weight).astype(bf16)
            d_acted = raw * weight
            gp[e] = (d_acted * up_h * (sig + silu * (1.0 - sig))).astype(bf16)
            up[e] = (d_acted * silu).astype(bf16)
            return carry

        lax.fori_loop(0, blocks, partner_expert, 0)
        def swap_of(e, l=l):
            return remote(sent.at[e], got.at[e], sw_s.at[e], sw_r.at[e], place.sibling)

        def send_grads(e, l=l):
            three = pl.ds(e * 3, 3)
            to_owner(l, lambda c: quarter.at[l, c, three], land.at[slot, three], zs.at[l], zr, zl.at[l])

        def finish(e, l=l, send_grads=send_grads):
            swap_of(e).wait()
            for j in range(3):
                at = e * 3 + j
                for c in range(planes):
                    quarter[l, c, at] = (
                        quarter[l, c, at].astype(f32) + got[e, j, c].astype(f32)
                    ).astype(bf16)

            @pl.when(jnp.logical_or(l == 0, e < SENT_AT_ONCE))
            def _():
                send_grads(e)

        def weight_grads(e, carry, l=l, finish=finish):
            sources = ((hf, gs, hp, gp), (hf, us, hp, up))
            for j in range(3):
                if j < 2:
                    left, right, left_p, right_p = sources[j]
                    value = dot(left[...], right[e, :, my_lanes], 0, 0) + dot(left_p[...], right_p[e], 0, 0)
                else:
                    value = dot(dyf[...], acts[e], 0, 0) + dot(dyp[l], ap[e], 0, 0)
                low, high = value[:, :part], value[:, part:]
                kept = jnp.where(s == 0, low, high).astype(bf16)
                given = jnp.where(s == 0, high, low).astype(bf16)
                for c in range(planes):
                    quarter[l, c, e * 3 + j] = kept[c * chunk : (c + 1) * chunk]
                    sent[e, j, c] = given[c * chunk : (c + 1) * chunk]
            swap_of(e).start()

            @pl.when(e > 0)
            def _():
                finish(e - 1)

            return carry

        early, middle = GRADS_BY[l]
        if l == 1:
            send_later = send_grads
        lax.fori_loop(0, early, weight_grads, 0)
        chances, gates, per_chosen = small[l, 0:8], small[l, 8:16], small[l, 16:24]
        totals = jnp.where(here, cnt[...], o_cnt[...])
        tokens_all = totals[7:8, 0:1]
        share = totals[:, 0:1] / (top * tokens_all)
        aux = jnp.where((token8 < length) & (t == 0), ALPHA * experts * share / tokens_all, 0.0)
        d_gates = gate_sum[...].T
        common = jnp.sum(d_gates * gates, axis=0, keepdims=True)
        d_chances = per_chosen * (d_gates - common) + aux
        d_logits = chances * (d_chances - jnp.sum(chances * d_chances, axis=0, keepdims=True))
        d_logits = d_logits.astype(bf16)
        router_grad = dot(d_logits, hf[...], 1, 0)
        route_w = route_weights(l)

        def hidden_product(lanes, d_logits=d_logits, route_w=route_w):
            total = dot(d_logits, route_w[:, lanes], 0, 0)
            for e in range(blocks):
                total = total + dot(gs[e], wg[e, lanes], 1, 1)
                total = total + dot(us[e], wu[e, lanes], 1, 1)
            return total

        scat = scatter_product(hidden_product, stage, land_f, rsf_s.at[l, 1], rsf_r.at[l, 1])
        lax.fori_loop(early, middle, weight_grads, 0)
        finish_all(scat)
        d_hidden = landed(stage, land_f)
        d_norm, gain_f_grad = rms_back(mid[l], gain_of(l, gain_f_own, o_gain_f), d_hidden)
        d_mid[...] = dyf[mine].astype(f32) + d_norm
        df[mine] = d_mid[...].astype(bf16)
        gathering = gather_rows(place, df, rows, ag_s.at[l, 3], ag_r.at[l, 3])

        if l == 0:
            send_half(1)
        lax.fori_loop(middle, blocks, weight_grads, 0)
        finish(blocks - 1)
        if l == 1:
            ffn_loads = ffn_weights(0)
            ffn_back = begin(moves(ffn_state, 0, True))
        else:
            finish_all(attn_w)
            finish_all(attn_back)
        finish_all(gathering)
        for h in range(heads):
            span = slice(h * HEAD_DIM, (h + 1) * HEAD_DIM)
            d_mixed = dot(df[...], wo[span], 1, 1).astype(bf16)
            for lo in range(0, seq_len, LANES):
                reach = lo + LANES
                weights = ps[h, lo:reach, 0:reach].astype(f32)
                d_probs = dot(d_mixed[lo:reach], vs[h, 0:reach], 1, 1)
                total = jnp.sum(weights * d_probs, axis=-1, keepdims=True)
                ds[lo:reach, 0:reach] = (weights * (d_probs - total)).astype(bf16)
                if reach < seq_len:
                    ds[lo:reach, reach:] = jnp.zeros((LANES, seq_len - reach), bf16)
            d_value = dot(ps[h], d_mixed, 0, 0)
            d_query = dot(ds[...], ks[h], 1, 0) * scale
            d_key = dot(ds[...], qs[h], 0, 0) * scale
            d_query = d_query * cosine - turn_halves(d_query) * signed
            d_key = d_key * cosine - turn_halves(d_key) * signed
            for j, value in enumerate((d_query, d_key, d_value)):
                at = j * heads_width + h * HEAD_DIM
                dqkv[:, at : at + HEAD_DIM] = value.astype(bf16)
        scat = scatter_product(
            lambda lanes: dot(dqkv[...], w_in[:, lanes], 1, 0), stage, land_a, rsa_s.at[l, pl.ds(chunks, chunks)], rsa_r.at[l, pl.ds(chunks, chunks)]
        )

        three_widths = 3 * heads_width
        gw[:, :three_widths] = dot(nf[...], dqkv[...], 0, 0).astype(bf16)
        gw[:, three_widths:] = dot(df[...], mx[...], 0, 0).astype(bf16)
        swap_half(l).start()
        finish_all(scat)
        d_normed = landed(stage, land_a)
        d_norm, gain_a_grad = rms_back(xs[l].astype(f32), gain_of(l, gain_a_own, o_gain_a), d_normed)
        dx = d_mid[...] + d_norm
        if l == 1:
            low_dx = dx.astype(bf16)
            dyf[mine] = low_dx
            gathering = gather_now(dyf, ag_s.at[0, 2], ag_r.at[0, 2])
            dx = low_dx.astype(f32)
            attn_w = attn_weights(0)
            attn_back = begin(moves(attn_state, 4, True))
            finish_all(y_scat)
            output_rows(1, land_y, stage_y)
        pack = jnp.concatenate(
            [
                jnp.concatenate([gain_a_grad, gain_f_grad, router_grad[:6]], axis=0),
                jnp.concatenate(
                    [jnp.zeros((2, 128), f32), jnp.where(t == 0, probs_sum[l, 0:6], 0.0)], axis=0
                ),
            ],
            axis=1,
        )

        @pl.when(here)
        def _(dx=dx, pack=pack):
            in_grads[s] = dx
            packs[0] = pack

        @pl.when(jnp.logical_not(here))
        def _(dx=dx, pack=pack):
            row_buf[...] = dx
            packs[1] = pack
            remote(row_buf, in_grads.at[s], gr_s, gr_r, place.sibling).start()
            remote(packs.at[1], packs.at[2], pk_s, pk_r, place.sibling).start()

    share_half(0)
    send_half(0)
    remote(packs.at[1], packs.at[2], pk_s, pk_r, place.sibling).wait()
    packs[0] = packs[0] + packs[2]
    finish_all(
        begin(
            [
                remote(packs.at[0], pack_t.at[k - 1], pt_s.at[k - 1], pt_r.at[k - 1], place.peer_id(k))
                for k in range(1, ranks)
            ]
        )
    )
    total = packs[0]
    for k in range(ranks - 1):
        total = total + pack_t[k]
    packs[0] = total
    finish_all(
        begin(
            [
                remote(packs.at[0], pack_z.at[k - 1], pz_s.at[k - 1], pz_r.at[k - 1], place.plane_id(k))
                for k in range(1, planes)
            ]
        )
    )
    total = packs[0]
    for k in range(planes - 1):
        total = total + pack_z[k]
    gain_a_out[...] = total[0:1, :width]
    gain_f_out[...] = total[1:2, :width]
    router_out[...] = total[2 : 2 + experts, :width]
    tokens_all = cnt[7:8, 0:1]
    products = cnt[0:experts, 0:1] / (top * tokens_all) * total[2 : 2 + experts, width : width + 1]
    balance[...] = experts * jnp.sum(products, axis=0, keepdims=True) / tokens_all

    for copy in exchange[first_w:]:
        copy.wait_send()
    remote(y_low.at[1 - s], out_rows.at[s], row_s, row_r, place.sibling).wait_send()
    remote(y_low.at[1 - s], out_rows.at[1 - s], row_s, row_r, place.sibling).wait_recv()
    remote(row_buf, in_grads.at[s], gr_s, gr_r, place.sibling).wait_send()
    remote(row_buf, in_grads.at[1 - s], gr_s, gr_r, place.sibling).wait_recv()
    for l in (1, 0):
        sent_to_owner(l, quarter.at[l], land, zs.at[l], zr, zl.at[l])
        sent_to_owner(l, half_a.at[l, odd], land_z, az_s.at[l], az_r, az_l.at[l])
    arrived(land, zs.at[0], zr)
    arrived(land_z, az_s.at[0], az_r)


def finish_kernel(planes, land, land_z, *refs):
    ins, outs, refs = refs[:6], refs[6:12], refs[12:]
    g_gate, g_up, g_down, s_gate, s_up, s_down, wq_out, wk_out, wv_out, wo_out = refs
    e = pl.program_id(0)
    experts = pl.num_programs(0) - 1
    part = land.shape[3]
    heads_width = wq_out.shape[1]
    for j, (routed, common) in enumerate(((g_gate, s_gate), (g_up, s_up), (g_down, s_down))):
        for core in range(2):
            for parity in range(2):
                value = land[core * planes + parity, j].astype(f32)
                for pair in range(1, planes // 2):
                    value = value + land[core * planes + 2 * pair + parity, j].astype(f32)
                lo = (2 * parity + core) * part

                @pl.when(e < experts)
                def _(value=value, lo=lo, routed=routed):
                    routed[0, :, lo : lo + part] = value

                @pl.when(e == experts)
                def _(value=value, lo=lo, common=common):
                    common[:, lo : lo + part] = value

    @pl.when(e == 1)
    def _():
        for src, dst in zip(ins, outs):
            dst[...] = src[...]
        sides = []
        for core in range(2):
            halves = []
            for parity in range(2):
                value = land_z[core * planes + parity].astype(f32)
                for pair in range(1, planes // 2):
                    value = value + land_z[core * planes + 2 * pair + parity].astype(f32)
                halves.append(value)
            sides.append(jnp.concatenate(halves, axis=0))
        wq_out[...] = sides[0][:, :heads_width]
        wk_out[...] = sides[0][:, heads_width:]
        wv_out[...] = sides[1][:, :heads_width]
        wo_out[...] = sides[1][:, heads_width:].T


def params(collective_id):
    return pltpu.CompilerParams(
        collective_id=collective_id, has_side_effects=True, vmem_limit_bytes=VMEM_LIMIT
    )


def shape_of(*dims, dtype=bf16):
    return jax.ShapeDtypeStruct(dims, dtype)


def on_device(ranks, planes, *args):
    (boundary, lengths, routes, attn_gain, w_query, w_key, w_value, w_out, ffn_gain, router) = args[:10]
    ffn_own = tuple(a[0] for a in args[10:])
    attn_own = (w_query[0].T, w_key[0].T, w_value[0].T, w_out[0])
    rows, width = boundary.shape[2:]
    seqs, seq_len = routes.shape[1:3]
    top = routes.shape[3]
    experts, _, inner = ffn_own[0].shape
    blocks = experts + 1
    heads_width = w_query.shape[2]
    heads = heads_width // HEAD_DIM
    chunks = width // LANES
    half, part = inner // 2, inner // 4
    chunk = width // planes
    peers = ranks - 1
    dma = pltpu.SemaphoreType.DMA

    def vmem(*dims, dtype=bf16):
        return pltpu.VMEM(dims, dtype)

    routes_t = jnp.swapaxes(routes[0], 1, 2)
    router_t = router[0].T
    tables = jnp.asarray(rope_tables(seq_len))
    head_shape = (heads, seq_len, HEAD_DIM)
    states = [
        (seq_len, width),
        head_shape,
        head_shape,
        head_shape,
        (heads, seq_len, seq_len),
        (seq_len, heads_width),
        (seq_len, width),
        (blocks, seq_len, inner),
        (blocks, seq_len, inner),
        (seq_len, width),
    ]
    weights = attn_own + ffn_own
    small_outs = [
        shape_of(2, rows, width),
        shape_of(seqs, rows, width, dtype=f32),
        shape_of(1, width, dtype=f32),
        shape_of(1, width, dtype=f32),
        shape_of(experts, width, dtype=f32),
        shape_of(1, 1, dtype=f32),
    ]
    result = pl.pallas_call(
        functools.partial(both_kernel, ranks, planes, top),
        out_shape=[shape_of(*w.shape) for w in weights]
        + [shape_of(*dims) for dims in states]
        + [
            shape_of(2 * planes, 3 * blocks, chunk, part),
            shape_of(2 * planes, chunk // 2, 2 * heads_width),
        ]
        + small_outs,
        in_specs=[SMEM] + [VMEM] * 6 + [ANY] * 10,
        out_specs=[ANY] * 22 + [VMEM] * 6,
        scratch_shapes=[vmem(*dims) for dims in states]
        + [
            vmem(3 * heads_width, width),
            vmem(heads_width, width),
            vmem(blocks, width, inner),
            vmem(blocks, width, inner),
            vmem(blocks, inner, width),
        ]
        + [vmem(seq_len, width), vmem(2, seq_len, width)]
        + [vmem(blocks, seq_len, half)] * 4
        + [vmem(seq_len, 8, dtype=f32)] * 2
        + [vmem(seq_len, width)] * 2
        + [vmem(peers, rows, width)] * 3
        + [vmem(rows, width, dtype=f32)] * 2
        + [
            vmem(blocks, 3, planes, chunk, part),
            vmem(blocks, 3, planes, chunk, part),
            vmem(2, planes, 3 * blocks, chunk, part),
            vmem(seq_len, width),
            vmem(seq_len, seq_len),
            vmem(seq_len, 3 * heads_width),
            vmem(width, 4 * heads_width),
            vmem(width, 2 * heads_width),
            vmem(2, 2, planes, chunk // 2, 2 * heads_width),
            vmem(2, planes, chunk // 2, 2 * heads_width),
        ]
        + [
            vmem(2, rows, width),
            vmem(2, rows, width, dtype=f32),
            vmem(2, 24, seq_len, dtype=f32),
            vmem(2, 24, seq_len, dtype=f32),
            vmem(2, 8, 128, dtype=f32),
            vmem(8, 128, dtype=f32),
            vmem(8, 128, dtype=f32),
            vmem(planes - 1, 8, 128, dtype=f32),
        ]
        + [
            vmem(rows, width),
            vmem(top, seq_len, dtype=jnp.int32),
            vmem(1, width, dtype=f32),
            vmem(1, width, dtype=f32),
            vmem(*router_t.shape),
            vmem(2, rows, width),
        ]
        + [
            vmem(3, 8, width + 128, dtype=f32),
            vmem(peers, 8, width + 128, dtype=f32),
            vmem(planes - 1, 8, width + 128, dtype=f32),
            vmem(1, width, dtype=f32),
        ]
        + [dma((2, 4, max(peers, 6)))] * 2
        + [dma((2, 2 * chunks, max(peers, 6)))] * 2
        + [dma((2, 2, chunks, max(peers, 6)))] * 2
        + [dma((chunks, max(peers, 6)))] * 2
        + [dma((15,))] * 2
        + [dma((2, 2))] * 2
        + [dma((ranks,))] * 2
        + [dma((2, ranks))] * 2
        + [dma((planes - 1,))] * 2
        + [dma] * 4
        + [dma((blocks,))] * 2
        + [dma((2, planes)), dma((2 * planes,)), dma((2,))]
        + [dma((2,))] * 2
        + [dma((2, planes)), dma((2 * planes,)), dma((2,))]
        + [dma((2,))] * 2
        + [dma] * 4
        + [dma((peers,))] * 2
        + [dma((planes - 1,))] * 2
        + [dma((N_FFN,)), dma((N_ATTN,)), dma((10,))],
        compiler_params=params(0),
        name="forward_backward",
    )(lengths, boundary[0], routes_t, attn_gain, ffn_gain, router_t, tables, *weights)
    land, land_z, *small_results = result[20:]

    def whole(shape):
        return pl.BlockSpec(shape, lambda e: (0,) * len(shape))

    routed = shape_of(experts, chunk, inner, dtype=f32)
    common = shape_of(chunk, inner, dtype=f32)
    square = shape_of(chunk, heads_width, dtype=f32)
    turned = shape_of(heads_width, chunk, dtype=f32)
    last = experts - 1
    done = pl.pallas_call(
        functools.partial(finish_kernel, planes),
        grid=(blocks,),
        out_shape=small_outs + [routed] * 3 + [common] * 3 + [square] * 3 + [turned],
        in_specs=[
            pl.BlockSpec((2 * planes, 3, chunk, part), lambda e: (0, e, 0, 0)),
            whole(land_z.shape),
        ]
        + [whole(o.shape) for o in small_outs],
        out_specs=[whole(o.shape) for o in small_outs]
        + [pl.BlockSpec((1, chunk, inner), lambda e: (jnp.minimum(e, last), 0, 0))] * 3
        + [whole(common.shape)] * 3
        + [whole(square.shape)] * 3
        + [whole(turned.shape)],
        compiler_params=pltpu.CompilerParams(vmem_limit_bytes=VMEM_LIMIT),
        name="finish",
    )(land, land_z, *small_results)
    (out_rows, in_grads, g_gain_a, g_gain_f, g_router, balance), done = done[:6], done[6:]
    g_eg, g_eu, g_ed, g_sg, g_su, g_sd, g_q, g_k, g_v, g_o = done
    return (
        out_rows[None],
        in_grads[None],
        g_gain_a,
        g_q[None],
        g_k[None],
        g_v[None],
        g_o[None],
        g_gain_f,
        g_router.T[None],
        g_eg[None],
        g_eu[None],
        jnp.swapaxes(g_ed, 1, 2)[None],
        g_sg[None],
        g_su[None],
        g_sd.T[None],
        balance.reshape(1),
    )


def solution(mesh):
    placed = (
        P("section", "dp", "tensor", None),
        P("dp"),
        P("section", "dp", None, None),
        P("section", None),
        P("section", None, "tensor"),
        P("section", None, "tensor"),
        P("section", None, "tensor"),
        P("section", "tensor", None),
        P("section", None),
        P("section", None, None),
        P("section", None, None, "tensor"),
        P("section", None, None, "tensor"),
        P("section", None, "tensor", None),
        P("section", None, "tensor"),
        P("section", None, "tensor"),
        P("section", "tensor", None),
    )
    return jax.shard_map(
        functools.partial(on_device, mesh.shape["tensor"], mesh.shape["dp"]),
        mesh=mesh,
        in_specs=placed,
        out_specs=(
            P("section", "dp", "tensor", None),
            P("section", "dp", "tensor", None),
            P("section", None),
            P("section", "dp", "tensor"),
            P("section", "dp", "tensor"),
            P("section", "dp", "tensor"),
            P("section", "tensor", "dp"),
            P("section", None),
            P("section", None, None),
            P("section", None, "dp", "tensor"),
            P("section", None, "dp", "tensor"),
            P("section", None, "tensor", "dp"),
            P("section", "dp", "tensor"),
            P("section", "dp", "tensor"),
            P("section", "tensor", "dp"),
            P("section"),
        ),
        check_vma=False,
    )
```

```python
import functools

import jax
import jax.numpy as jnp
import numpy as np
from jax import lax
from jax.experimental import pallas as pl
from jax.experimental.pallas import tpu as pltpu
from jax.sharding import PartitionSpec as P

HEAD_DIM = 64
HALF_DIM = HEAD_DIM // 2
EPSILON = 1e-06
ALPHA = 0.01
THETA = 10000.0
MASKED = -1e30
LANES = 256
VMEM_LIMIT = 63 * 2**20 + 2**19

f32 = jnp.float32
bf16 = jnp.bfloat16
MESH = pl.DeviceIdType.MESH
ANY = pl.BlockSpec(memory_space=pl.ANY)
VMEM = pl.BlockSpec(memory_space=pltpu.VMEM)
SMEM = pl.BlockSpec(memory_space=pltpu.SMEM)


def dot(left, right, left_dim, right_dim):
    return lax.dot_general(
        left, right, (((left_dim,), (right_dim,)), ((), ())), preferred_element_type=f32
    )


def rope_tables(seq_len):
    frequency = (THETA ** (-np.arange(HALF_DIM, dtype=np.float32) / HALF_DIM)).astype(np.float32)
    angles = np.arange(seq_len, dtype=np.float32)[:, None] * frequency[None, :]
    cosine, sine = np.cos(angles), np.sin(angles)
    return np.concatenate([cosine, cosine, -sine, sine], axis=-1).astype(np.float32)


def turn_halves(values):
    return jnp.concatenate([values[:, HALF_DIM:], values[:, :HALF_DIM]], axis=1)


class Place:
    def __init__(self, ranks, planes):
        self.s = lax.axis_index("section")
        self.t = lax.axis_index("tensor")
        self.z = lax.axis_index("dp")
        self.ranks, self.planes = ranks, planes
        self.odd = lax.rem(self.z, 2)
        self.sibling = (1 - self.s, self.t, self.z)
        self.partner = (self.s, self.t, self.z + 1 - 2 * self.odd)

    def peer(self, k):
        return lax.rem(self.t + k, self.ranks)

    def peer_id(self, k):
        return (self.s, self.peer(k), self.z)

    def plane_id(self, k):
        return (self.s, self.t, lax.rem(self.z + k, self.planes))

    def greet(self):
        barrier = pltpu.get_barrier_semaphore()
        others = [self.sibling] + [self.peer_id(k) for k in range(1, self.ranks)]
        for k in range(1, self.planes):
            _, t, z = self.plane_id(k)
            others += [(self.s, t, z), (1 - self.s, t, z)]
        for other in others:
            pl.semaphore_signal(barrier, inc=1, device_id=other, device_id_type=MESH)
        pl.semaphore_wait(barrier, len(others))


def remote(src, dst, send, recv, device):
    return pltpu.make_async_remote_copy(
        src_ref=src, dst_ref=dst, send_sem=send, recv_sem=recv, device_id=device, device_id_type=MESH
    )


def gather_rows(place, full, rows, send, recv):
    mine = full.at[pl.ds(place.t * rows, rows)]
    copies = []
    for k in range(1, place.ranks):
        copy = remote(mine, mine, send.at[k - 1], recv.at[k - 1], place.peer_id(k))
        copy.start()
        copies.append(copy)
    return copies


def scatter_block(place, stage, landing, rows, lo, width, send, recv):
    copies = []
    for k in range(1, place.ranks):
        src = stage.at[pl.ds(place.peer(k) * rows, rows), pl.ds(lo, width)]
        dst = landing.at[k - 1, :, pl.ds(lo, width)]
        copy = remote(src, dst, send.at[k - 1], recv.at[k - 1], place.peer_id(k))
        copy.start()
        copies.append(copy)
    return copies


def landed_sum(own, landing, ranks):
    total = own
    for k in range(ranks - 1):
        total = total + landing[k].astype(f32)
    return total


def rms_rows(values, gain):
    return values * lax.rsqrt(jnp.mean(values * values, axis=-1, keepdims=True) + EPSILON) * gain


def rms_back(values, gain, grad):
    r = lax.rsqrt(jnp.mean(values * values, axis=-1, keepdims=True) + EPSILON)
    normed = values * r
    scaled = grad * gain
    inner = jnp.mean(scaled * normed, axis=-1, keepdims=True)
    return r * (scaled - normed * inner), jnp.sum(grad * normed, axis=0, keepdims=True)


def name_rows(routes):
    expert = lax.broadcasted_iota(jnp.int32, (8, routes.shape[1]), 0)
    named = routes[0:1] == expert
    for j in range(1, routes.shape[0]):
        named = named | (routes[j : j + 1] == expert)
    return named.astype(f32)


def column(matrix, index):
    lane = lax.broadcasted_iota(jnp.int32, matrix.shape, 1)
    return jnp.sum(jnp.where(lane == index, matrix, 0.0), axis=1, keepdims=True)


def load_choice(first, pairs, sems):
    for i, (own, other, dst) in enumerate(pairs):

        @pl.when(first)
        def _(own=own, dst=dst, i=i):
            pltpu.make_async_copy(own, dst, sems.at[i]).start()

        @pl.when(jnp.logical_not(first))
        def _(other=other, dst=dst, i=i):
            pltpu.make_async_copy(other, dst, sems.at[i]).start()

    return [pltpu.make_async_copy(own, dst, sems.at[i]) for i, (own, other, dst) in enumerate(pairs)]


N_ATTN = 4
N_FFN = 6
SENT_AT_ONCE = 3
GRADS_BY = ((2, 4), (2, 4))


def attn_targets(w_in, w_out, heads_width):
    return [w_in.at[pl.ds(i * heads_width, heads_width)] for i in range(3)] + [w_out]


def ffn_targets(wg, wu, wd):
    experts = wg.shape[0] - 1
    first = pl.ds(0, experts)
    return [wg.at[first], wu.at[first], wd.at[first], wg.at[experts], wu.at[experts], wd.at[experts]]


def both_kernel(ranks, planes, top, *refs):
    (lens, bnd, routes, gain_a_own, gain_f_own, router, tables), refs = refs[:7], refs[7:]
    own, refs = refs[:10], refs[10:]
    other, refs = refs[:10], refs[10:]
    (nf_o, q_o, k_o, v_o, p_o, mx_o, hf_o, g_o, u_o, hp_o, land, land_z), refs = refs[:12], refs[12:]
    (out_rows, in_grads, gain_a_out, gain_f_out, router_out, balance), refs = refs[:6], refs[6:]
    (nf, qs, ks, vs, ps, mx, hf, gs, us, hp), refs = refs[:10], refs[10:]
    (w_in, wo, wg, wu, wd), refs = refs[:5], refs[5:]
    (dyf, dyp, acts, gp, up, ap, coef, gate_sum), refs = refs[:8], refs[8:]
    (stage, stage_y, land_a, land_f, land_y, row_buf, d_mid), refs = refs[:7], refs[7:]
    (sent, got, quarter, df, ds, dqkv, gw, got_a, half_a, pair_in), refs = refs[:10], refs[10:]
    (xs, mid, small, o_small, probs_sum, cnt, o_cnt, cnt_in), refs = refs[:8], refs[8:]
    (o_bnd, o_routes, o_gain_a, o_gain_f, o_router, y_low), refs = refs[:6], refs[6:]
    (packs, pack_t, pack_z, gain_now), refs = refs[:4], refs[4:]
    (ag_s, ag_r, rsa_s, rsa_r, rsf_s, rsf_r, rsy_s, rsy_r, ex_s, ex_r), refs = refs[:10], refs[10:]
    (hp_s, hp_r, hq_s, hq_r, dp_s, dp_r, cz_s, cz_r, cs_s, cs_r, row_s, row_r), refs = refs[:12], refs[12:]
    (sw_s, sw_r, zs, zr, zl, as_s, as_r, az_s, az_r, az_l), refs = refs[:10], refs[10:]
    (pr_s, pr_r, gr_s, gr_r, pk_s, pk_r, pt_s, pt_r, pz_s, pz_r, ffn_sem, attn_sem, save_sem) = refs

    place = Place(ranks, planes)
    s, t, z, odd = place.s, place.t, place.z, place.odd
    rows, width = bnd.shape[1], bnd.shape[2]
    seq_len = hf.shape[0]
    experts = wg.shape[0] - 1
    blocks = experts + 1
    inner = wg.shape[2]
    half = inner // 2
    part = half // 2
    heads = qs.shape[0]
    heads_width = heads * HEAD_DIM
    chunk = width // planes
    chunks = width // LANES
    mine = pl.ds(t * rows, rows)
    my_lanes = pl.ds(pl.multiple_of(odd * half, half), half)
    far_lanes = pl.ds(pl.multiple_of((1 - odd) * half, half), half)
    slot = s * planes + z
    scale = HEAD_DIM ** (-0.5)

    def ffn_weights(l):
        targets = ffn_targets(wg, wu, wd)
        return load_choice(s == l, [(own[4 + i], other[4 + i], targets[i]) for i in range(N_FFN)], ffn_sem)

    def attn_weights(l):
        targets = attn_targets(w_in, wo, heads_width)
        return load_choice(s == l, [(own[i], other[i], targets[i]) for i in range(N_ATTN)], attn_sem)

    ffn_state = [(gs, g_o), (us, u_o), (hf, hf_o), (hp, hp_o)]
    attn_state = [(nf, nf_o), (qs, q_o), (ks, k_o), (vs, v_o), (ps, p_o), (mx, mx_o)]

    def moves(pairs, first, back):
        copies = []
        for i, (inside, outside) in enumerate(pairs):
            src, dst = (outside, inside) if back else (inside, outside)
            copies.append(pltpu.make_async_copy(src, dst, save_sem.at[first + i]))
        return copies

    def begin(copies):
        for copy in copies:
            copy.start()
        return copies

    def finish_all(copies):
        for copy in copies:
            copy.wait()

    class RelayGather:
        def __init__(self, full, send, recv):
            near = t + 1 - 2 * lax.rem(t, 2)
            far = lax.rem(t + 2, ranks)
            side = rows // 2

            def copy(owner, upper, at, to):
                piece = full.at[pl.ds(owner * rows + upper * side, side)]
                return remote(piece, piece, send.at[at], recv.at[at], (s, to, z))

            self.near, self.far = near, far
            self.diagonal = lax.rem(near + 2, ranks)
            self.first = [copy(t, 0, 0, near), copy(t, 1, 2, far), copy(t, 1, 1, near), copy(t, 0, 3, far)]
            self.relays = [copy(near, 0, 4, far), copy(far, 1, 5, near)]
            begin(self.first)

        def wait(self, arrived=lambda rank: None):
            for copy, relay in zip(self.first[:2], self.relays):
                copy.wait_recv()
                relay.start()
            for copy, rank in zip(self.first[2:], (self.near, self.far)):
                copy.wait_recv()
                arrived(rank)
            for relay in self.relays:
                relay.wait_recv()
            arrived(self.diagonal)
            for copy in self.first + self.relays:
                copy.wait_send()

    def gather_now(full, send, recv):
        if ranks == 4:
            return [RelayGather(full, send, recv)]
        return gather_rows(place, full, rows, send, recv)

    def gain_of(l, mine_ref, other_ref):
        return jnp.where(s == l, mine_ref[...], other_ref[...])

    def route_weights(l):
        value = jnp.where(s == l, router[...], o_router[...]).astype(f32)
        if experts < 8:
            value = jnp.concatenate([value, jnp.zeros((8 - experts, width), f32)], axis=0)
        return value.astype(bf16)

    def to_owner(l, src, dst, send, recv, local):
        for c in range(planes):
            own_copy = (z == c) & (s == l)

            @pl.when(own_copy)
            def _(c=c):
                pltpu.make_async_copy(src(c), dst, local).start()

            @pl.when(jnp.logical_not(own_copy))
            def _(c=c):
                remote(src(c), dst, send.at[c], recv.at[slot], (l, t, c)).start()

    def sent_to_owner(l, whole, dst, send, recv, local):
        for c in range(planes):
            own_copy = (z == c) & (s == l)

            @pl.when(own_copy)
            def _(c=c):
                pltpu.make_async_copy(whole.at[c], dst.at[slot], local).wait()

            @pl.when(jnp.logical_not(own_copy))
            def _(c=c):
                remote(whole.at[c], dst.at[slot], send.at[c], recv.at[slot], (l, t, c)).wait_send()

    def arrived(dst, send, recv):
        for source in range(2 * planes):

            @pl.when(source != slot)
            def _(source=source):
                remote(
                    dst.at[source], dst.at[source], send.at[0], recv.at[source], place.sibling
                ).wait_recv()

    class RelayScatter:
        def __init__(self, staged, landing, send, recv):
            self.near, self.far = t + 1 - 2 * lax.rem(t, 2), lax.rem(t + 2, ranks)
            self.diagonal = lax.rem(self.near + 2, ranks)
            self.staged, self.landing, self.send, self.recv = staged, landing, send, recv
            self.side = rows // 2
            self.first, self.relays = [], []

        def rows_of(self, rank, upper):
            return pl.ds(pl.multiple_of(rank * rows + upper * self.side, self.side), self.side)

        def add(self, n):
            lanes, side = pl.ds(n * LANES, LANES), self.side

            def copy(owner, upper, room, upper_room, at, to):
                src = self.staged.at[self.rows_of(owner, upper), lanes]
                dst = self.landing.at[room, pl.ds(upper_room * side, side), lanes]
                return remote(src, dst, self.send.at[n, at], self.recv.at[n, at], (s, to, z))

            near, far, diagonal = self.near, self.far, self.diagonal
            self.first.append(
                begin(
                    [
                        copy(diagonal, 0, 2, 0, 0, near),
                        copy(diagonal, 1, 2, 1, 1, far),
                        copy(near, 0, 0, 0, 2, near),
                        copy(far, 1, 1, 1, 3, far),
                    ]
                )
            )
            self.relays.append([copy(far, 0, 1, 0, 4, far), copy(near, 1, 0, 1, 5, near)])

        def wait(self):
            for n, (first, relays) in enumerate(zip(self.first, self.relays)):
                lanes = slice(n * LANES, (n + 1) * LANES)
                for upper, rank in enumerate((self.far, self.near)):
                    first[upper].wait_recv()
                    here_rows = self.rows_of(rank, upper)
                    passed = self.landing[2, upper * self.side : (upper + 1) * self.side, lanes]
                    summed = self.staged[here_rows, lanes].astype(f32) + passed.astype(f32)
                    self.staged[here_rows, lanes] = summed.astype(bf16)
                    relays[upper].start()
            for first, relays in zip(self.first, self.relays):
                finish_all([Half(copy.wait_recv) for copy in first[2:] + relays])
                finish_all([Half(copy.wait_send) for copy in first + relays])

    class Half:
        def __init__(self, wait):
            self.wait = wait

    def landed(staged, landing, relayed=False):
        own_rows = staged[mine].astype(f32)
        return landed_sum(own_rows, landing, 3 if relayed and ranks == 4 else ranks)

    def scatter_product(product, staged, landing, send, recv, relayed=False):
        relayed = relayed and ranks == 4
        copies = [RelayScatter(staged, landing, send, recv)] if relayed else []
        for n in range(chunks):
            lanes = slice(n * LANES, (n + 1) * LANES)
            staged[:, lanes] = product(lanes).astype(bf16)
            if relayed:
                copies[0].add(n)
            else:
                copies += scatter_block(
                    place, staged, landing, rows, n * LANES, LANES, send.at[n], recv.at[n]
                )
        return copies

    def share_of(l):
        return remote(half_a.at[l, 1 - odd], pair_in.at[l], pr_s.at[l], pr_r.at[l], place.partner)

    side = 2 * heads_width

    def swap_half(l):
        theirs = pl.ds(pl.multiple_of((1 - s) * side, 128), side)
        return remote(gw.at[:, theirs], got_a, as_s.at[l], as_r.at[l], place.sibling)

    def share_half(l):
        swap_half(l).wait()
        ours = pl.ds(pl.multiple_of(s * side, 128), side)
        kept = (gw[:, ours].astype(f32) + got_a[...].astype(f32)).astype(bf16)
        for side_b in range(2):
            for c in range(planes):
                lo = c * chunk + side_b * (chunk // 2)
                half_a[l, side_b, c] = kept[lo : lo + chunk // 2]
        share_of(l).start()

    def send_half(l):
        share_of(l).wait()
        half_a[l, odd] = (half_a[l, odd].astype(f32) + pair_in[l].astype(f32)).astype(bf16)
        to_owner(l, lambda c: half_a.at[l, odd, c], land_z.at[slot], az_s.at[l], az_r, az_l.at[l])

    def forward_chunks(gathering, full, landing, send, recv):
        copies = begin([remote(full.at[mine], landing.at[mine], send.at[0], recv.at[0], place.partner)])

        def onward(rank):
            they = pl.ds(rank * rows, rows)
            at = len(copies)
            copies.extend(
                begin([remote(full.at[they], landing.at[they], send.at[at], recv.at[at], place.partner)])
            )

        if ranks == 4:
            gathering[0].wait(onward)
        else:
            for k, copy in enumerate(gathering, 1):
                copy.wait()
                onward(place.peer(ranks - k))
        return copies

    place.greet()
    first_w = 5
    ex_pairs = [
        (bnd.at[1 - s], o_bnd),
        (gain_a_own, o_gain_a),
        (gain_f_own, o_gain_f),
        (router, o_router),
        (routes.at[1 - s], o_routes),
    ] + [(own[i], other[i]) for i in range(10)]
    exchange = [
        remote(src, dst, ex_s.at[i], ex_r.at[i], place.sibling) for i, (src, dst) in enumerate(ex_pairs)
    ]
    begin(exchange)
    row8 = lax.broadcasted_iota(jnp.int32, (8, seq_len), 0)
    token8 = lax.broadcasted_iota(jnp.int32, (8, seq_len), 1)
    length = lens[s]
    cosine, signed = tables[:, :HEAD_DIM], tables[:, HEAD_DIM:]

    def attn_begin(l):
        if l == 0:

            @pl.when(s == 0)
            def _():
                gain_now[...] = gain_a_own[...]

            @pl.when(s != 0)
            def _():
                gain_now[...] = o_gain_a[...]

        else:
            gain_now[...] = gain_of(l, gain_a_own, o_gain_a)
        nf[mine] = rms_rows(xs[l].astype(f32), gain_now[...]).astype(bf16)
        return gather_now(nf, ag_s.at[l, 0], ag_r.at[l, 0])

    def attn_forward(l, gathering, loads, between):
        finish_all(loads)
        finish_all(gathering)
        between()
        projected = dot(nf[...], w_in[...], 1, 1)
        for j, dst in enumerate((qs, ks, vs)):
            for h in range(heads):
                at = j * heads_width + h * HEAD_DIM
                piece = projected[:, at : at + HEAD_DIM]
                if j < 2:
                    piece = piece * cosine + turn_halves(piece) * signed
                dst[h] = piece.astype(bf16)
        place_q = lax.broadcasted_iota(jnp.int32, (seq_len, seq_len), 0)
        place_k = lax.broadcasted_iota(jnp.int32, (seq_len, seq_len), 1)
        allowed = (place_k <= place_q) & (place_k < length)
        for h in range(heads):
            scores = dot(qs[h], ks[h], 1, 1) * scale
            scores = jnp.where(allowed, scores, MASKED)
            peak = jnp.max(scores, axis=-1, keepdims=True)
            raised = jnp.exp(scores - peak)
            total = jnp.sum(raised, axis=-1, keepdims=True)
            weights = (raised / total).astype(bf16)
            ps[h] = weights
            mx[:, h * HEAD_DIM : (h + 1) * HEAD_DIM] = dot(weights, vs[h], 1, 0).astype(bf16)
        return scatter_product(
            lambda lanes: dot(mx[...], wo[:, lanes], 1, 0),
            stage,
            land_a,
            rsa_s.at[l, pl.ds(0, chunks)],
            rsa_r.at[l, pl.ds(0, chunks)],
            True,
        )

    def attn_finish(l, scattering):
        finish_all(scattering)
        middle = xs[l].astype(f32) + landed(stage, land_a, True)
        mid[l] = middle
        hf[mine] = rms_rows(middle, gain_of(l, gain_f_own, o_gain_f)).astype(bf16)
        return gather_now(hf, ag_s.at[l, 1], ag_r.at[l, 1])

    def route(l):
        names = name_rows(jnp.where(s == l, routes[s], o_routes[...]))
        logits = dot(route_weights(l), hf[...], 1, 1)
        logits = jnp.where(row8 < experts, logits, MASKED)
        raised = jnp.exp(logits - jnp.max(logits, axis=0, keepdims=True))
        raised = jnp.where(row8 < experts, raised, 0.0)
        chances = raised / jnp.sum(raised, axis=0, keepdims=True)
        per_chosen = names / jnp.sum(chances * names, axis=0, keepdims=True)
        gates = chances * per_chosen
        small[l, 0:8] = chances
        small[l, 8:16] = gates
        small[l, 16:24] = per_chosen
        remote(small.at[l], o_small.at[l], hp_s.at[l, 1], hp_r.at[l, 1], place.partner).start()
        summed = jnp.sum(jnp.where(token8 < length, chances, 0.0), axis=1, keepdims=True)
        probs_sum[l] = jnp.broadcast_to(summed, (8, 128))
        coef[...] = jnp.where(row8 == experts, 1.0, gates).T

    def split_acts(e, value):
        low, high = value[:, :half], value[:, half:]
        acts[e] = jnp.where(odd == 0, low, high).astype(bf16)
        gp[e] = jnp.where(odd == 0, high, low).astype(bf16)

    def branch_product(lanes):
        total = dot(acts[0], wd[0, my_lanes, lanes], 1, 0) + dot(gp[0], wd[0, far_lanes, lanes], 1, 0)
        for e in range(1, blocks):
            total = total + dot(acts[e], wd[e, my_lanes, lanes], 1, 0)
            total = total + dot(gp[e], wd[e, far_lanes, lanes], 1, 0)
        return total

    def output_rows(l, landing, staged):
        output = mid[l] + landed(staged, landing, l == 0)
        y_low[l] = output.astype(bf16)

        @pl.when(s == l)
        def _():
            out_rows[s] = y_low[l]

        @pl.when(s != l)
        def _():
            remote(y_low.at[l], out_rows.at[s], row_s, row_r, place.sibling).start()

    @pl.when(s == 0)
    def _():
        xs[0] = bnd[0]

    @pl.when(s != 0)
    def _():
        finish_all(exchange[:first_w])
        xs[0] = o_bnd[...]

    gathering = attn_begin(0)

    @pl.when(s != 0)
    def _():
        for copy in exchange[first_w : first_w + N_ATTN]:
            copy.wait_recv()

    loads = attn_weights(0)
    counted = jnp.zeros((8, 1), f32)
    for q in range(2):
        live = jnp.where(token8 < lens[q], 1.0, 0.0)
        counts = jnp.where(row8 == 7, live, name_rows(routes[q]) * live)
        counted = counted + jnp.sum(counts, axis=1, keepdims=True)
    cnt[...] = jnp.broadcast_to(counted, cnt.shape)
    count_copies = begin(
        [
            remote(cnt, cnt_in.at[k - 1], cz_s.at[k - 1], cz_r.at[k - 1], place.plane_id(k))
            for k in range(1, planes)
        ]
    )

    @pl.when(s == 0)
    def _():
        finish_all(exchange[:first_w])

    cotangent = jnp.where(s == 0, o_bnd[...], bnd[1]).astype(f32)
    position = lax.broadcasted_iota(jnp.int32, (rows, width), 0) + t * rows
    dyf[mine] = jnp.where(position < length, cotangent, 0.0).astype(bf16)
    cot_gather = []

    def gather_cotangent():
        cot_gather.extend(gather_rows(place, dyf, rows, ag_s.at[1, 2], ag_r.at[1, 2]))

    scattering = attn_forward(0, gathering, loads, gather_cotangent)

    @pl.when(s != 0)
    def _():
        for copy in exchange[first_w + N_ATTN :]:
            copy.wait_recv()

    ffn_loads = ffn_weights(0)
    attn_saves = begin(moves(attn_state, 4, False))
    gathering = attn_finish(0, scattering)

    @pl.when(s == 0)
    def _():
        for copy in exchange[first_w : first_w + N_ATTN]:
            copy.wait_recv()

    attn_w = attn_weights(1)
    finish_all(count_copies)
    total = cnt[...]
    for k in range(planes - 1):
        total = total + cnt_in[k]
    cnt[...] = total
    share_counts = remote(cnt, o_cnt, cs_s, cs_r, place.sibling)
    share_counts.start()
    finish_all(ffn_loads)
    finish_all(gathering)
    ffn_saves = begin(moves(ffn_state[2:3], 2, False))
    hidden_sent = [remote(hf, hp_o, hp_s.at[0, 0], hp_r.at[0, 0], place.partner)]
    begin(hidden_sent)
    route(0)

    def forward_expert(e, carry):
        gate_h = dot(hf[...], wg[e], 1, 0)
        up_h = dot(hf[...], wu[e], 1, 0)
        gs[e] = gate_h.astype(bf16)
        us[e] = up_h.astype(bf16)
        split_acts(e, gate_h * jax.nn.sigmoid(gate_h) * up_h * column(coef[...], e))
        return carry

    lax.fori_loop(0, blocks, forward_expert, 0)
    ffn_saves += begin(moves(ffn_state[:2], 0, False))
    finish_all(attn_saves)
    scat = scatter_product(branch_product, stage, land_f, rsf_s.at[0, 0], rsf_r.at[0, 0], True)

    @pl.when(s == 0)
    def _():
        for copy in exchange[first_w + N_ATTN :]:
            copy.wait_recv()

    ffn_loads = ffn_weights(1)
    finish_all(cot_gather)
    cot_sent = remote(dyf, dyp.at[1], dp_s.at[1, 0], dp_r.at[1, 0], place.partner)
    cot_sent.start()
    finish_all(scat)
    output_rows(0, land_f, stage)
    xs[1] = y_low[0]

    gathering = attn_begin(1)
    finish_all(hidden_sent)
    finish_all(ffn_saves)
    scattering = attn_forward(1, gathering, attn_w, lambda: None)
    gathering = attn_finish(1, scattering)
    hidden_sent = forward_chunks(gathering, hf, hp, hq_s, hq_r)
    finish_all(ffn_loads)
    route(1)
    gate_sum[...] = jnp.zeros_like(gate_sum)
    lane8 = lax.broadcasted_iota(jnp.int32, gate_sum.shape, 1)

    def expert_grads(e, gate_h, up_h, raw):
        sig = jax.nn.sigmoid(gate_h)
        silu = gate_h * sig
        acted = silu * up_h
        inner_sum = jnp.sum(acted * raw, axis=1, keepdims=True)
        gate_sum[...] = jnp.where(lane8 == e, inner_sum, gate_sum[...])
        weight = column(coef[...], e)
        d_acted = raw * weight
        gs[e] = (d_acted * up_h * (sig + silu * (1.0 - sig))).astype(bf16)
        us[e] = (d_acted * silu).astype(bf16)
        return acted * weight

    def both_expert(e, carry):
        gate_h = dot(hf[...], wg[e], 1, 0)
        up_h = dot(hf[...], wu[e], 1, 0)
        raw = dot(dyf[...], wd[e], 1, 1)
        split_acts(e, expert_grads(e, gate_h, up_h, raw))
        return carry

    def back_expert(e, carry):
        raw = dot(dyf[...], wd[e], 1, 1)
        value = expert_grads(e, gs[e].astype(f32), us[e].astype(f32), raw)
        acts[e] = jnp.where(odd == 0, value[:, :half], value[:, half:]).astype(bf16)
        return carry

    lax.fori_loop(0, blocks, both_expert, 0)
    share_counts.wait()
    y_scat = []

    for l in (1, 0):
        here = s == l
        if l == 0:
            finish_all(ffn_loads)
            finish_all(ffn_back)
            coef[...] = jnp.where(row8 == experts, 1.0, small[l, 8:16]).T
            gate_sum[...] = jnp.zeros_like(gate_sum)
            to_partner = forward_chunks(gathering, dyf, dyp.at[l], dp_s.at[l], dp_r.at[l])
            share_half(1)
            for e in range(SENT_AT_ONCE, blocks):
                send_later(e)
            lax.fori_loop(0, blocks, back_expert, 0)
        else:
            to_partner = [cot_sent]
        if l == 1:
            y_scat = scatter_product(branch_product, stage_y, land_y, rsy_s, rsy_r)
        finish_all(to_partner)
        if l == 1:
            finish_all(hidden_sent)
        remote(small.at[l], o_small.at[l], hp_s.at[l, 1], hp_r.at[l, 1], place.partner).wait()
        coef[...] = jnp.where(row8 == experts, 1.0, o_small[l, 8:16]).T

        def partner_expert(e, carry, l=l):
            gate_h = dot(hp[...], wg[e, :, my_lanes], 1, 0)
            up_h = dot(hp[...], wu[e, :, my_lanes], 1, 0)
            raw = dot(dyp[l], wd[e, my_lanes], 1, 1)
            sig = jax.nn.sigmoid(gate_h)
            silu = gate_h * sig
            weight = column(coef[...], e)
            ap[e] = (silu * up_h * weight).astype(bf16)
            d_acted = raw * weight
            gp[e] = (d_acted * up_h * (sig + silu * (1.0 - sig))).astype(bf16)
            up[e] = (d_acted * silu).astype(bf16)
            return carry

        lax.fori_loop(0, blocks, partner_expert, 0)
        def swap_of(e, l=l):
            return remote(sent.at[e], got.at[e], sw_s.at[e], sw_r.at[e], place.sibling)

        def send_grads(e, l=l):
            three = pl.ds(e * 3, 3)
            to_owner(l, lambda c: quarter.at[l, c, three], land.at[slot, three], zs.at[l], zr, zl.at[l])

        def finish(e, l=l, send_grads=send_grads):
            swap_of(e).wait()
            for j in range(3):
                at = e * 3 + j
                for c in range(planes):
                    quarter[l, c, at] = (
                        quarter[l, c, at].astype(f32) + got[e, j, c].astype(f32)
                    ).astype(bf16)

            @pl.when(jnp.logical_or(l == 0, e < SENT_AT_ONCE))
            def _():
                send_grads(e)

        def weight_grads(e, carry, l=l, finish=finish):
            sources = ((hf, gs, hp, gp), (hf, us, hp, up))
            for j in range(3):
                if j < 2:
                    left, right, left_p, right_p = sources[j]
                    value = dot(left[...], right[e, :, my_lanes], 0, 0) + dot(left_p[...], right_p[e], 0, 0)
                else:
                    value = dot(dyf[...], acts[e], 0, 0) + dot(dyp[l], ap[e], 0, 0)
                low, high = value[:, :part], value[:, part:]
                kept = jnp.where(s == 0, low, high).astype(bf16)
                given = jnp.where(s == 0, high, low).astype(bf16)
                for c in range(planes):
                    quarter[l, c, e * 3 + j] = kept[c * chunk : (c + 1) * chunk]
                    sent[e, j, c] = given[c * chunk : (c + 1) * chunk]
            swap_of(e).start()

            @pl.when(e > 0)
            def _():
                finish(e - 1)

            return carry

        early, middle = GRADS_BY[l]
        if l == 1:
            send_later = send_grads
        lax.fori_loop(0, early, weight_grads, 0)
        chances, gates, per_chosen = small[l, 0:8], small[l, 8:16], small[l, 16:24]
        totals = jnp.where(here, cnt[...], o_cnt[...])
        tokens_all = totals[7:8, 0:1]
        share = totals[:, 0:1] / (top * tokens_all)
        aux = jnp.where((token8 < length) & (t == 0), ALPHA * experts * share / tokens_all, 0.0)
        d_gates = gate_sum[...].T
        common = jnp.sum(d_gates * gates, axis=0, keepdims=True)
        d_chances = per_chosen * (d_gates - common) + aux
        d_logits = chances * (d_chances - jnp.sum(chances * d_chances, axis=0, keepdims=True))
        d_logits = d_logits.astype(bf16)
        router_grad = dot(d_logits, hf[...], 1, 0)
        route_w = route_weights(l)

        def hidden_product(lanes, d_logits=d_logits, route_w=route_w):
            total = dot(d_logits, route_w[:, lanes], 0, 0)
            for e in range(blocks):
                total = total + dot(gs[e], wg[e, lanes], 1, 1)
                total = total + dot(us[e], wu[e, lanes], 1, 1)
            return total

        scat = scatter_product(hidden_product, stage, land_f, rsf_s.at[l, 1], rsf_r.at[l, 1])
        lax.fori_loop(early, middle, weight_grads, 0)
        finish_all(scat)
        d_hidden = landed(stage, land_f)
        d_norm, gain_f_grad = rms_back(mid[l], gain_of(l, gain_f_own, o_gain_f), d_hidden)
        d_mid[...] = dyf[mine].astype(f32) + d_norm
        df[mine] = d_mid[...].astype(bf16)
        gathering = gather_rows(place, df, rows, ag_s.at[l, 3], ag_r.at[l, 3])

        if l == 0:
            send_half(1)
        lax.fori_loop(middle, blocks, weight_grads, 0)
        finish(blocks - 1)
        if l == 1:
            ffn_loads = ffn_weights(0)
            ffn_back = begin(moves(ffn_state, 0, True))
        else:
            finish_all(attn_w)
            finish_all(attn_back)
        finish_all(gathering)
        for h in range(heads):
            span = slice(h * HEAD_DIM, (h + 1) * HEAD_DIM)
            d_mixed = dot(df[...], wo[span], 1, 1).astype(bf16)
            for lo in range(0, seq_len, LANES):
                reach = lo + LANES
                weights = ps[h, lo:reach, 0:reach].astype(f32)
                d_probs = dot(d_mixed[lo:reach], vs[h, 0:reach], 1, 1)
                total = jnp.sum(weights * d_probs, axis=-1, keepdims=True)
                ds[lo:reach, 0:reach] = (weights * (d_probs - total)).astype(bf16)
                if reach < seq_len:
                    ds[lo:reach, reach:] = jnp.zeros((LANES, seq_len - reach), bf16)
            d_value = dot(ps[h], d_mixed, 0, 0)
            d_query = dot(ds[...], ks[h], 1, 0) * scale
            d_key = dot(ds[...], qs[h], 0, 0) * scale
            d_query = d_query * cosine - turn_halves(d_query) * signed
            d_key = d_key * cosine - turn_halves(d_key) * signed
            for j, value in enumerate((d_query, d_key, d_value)):
                at = j * heads_width + h * HEAD_DIM
                dqkv[:, at : at + HEAD_DIM] = value.astype(bf16)
        scat = scatter_product(
            lambda lanes: dot(dqkv[...], w_in[:, lanes], 1, 0), stage, land_a, rsa_s.at[l, pl.ds(chunks, chunks)], rsa_r.at[l, pl.ds(chunks, chunks)], True
        )

        three_widths = 3 * heads_width
        gw[:, :three_widths] = dot(nf[...], dqkv[...], 0, 0).astype(bf16)
        gw[:, three_widths:] = dot(df[...], mx[...], 0, 0).astype(bf16)
        swap_half(l).start()
        finish_all(scat)
        d_normed = landed(stage, land_a, True)
        d_norm, gain_a_grad = rms_back(xs[l].astype(f32), gain_of(l, gain_a_own, o_gain_a), d_normed)
        dx = d_mid[...] + d_norm
        if l == 1:
            low_dx = dx.astype(bf16)
            dyf[mine] = low_dx
            gathering = gather_now(dyf, ag_s.at[0, 2], ag_r.at[0, 2])
            dx = low_dx.astype(f32)
            attn_w = attn_weights(0)
            attn_back = begin(moves(attn_state, 4, True))
            finish_all(y_scat)
            output_rows(1, land_y, stage_y)
        pack = jnp.concatenate(
            [
                jnp.concatenate([gain_a_grad, gain_f_grad, router_grad[:6]], axis=0),
                jnp.concatenate(
                    [jnp.zeros((2, 128), f32), jnp.where(t == 0, probs_sum[l, 0:6], 0.0)], axis=0
                ),
            ],
            axis=1,
        )

        @pl.when(here)
        def _(dx=dx, pack=pack):
            in_grads[s] = dx
            packs[0] = pack

        @pl.when(jnp.logical_not(here))
        def _(dx=dx, pack=pack):
            row_buf[...] = dx
            packs[1] = pack
            remote(row_buf, in_grads.at[s], gr_s, gr_r, place.sibling).start()
            remote(packs.at[1], packs.at[2], pk_s, pk_r, place.sibling).start()

    share_half(0)
    send_half(0)
    remote(packs.at[1], packs.at[2], pk_s, pk_r, place.sibling).wait()
    packs[0] = packs[0] + packs[2]
    finish_all(
        begin(
            [
                remote(packs.at[0], pack_t.at[k - 1], pt_s.at[k - 1], pt_r.at[k - 1], place.peer_id(k))
                for k in range(1, ranks)
            ]
        )
    )
    total = packs[0]
    for k in range(ranks - 1):
        total = total + pack_t[k]
    packs[0] = total
    finish_all(
        begin(
            [
                remote(packs.at[0], pack_z.at[k - 1], pz_s.at[k - 1], pz_r.at[k - 1], place.plane_id(k))
                for k in range(1, planes)
            ]
        )
    )
    total = packs[0]
    for k in range(planes - 1):
        total = total + pack_z[k]
    gain_a_out[...] = total[0:1, :width]
    gain_f_out[...] = total[1:2, :width]
    router_out[...] = total[2 : 2 + experts, :width]
    tokens_all = cnt[7:8, 0:1]
    products = cnt[0:experts, 0:1] / (top * tokens_all) * total[2 : 2 + experts, width : width + 1]
    balance[...] = experts * jnp.sum(products, axis=0, keepdims=True) / tokens_all

    for copy in exchange[first_w:]:
        copy.wait_send()
    remote(y_low.at[1 - s], out_rows.at[s], row_s, row_r, place.sibling).wait_send()
    remote(y_low.at[1 - s], out_rows.at[1 - s], row_s, row_r, place.sibling).wait_recv()
    remote(row_buf, in_grads.at[s], gr_s, gr_r, place.sibling).wait_send()
    remote(row_buf, in_grads.at[1 - s], gr_s, gr_r, place.sibling).wait_recv()
    for l in (1, 0):
        sent_to_owner(l, quarter.at[l], land, zs.at[l], zr, zl.at[l])
        sent_to_owner(l, half_a.at[l, odd], land_z, az_s.at[l], az_r, az_l.at[l])
    arrived(land, zs.at[0], zr)
    arrived(land_z, az_s.at[0], az_r)


def finish_kernel(planes, land, land_z, *refs):
    ins, outs, refs = refs[:6], refs[6:12], refs[12:]
    g_gate, g_up, g_down, s_gate, s_up, s_down, wq_out, wk_out, wv_out, wo_out = refs
    e = pl.program_id(0)
    experts = pl.num_programs(0) - 1
    part = land.shape[3]
    heads_width = wq_out.shape[1]
    for j, (routed, common) in enumerate(((g_gate, s_gate), (g_up, s_up), (g_down, s_down))):
        for core in range(2):
            for parity in range(2):
                value = land[core * planes + parity, j].astype(f32)
                for pair in range(1, planes // 2):
                    value = value + land[core * planes + 2 * pair + parity, j].astype(f32)
                lo = (2 * parity + core) * part

                @pl.when(e < experts)
                def _(value=value, lo=lo, routed=routed):
                    routed[0, :, lo : lo + part] = value

                @pl.when(e == experts)
                def _(value=value, lo=lo, common=common):
                    common[:, lo : lo + part] = value

    @pl.when(e == 1)
    def _():
        for src, dst in zip(ins, outs):
            dst[...] = src[...]
        sides = []
        for core in range(2):
            halves = []
            for parity in range(2):
                value = land_z[core * planes + parity].astype(f32)
                for pair in range(1, planes // 2):
                    value = value + land_z[core * planes + 2 * pair + parity].astype(f32)
                halves.append(value)
            sides.append(jnp.concatenate(halves, axis=0))
        wq_out[...] = sides[0][:, :heads_width]
        wk_out[...] = sides[0][:, heads_width:]
        wv_out[...] = sides[1][:, :heads_width]
        wo_out[...] = sides[1][:, heads_width:].T


def params(collective_id):
    return pltpu.CompilerParams(
        collective_id=collective_id, has_side_effects=True, vmem_limit_bytes=VMEM_LIMIT
    )


def shape_of(*dims, dtype=bf16):
    return jax.ShapeDtypeStruct(dims, dtype)


def on_device(ranks, planes, *args):
    (boundary, lengths, routes, attn_gain, w_query, w_key, w_value, w_out, ffn_gain, router) = args[:10]
    ffn_own = tuple(a[0] for a in args[10:])
    attn_own = (w_query[0].T, w_key[0].T, w_value[0].T, w_out[0])
    rows, width = boundary.shape[2:]
    seqs, seq_len = routes.shape[1:3]
    top = routes.shape[3]
    experts, _, inner = ffn_own[0].shape
    blocks = experts + 1
    heads_width = w_query.shape[2]
    heads = heads_width // HEAD_DIM
    chunks = width // LANES
    half, part = inner // 2, inner // 4
    chunk = width // planes
    peers = ranks - 1
    dma = pltpu.SemaphoreType.DMA

    def vmem(*dims, dtype=bf16):
        return pltpu.VMEM(dims, dtype)

    routes_t = jnp.swapaxes(routes[0], 1, 2)
    router_t = router[0].T
    tables = jnp.asarray(rope_tables(seq_len))
    head_shape = (heads, seq_len, HEAD_DIM)
    states = [
        (seq_len, width),
        head_shape,
        head_shape,
        head_shape,
        (heads, seq_len, seq_len),
        (seq_len, heads_width),
        (seq_len, width),
        (blocks, seq_len, inner),
        (blocks, seq_len, inner),
        (seq_len, width),
    ]
    weights = attn_own + ffn_own
    small_outs = [
        shape_of(2, rows, width),
        shape_of(seqs, rows, width, dtype=f32),
        shape_of(1, width, dtype=f32),
        shape_of(1, width, dtype=f32),
        shape_of(experts, width, dtype=f32),
        shape_of(1, 1, dtype=f32),
    ]
    result = pl.pallas_call(
        functools.partial(both_kernel, ranks, planes, top),
        out_shape=[shape_of(*w.shape) for w in weights]
        + [shape_of(*dims) for dims in states]
        + [
            shape_of(2 * planes, 3 * blocks, chunk, part),
            shape_of(2 * planes, chunk // 2, 2 * heads_width),
        ]
        + small_outs,
        in_specs=[SMEM] + [VMEM] * 6 + [ANY] * 10,
        out_specs=[ANY] * 22 + [VMEM] * 6,
        scratch_shapes=[vmem(*dims) for dims in states]
        + [
            vmem(3 * heads_width, width),
            vmem(heads_width, width),
            vmem(blocks, width, inner),
            vmem(blocks, width, inner),
            vmem(blocks, inner, width),
        ]
        + [vmem(seq_len, width), vmem(2, seq_len, width)]
        + [vmem(blocks, seq_len, half)] * 4
        + [vmem(seq_len, 8, dtype=f32)] * 2
        + [vmem(seq_len, width)] * 2
        + [vmem(peers, rows, width)] * 3
        + [vmem(rows, width, dtype=f32)] * 2
        + [
            vmem(blocks, 3, planes, chunk, part),
            vmem(blocks, 3, planes, chunk, part),
            vmem(2, planes, 3 * blocks, chunk, part),
            vmem(seq_len, width),
            vmem(seq_len, seq_len),
            vmem(seq_len, 3 * heads_width),
            vmem(width, 4 * heads_width),
            vmem(width, 2 * heads_width),
            vmem(2, 2, planes, chunk // 2, 2 * heads_width),
            vmem(2, planes, chunk // 2, 2 * heads_width),
        ]
        + [
            vmem(2, rows, width),
            vmem(2, rows, width, dtype=f32),
            vmem(2, 24, seq_len, dtype=f32),
            vmem(2, 24, seq_len, dtype=f32),
            vmem(2, 8, 128, dtype=f32),
            vmem(8, 128, dtype=f32),
            vmem(8, 128, dtype=f32),
            vmem(planes - 1, 8, 128, dtype=f32),
        ]
        + [
            vmem(rows, width),
            vmem(top, seq_len, dtype=jnp.int32),
            vmem(1, width, dtype=f32),
            vmem(1, width, dtype=f32),
            vmem(*router_t.shape),
            vmem(2, rows, width),
        ]
        + [
            vmem(3, 8, width + 128, dtype=f32),
            vmem(peers, 8, width + 128, dtype=f32),
            vmem(planes - 1, 8, width + 128, dtype=f32),
            vmem(1, width, dtype=f32),
        ]
        + [dma((2, 4, max(peers, 6)))] * 2
        + [dma((2, 2 * chunks, max(peers, 6)))] * 2
        + [dma((2, 2, chunks, max(peers, 6)))] * 2
        + [dma((chunks, max(peers, 6)))] * 2
        + [dma((15,))] * 2
        + [dma((2, 2))] * 2
        + [dma((ranks,))] * 2
        + [dma((2, ranks))] * 2
        + [dma((planes - 1,))] * 2
        + [dma] * 4
        + [dma((blocks,))] * 2
        + [dma((2, planes)), dma((2 * planes,)), dma((2,))]
        + [dma((2,))] * 2
        + [dma((2, planes)), dma((2 * planes,)), dma((2,))]
        + [dma((2,))] * 2
        + [dma] * 4
        + [dma((peers,))] * 2
        + [dma((planes - 1,))] * 2
        + [dma((N_FFN,)), dma((N_ATTN,)), dma((10,))],
        compiler_params=params(0),
        name="forward_backward",
    )(lengths, boundary[0], routes_t, attn_gain, ffn_gain, router_t, tables, *weights)
    land, land_z, *small_results = result[20:]

    def whole(shape):
        return pl.BlockSpec(shape, lambda e: (0,) * len(shape))

    routed = shape_of(experts, chunk, inner, dtype=f32)
    common = shape_of(chunk, inner, dtype=f32)
    square = shape_of(chunk, heads_width, dtype=f32)
    turned = shape_of(heads_width, chunk, dtype=f32)
    last = experts - 1
    done = pl.pallas_call(
        functools.partial(finish_kernel, planes),
        grid=(blocks,),
        out_shape=small_outs + [routed] * 3 + [common] * 3 + [square] * 3 + [turned],
        in_specs=[
            pl.BlockSpec((2 * planes, 3, chunk, part), lambda e: (0, e, 0, 0)),
            whole(land_z.shape),
        ]
        + [whole(o.shape) for o in small_outs],
        out_specs=[whole(o.shape) for o in small_outs]
        + [pl.BlockSpec((1, chunk, inner), lambda e: (jnp.minimum(e, last), 0, 0))] * 3
        + [whole(common.shape)] * 3
        + [whole(square.shape)] * 3
        + [whole(turned.shape)],
        compiler_params=pltpu.CompilerParams(vmem_limit_bytes=VMEM_LIMIT),
        name="finish",
    )(land, land_z, *small_results)
    (out_rows, in_grads, g_gain_a, g_gain_f, g_router, balance), done = done[:6], done[6:]
    g_eg, g_eu, g_ed, g_sg, g_su, g_sd, g_q, g_k, g_v, g_o = done
    return (
        out_rows[None],
        in_grads[None],
        g_gain_a,
        g_q[None],
        g_k[None],
        g_v[None],
        g_o[None],
        g_gain_f,
        g_router.T[None],
        g_eg[None],
        g_eu[None],
        jnp.swapaxes(g_ed, 1, 2)[None],
        g_sg[None],
        g_su[None],
        g_sd.T[None],
        balance.reshape(1),
    )


def solution(mesh):
    placed = (
        P("section", "dp", "tensor", None),
        P("dp"),
        P("section", "dp", None, None),
        P("section", None),
        P("section", None, "tensor"),
        P("section", None, "tensor"),
        P("section", None, "tensor"),
        P("section", "tensor", None),
        P("section", None),
        P("section", None, None),
        P("section", None, None, "tensor"),
        P("section", None, None, "tensor"),
        P("section", None, "tensor", None),
        P("section", None, "tensor"),
        P("section", None, "tensor"),
        P("section", "tensor", None),
    )
    return jax.shard_map(
        functools.partial(on_device, mesh.shape["tensor"], mesh.shape["dp"]),
        mesh=mesh,
        in_specs=placed,
        out_specs=(
            P("section", "dp", "tensor", None),
            P("section", "dp", "tensor", None),
            P("section", None),
            P("section", "dp", "tensor"),
            P("section", "dp", "tensor"),
            P("section", "dp", "tensor"),
            P("section", "tensor", "dp"),
            P("section", None),
            P("section", None, None),
            P("section", None, "dp", "tensor"),
            P("section", None, "dp", "tensor"),
            P("section", None, "tensor", "dp"),
            P("section", "dp", "tensor"),
            P("section", "dp", "tensor"),
            P("section", "tensor", "dp"),
            P("section"),
        ),
        check_vma=False,
    )
```
